32 devices in a mesh: section: 2 (over x), tok: 16 (over z, y, core).
Axes of the slice: x: 2, y: 2, z: 4, core: 2. Of those that a mesh axis runs over, the one named last changes fastest.
Arguments:
- inputs: bfloat16 [2, 1024, 1024], P(None, 'tok'), may hold values from -6 to 6
- cotangent: bfloat16 [2, 1024, 1024], P(None, 'tok'), may hold values from -6 to 6
- lengths: int32 [2, 8], replicated, may hold values from 1 to 1017, as said below
- prefix_keys: bfloat16 [2, 64, 1024], P('section'), may hold values from -6 to 6
- prefix_values: bfloat16 [2, 64, 1024], P('section'), may hold values from -6 to 6
- w_query: bfloat16 [2, 1024, 1024], P('section', 'tok'), may hold values from -0.1875 to 0.1875
- b_query: bfloat16 [2, 1024], P('section', 'tok'), may hold values from -3 to 3
- w_key: bfloat16 [2, 1024, 1024], P('section', 'tok'), may hold values from -0.1875 to 0.1875
- w_value: bfloat16 [2, 1024, 1024], P('section', 'tok'), may hold values from -0.1875 to 0.1875
- b_value: bfloat16 [2, 1024], P('section', 'tok'), may hold values from -3 to 3
- w_out: bfloat16 [2, 1024, 1024], P('section', 'tok'), may hold values from -6 to 6
- b_out: bfloat16 [2, 1024], P('section', 'tok'), may hold values from -6 to 6
- norm1_gain: bfloat16 [2, 1024], P('section', 'tok'), may hold values from 0.25 to 1.75
- norm1_shift: bfloat16 [2, 1024], P('section', 'tok'), may hold values from -3 to 3
- w_up: bfloat16 [2, 1024, 4096], P('section', 'tok'), may hold values from -0.1875 to 0.1875
- b_up: bfloat16 [2, 4096], P('section', 'tok'), may hold values from -3 to 3
- w_down: bfloat16 [2, 4096, 1024], P('section', 'tok'), may hold values from -0.09375 to 0.09375
- b_down: bfloat16 [2, 1024], P('section', 'tok'), may hold values from -3 to 3
- norm2_gain: bfloat16 [2, 1024], P('section', 'tok'), may hold values from 0.25 to 1.75
- norm2_shift: bfloat16 [2, 1024], P('section', 'tok'), may hold values from -3 to 3
Outputs:
- layer_outputs: bfloat16 [2, 2, 1024, 1024], P('section', None, 'tok')
- input_grads: bfloat16 [2, 2, 1024, 1024], P('section', None, 'tok')
- grad_w_query: float32 [2, 1024, 1024], P('section', 'tok')
- grad_b_query: float32 [2, 1024], P('section', 'tok')
- grad_w_key: float32 [2, 1024, 1024], P('section', 'tok')
- grad_w_value: float32 [2, 1024, 1024], P('section', 'tok')
- grad_b_value: float32 [2, 1024], P('section', 'tok')
- grad_w_out: float32 [2, 1024, 1024], P('section', 'tok')
- grad_b_out: float32 [2, 1024], P('section', 'tok')
- grad_norm1_gain: float32 [2, 1024], P('section', 'tok')
- grad_norm1_shift: float32 [2, 1024], P('section', 'tok')
- grad_w_up: float32 [2, 1024, 4096], P('section', 'tok')
- grad_b_up: float32 [2, 4096], P('section', 'tok')
- grad_w_down: float32 [2, 4096, 1024], P('section', 'tok')
- grad_b_down: float32 [2, 1024], P('section', 'tok')
- grad_norm2_gain: float32 [2, 1024], P('section', 'tok')
- grad_norm2_shift: float32 [2, 1024], P('section', 'tok')
- grad_prefix_keys: float32 [2, 64, 1024], P('section')
- grad_prefix_values: float32 [2, 64, 1024], P('section')
The draws below stay inside these ranges and needn't reach their ends.
Inputs may be any that keep to these rules, and one draw needn't show every extreme that they name: In each micro-batch the 8 lengths sum to 1024; one document, at a position drawn per micro-batch, covers rows of the first and of the last 64 tokens.
All inputs are finite; a program needn't handle non-finite values.
Results may differ from the reference program's by a relative error of at most 0.028.
Values may be sent and summed in bfloat16 or wider, within the bound.
A program may use at most 256 MiB of HBM per device.

```python
import jax
import jax.numpy as jnp
from jax import lax

D = 1024
FF = 4096
HEADS = 16
HEAD = 64
PREFIX = 64
SEGS = 8
MICRO = 2
TOK_DEV = 64
LENGTH = 1024


def draw_lengths(key, part):
    key = jax.random.fold_in(key, 11)
    short_key, place_key = jax.random.split(key)
    shorts = jax.random.randint(short_key, (MICRO, SEGS - 1), 1, TOK_DEV // 8 + 1, dtype=jnp.int32)
    micro_rows = jnp.arange(MICRO, dtype=jnp.int32)[:, None]
    shorts = jnp.where(micro_rows == 0, jnp.ones_like(shorts), shorts).astype(jnp.int32)
    place = jax.random.randint(place_key, (MICRO, 1), 0, SEGS, dtype=jnp.int32)
    longest = LENGTH - jnp.sum(shorts, axis=1, keepdims=True, dtype=jnp.int32)
    filler = jnp.zeros((MICRO, 1), jnp.int32)
    shorts_left = jnp.concatenate([shorts, filler], axis=1)
    shorts_right = jnp.concatenate([filler, shorts], axis=1)
    slots = jnp.arange(SEGS, dtype=jnp.int32)[None, :]
    return jnp.where(slots < place, shorts_left, jnp.where(slots == place, longest, shorts_right)).astype(jnp.int32)


def steps_of(rng, shape, cuts, smallest, top_value):
    level = 1.0
    for position, blocks in cuts:
        steps = jax.random.uniform(jax.random.fold_in(jax.random.fold_in(rng, 6), position), (blocks,), jnp.float32, smallest / len(cuts), top_value / len(cuts))
        level = level * jnp.repeat(jnp.exp(steps), shape[position] // blocks).reshape((-1,) + (1,) * (len(shape) - 1 - position))
    return level


def bell_draw(stream_key, shape, scale, reach, cuts=(), kind=jnp.bfloat16):
    factor_of = steps_of(stream_key, shape, cuts, -0.22, 0.18) if cuts else 1.0
    values = jax.random.normal(stream_key, shape, jnp.float32) * scale * factor_of
    return jnp.minimum(jnp.maximum(values, -reach), reach).astype(kind)


def setup_inputs(seed: int = 0) -> dict:
    seeds = jax.random.split(jax.random.key(seed), 21)
    return {
        "inputs": bell_draw(seeds[0], (MICRO, LENGTH, D), 1.0, 6.0, ((1, 16),)),
        "cotangent": bell_draw(seeds[1], (MICRO, LENGTH, D), 1.0, 6.0, ((1, 16),)),
        "lengths": draw_lengths(jax.random.fold_in(seeds[20], 71), 0),
        "prefix_keys": bell_draw(seeds[3], (2, PREFIX, D), 1.0, 6.0, ((0, 2),)),
        "prefix_values": bell_draw(seeds[4], (2, PREFIX, D), 1.0, 6.0, ((0, 2),)),
        "w_query": bell_draw(seeds[5], (2, D, D), D ** -0.5, 0.1875, ((0, 2), (1, 16))),
        "b_query": bell_draw(seeds[6], (2, D), 0.5, 3.0, ((0, 2), (1, 16))),
        "w_key": bell_draw(seeds[7], (2, D, D), D ** -0.5, 0.1875, ((0, 2), (1, 16))),
        "w_value": bell_draw(seeds[8], (2, D, D), D ** -0.5, 0.1875, ((0, 2), (1, 16))),
        "b_value": bell_draw(seeds[9], (2, D), 0.5, 3.0, ((0, 2), (1, 16))),
        "w_out": bell_draw(seeds[10], (2, D, D), ((LENGTH / D) ** 0.5), 6.0, ((0, 2), (1, 16))),
        "b_out": bell_draw(seeds[11], (2, D), 1.0, 6.0, ((0, 2), (1, 16))),
        "norm1_gain": jnp.clip(1.0 + 0.15 * jax.random.normal(seeds[12], (2, D), jnp.float32), 0.25, 1.75).astype(jnp.bfloat16),
        "norm1_shift": bell_draw(seeds[13], (2, D), 0.5, 3.0, ((0, 2), (1, 16))),
        "w_up": bell_draw(seeds[14], (2, D, FF), D ** -0.5, 0.1875, ((0, 2), (1, 16))),
        "b_up": bell_draw(seeds[15], (2, FF), 0.5, 3.0, ((0, 2), (1, 16))),
        "w_down": bell_draw(seeds[16], (2, FF, D), FF ** -0.5, 0.09375, ((0, 2), (1, 16))),
        "b_down": bell_draw(seeds[17], (2, D), 0.5, 3.0, ((0, 2), (1, 16))),
        "norm2_gain": jnp.clip(1.0 + 0.15 * jax.random.normal(seeds[18], (2, D), jnp.float32), 0.25, 1.75).astype(jnp.bfloat16),
        "norm2_shift": bell_draw(seeds[19], (2, D), 0.5, 3.0, ((0, 2), (1, 16))),
    }


@jax.custom_vjp
def low(v):
    return lax.optimization_barrier(v.astype(jnp.bfloat16)).astype(jnp.float32)

@jax.custom_vjp
def low_back(v):
    return v

def low_keep(v):
    return (low(v), None)

def low_pass(kept, grad):
    return (grad,)

def back_keep(v):
    return (v, None)

def back_low(kept, grad):
    return (low(grad),)
low.defvjp(low_keep, low_pass)
low_back.defvjp(back_keep, back_low)
HIGHEST = lax.Precision.HIGHEST

def segment_of(lengths_row, positions):
    ends = jnp.cumsum(lengths_row, dtype=jnp.int32)
    return lax.optimization_barrier(jnp.sum((positions[:, None] >= ends[None, :]).astype(jnp.int32), axis=1, dtype=jnp.int32))

def normalize(value, gain, shift):
    centred = value - lax.optimization_barrier(jnp.mean(value, axis=-1, keepdims=True))
    spread = lax.optimization_barrier(jnp.mean(centred * centred, axis=-1, keepdims=True))
    return centred * lax.rsqrt(spread + 1e-05) * gain + shift

def product(left, right):
    return jnp.dot(left, right, precision=HIGHEST)

def attention(queries, key_rows, value_rows, prefix_key_rows, prefix_value_rows, segment):
    total_rows = queries.shape[0]
    query_heads = queries.reshape(total_rows, HEADS, HEAD)
    all_keys = jnp.concatenate([prefix_key_rows, key_rows], axis=0).reshape(-1, HEADS, HEAD)
    all_values = jnp.concatenate([prefix_value_rows, value_rows], axis=0).reshape(-1, HEADS, HEAD)
    key_segment = jnp.concatenate([jnp.full((PREFIX,), -1, jnp.int32), segment])
    block_rows = min(512, total_rows)

    def score_block(packet):
        query_block, segment_block = packet
        raw_scores = low_back(jnp.einsum('qhe,khe->hqk', query_block, all_keys, precision=HIGHEST) * HEAD ** (-0.5))
        visible = (segment_block[:, None] == key_segment[None, :]) | (key_segment[None, :] < 0)
        raw_scores = jnp.where(visible[None], raw_scores, -1e+30)
        probs_full = jax.nn.softmax(raw_scores, axis=-1)
        return jnp.einsum('hqk,khe->qhe', low(probs_full), all_values, precision=HIGHEST)
    result = lax.map(jax.checkpoint(score_block), (query_heads.reshape(total_rows // block_rows, block_rows, HEADS, HEAD), segment.reshape(total_rows // block_rows, block_rows)))
    return result.reshape(total_rows, HEADS * HEAD)

def layer_pass(inbound, segment, params):
    w_query, b_query, w_key, w_value, b_value, w_out, b_out, gain_one, shift_one, w_up, b_up, w_down, b_down, gain_two, shift_two, prefix_key_rows, prefix_value_rows = params
    queries = low_back(low(product(inbound, w_query) + b_query))
    key_rows = low_back(low(product(inbound, w_key)))
    value_rows = low_back(low(product(inbound, w_value) + b_value))
    context = attention(queries, key_rows, value_rows, prefix_key_rows, prefix_value_rows, segment)
    context = low_back(low(context))
    attended = low_back(product(context, w_out) + b_out)
    normal_one = normalize(inbound + attended, gain_one, shift_one)
    pre_act = low_back(product(low(normal_one), w_up) + b_up)
    mixed = low_back(product(low(jax.nn.gelu(pre_act, approximate=False)), w_down) + b_down)
    return normalize(normal_one + mixed, gain_two, shift_two)

def reference(inputs, cotangent, lengths, prefix_keys, prefix_values, w_query, b_query, w_key, w_value, b_value, w_out, b_out, norm1_gain, norm1_shift, w_up, b_up, w_down, b_down, norm2_gain, norm2_shift):
    weight_args = (w_query, b_query, w_key, w_value, b_value, w_out, b_out, norm1_gain, norm1_shift, w_up, b_up, w_down, b_down, norm2_gain, norm2_shift, prefix_keys, prefix_values)
    floats = tuple((member.astype(jnp.float32) for member in weight_args))
    first_params = tuple((member[0] for member in floats))
    second_params = tuple((member[1] for member in floats))
    positions = jnp.arange(LENGTH, dtype=jnp.int32)
    segments = [segment_of(lengths[micro_index], positions) for micro_index in range(MICRO)]
    input_float = inputs.astype(jnp.float32)
    shifts = jnp.zeros_like(input_float)

    def forward(params_first, params_second, input_values, shift_values):
        finals = []
        middles = []
        for micro_index in range(MICRO):
            middle = low_back(low(layer_pass(input_values[micro_index], segments[micro_index], params_first))) + shift_values[micro_index]
            finals.append(layer_pass(middle, segments[micro_index], params_second))
            middles.append(middle)
        return (jnp.stack(finals), jnp.stack(middles))
    finals, pull_back, middles = jax.vjp(forward, first_params, second_params, input_float, shifts, has_aux=True)
    grad_first, grad_second, grad_input, grad_middle = pull_back(cotangent.astype(jnp.float32))
    stacked = [jnp.stack([grad_first[slot], grad_second[slot]]) for slot in range(17)]
    layer_outputs = jnp.stack([middles, finals]).astype(jnp.bfloat16)
    input_grads = jnp.stack([grad_input, grad_middle]).astype(jnp.bfloat16)
    return (layer_outputs, input_grads, stacked[0], stacked[1], stacked[2], stacked[3], stacked[4], stacked[5], stacked[6], stacked[7], stacked[8], stacked[9], stacked[10], stacked[11], stacked[12], stacked[13], stacked[14], stacked[15], stacked[16])
```

```python
import jax
import jax.numpy as jnp
from jax import lax
from jax.experimental import pallas as pl
from jax.experimental.pallas import tpu as pltpu
from jax.sharding import PartitionSpec as P

HEADS = 16
HEAD = 64


NEGATIVE = -1e30


def from_behind(block, axis, distance):
    devices = range(lax.axis_size(axis))
    route = [(i - distance, i) for i in devices if i - distance in devices]
    return lax.ppermute(block, axis, route)


def segment_of(lengths_row, positions):
    ends = jnp.cumsum(lengths_row, dtype=jnp.int32)
    return jnp.sum((positions[:, None] >= ends[None, :]).astype(jnp.int32), axis=1, dtype=jnp.int32)


def normalize(value, gain, shift):
    centred = value - jnp.mean(value, axis=-1, keepdims=True)
    spread = jnp.mean(centred * centred, axis=-1, keepdims=True)
    return centred * lax.rsqrt(spread + 1e-05) * gain + shift


def gelu_exact(value):
    return jax.nn.gelu(value, approximate=False)


def project(left, right):
    return jnp.dot(left, right, preferred_element_type=jnp.float32)


def project_back(left, weight):
    return jnp.einsum("tf,df->td", left, weight, preferred_element_type=jnp.float32)


def contract_rows(left, right):
    return jnp.einsum("tf,td->fd", left, right, preferred_element_type=jnp.float32)


def split_heads(value):
    return value.reshape(value.shape[0], HEADS, HEAD)


def in_blocks(step_fn, running, arrays, offset_row):
    total_rows = arrays[0].shape[0]
    block_rows = 1024 if total_rows > 1024 and total_rows % 1024 == 0 else total_rows
    if block_rows == total_rows:
        return step_fn(running, arrays, offset_row)
    stacked = tuple(
        (
            member.reshape((total_rows // block_rows, block_rows) + member.shape[1:])
            for member in arrays
        )
    )
    offsets = offset_row + block_rows * jnp.arange(total_rows // block_rows, dtype=jnp.int32)

    def scan_step(inner, packet):
        return (step_fn(inner, packet[0], packet[1]), None)

    result, unused = lax.scan(scan_step, running, (stacked, offsets))
    return result


def masked_scores(query_part, key_part, query_segment, key_segment):
    raw_scores = jnp.einsum(
        "qhe,khe->hqk",
        split_heads(query_part),
        split_heads(key_part),
        preferred_element_type=jnp.float32,
    ) * HEAD ** (-0.5)
    return jnp.where((query_segment[:, None] == key_segment[None, :])[None], raw_scores, NEGATIVE)


def prefix_scores(queries, prefix_key_rows):
    return jnp.einsum(
        "qhe,khe->hqk",
        split_heads(queries),
        split_heads(prefix_key_rows),
        preferred_element_type=jnp.float32,
    ) * HEAD ** (-0.5)


def gather_weights(shards):
    return (
        lax.all_gather(shards[0], "tok", axis=1, tiled=True),
        lax.all_gather(shards[1], "tok", axis=1, tiled=True),
        lax.all_gather(shards[2], "tok", axis=1, tiled=True),
        lax.all_gather(shards[3], "tok", axis=1, tiled=True),
        lax.all_gather(shards[4], "tok", axis=1, tiled=True),
        lax.all_gather(shards[5], "tok", axis=1, tiled=True),
        lax.all_gather(shards[6], "tok", axis=1, tiled=True),
        lax.all_gather(shards[7], "tok", axis=1, tiled=True),
        lax.all_gather(shards[8], "tok", axis=1, tiled=True),
        lax.all_gather(shards[9], "tok", axis=1, tiled=True),
        lax.all_gather(shards[10], "tok", axis=1, tiled=True),
        lax.all_gather(shards[11], "tok", axis=1, tiled=True),
        lax.all_gather(shards[12], "tok", axis=1, tiled=True),
        lax.all_gather(shards[13], "tok", axis=1, tiled=True),
        lax.all_gather(shards[14], "tok", axis=1, tiled=True),
    )


def front_part(inbound, weights):
    queries = (project(inbound, weights[0]) + weights[1].astype(jnp.float32)).astype(jnp.bfloat16)
    key_rows = project(inbound, weights[2]).astype(jnp.bfloat16)
    value_rows = (project(inbound, weights[3]) + weights[4].astype(jnp.float32)).astype(
        jnp.bfloat16
    )
    return (queries, key_rows, value_rows)


def attention_forward(
    queries, key_rows, value_rows, prefix_key_rows, prefix_value_rows, lengths_row, own_segment
):
    first_scores = prefix_scores(queries, prefix_key_rows)
    highest = jnp.max(first_scores, axis=2)
    denominator = jnp.sum(jnp.exp(first_scores - highest[..., None]), axis=2)

    def total_block(state, piece, offset_row):
        old_high, old_denominator = state
        key_part = piece[0]
        key_segment = segment_of(
            lengths_row, offset_row + jnp.arange(key_part.shape[0], dtype=jnp.int32)
        )
        raw_scores = masked_scores(queries, key_part, own_segment, key_segment)
        new_high = jnp.maximum(old_high, jnp.max(raw_scores, axis=2))
        new_denominator = old_denominator * jnp.exp(old_high - new_high) + jnp.sum(
            jnp.exp(raw_scores - new_high[..., None]), axis=2
        )
        return (new_high, new_denominator)

    highest, denominator = in_blocks(
        total_block,
        (highest, denominator),
        (lax.all_gather(key_rows, "tok", axis=0, tiled=True),),
        jnp.int32(0),
    )
    logsum = highest + jnp.log(denominator)
    summed = jnp.einsum(
        "hqk,khe->qhe",
        jnp.exp(first_scores - logsum[..., None]).astype(jnp.bfloat16),
        split_heads(prefix_value_rows),
        preferred_element_type=jnp.float32,
    )

    def absorb_block(running, piece, offset_row):
        key_part, value_part = piece
        key_segment = segment_of(
            lengths_row, offset_row + jnp.arange(key_part.shape[0], dtype=jnp.int32)
        )
        probs_part = jnp.exp(
            masked_scores(queries, key_part, own_segment, key_segment) - logsum[..., None]
        )
        return running + jnp.einsum(
            "hqk,khe->qhe",
            probs_part.astype(jnp.bfloat16),
            split_heads(value_part),
            preferred_element_type=jnp.float32,
        )

    summed = in_blocks(
        absorb_block,
        summed,
        (
            lax.all_gather(key_rows, "tok", axis=0, tiled=True),
            lax.all_gather(value_rows, "tok", axis=0, tiled=True),
        ),
        jnp.int32(0),
    )
    context = summed.reshape(queries.shape[0], -1)
    return (context, logsum)


def back_part(inbound, context, weights):
    context_low = context.astype(jnp.bfloat16)
    attended = project(context_low, weights[5]) + weights[6].astype(jnp.float32)
    normal_one, pull_one = jax.vjp(
        normalize,
        inbound.astype(jnp.float32) + attended,
        weights[7].astype(jnp.float32),
        weights[8].astype(jnp.float32),
    )
    normal_one_low = normal_one.astype(jnp.bfloat16)
    activation, pull_gelu = jax.vjp(
        gelu_exact, project(normal_one_low, weights[9]) + weights[10].astype(jnp.float32)
    )
    activation_low = activation.astype(jnp.bfloat16)
    mixed = project(activation_low, weights[11]) + weights[12].astype(jnp.float32)
    result, pull_two = jax.vjp(
        normalize,
        normal_one + mixed,
        weights[13].astype(jnp.float32),
        weights[14].astype(jnp.float32),
    )
    return (result, context_low, normal_one_low, pull_one, activation_low, pull_gelu, pull_two)


def query_backward(
    queries,
    d_context,
    logsum,
    delta,
    prefix_key_rows,
    prefix_value_rows,
    key_rows,
    value_rows,
    lengths_row,
    own_segment,
):
    context_heads = split_heads(d_context)
    query_heads = split_heads(queries)
    prefix_prob = jnp.exp(prefix_scores(queries, prefix_key_rows) - logsum[..., None])
    prefix_dprob = jnp.einsum(
        "qhe,khe->hqk",
        context_heads,
        split_heads(prefix_value_rows),
        preferred_element_type=jnp.float32,
    )
    prefix_dscore = (prefix_prob * (prefix_dprob - delta[..., None])).astype(jnp.bfloat16)
    grad_prefix_keys = jnp.einsum(
        "hqk,qhe->khe", prefix_dscore, query_heads, preferred_element_type=jnp.float32
    ) * HEAD ** (-0.5)
    grad_prefix_values = jnp.einsum(
        "hqk,qhe->khe",
        prefix_prob.astype(jnp.bfloat16),
        context_heads,
        preferred_element_type=jnp.float32,
    )
    grad_start = jnp.einsum(
        "hqk,khe->qhe",
        prefix_dscore,
        split_heads(prefix_key_rows),
        preferred_element_type=jnp.float32,
    )

    def pull_block(running, piece, offset_row):
        key_part, value_part = piece
        key_segment = segment_of(
            lengths_row, offset_row + jnp.arange(key_part.shape[0], dtype=jnp.int32)
        )
        probs_part = jnp.exp(
            masked_scores(queries, key_part, own_segment, key_segment) - logsum[..., None]
        )
        dprob = jnp.einsum(
            "qhe,khe->hqk",
            context_heads,
            split_heads(value_part),
            preferred_element_type=jnp.float32,
        )
        dscore = (probs_part * (dprob - delta[..., None])).astype(jnp.bfloat16)
        return running + jnp.einsum(
            "hqk,khe->qhe", dscore, split_heads(key_part), preferred_element_type=jnp.float32
        )

    grad_queries = in_blocks(
        pull_block,
        grad_start,
        (
            lax.all_gather(key_rows, "tok", axis=0, tiled=True),
            lax.all_gather(value_rows, "tok", axis=0, tiled=True),
        ),
        jnp.int32(0),
    )
    row_count = queries.shape[0]
    return (
        (grad_queries * HEAD ** (-0.5)).reshape(row_count, -1),
        grad_prefix_keys.reshape(prefix_key_rows.shape),
        grad_prefix_values.reshape(prefix_value_rows.shape),
    )


def key_backward(queries, d_context, logsum, delta, key_rows, value_rows, lengths_row, own_segment):
    all_logsum, all_delta = (
        lax.all_gather(logsum, "tok", axis=1, tiled=True),
        lax.all_gather(delta, "tok", axis=1, tiled=True),
    )
    value_heads = split_heads(value_rows)

    def spread_block(running, piece, offset_row):
        grad_keys, grad_values = running
        query_part, context_part = piece
        part_rows = query_part.shape[0]
        part_logsum = lax.dynamic_slice_in_dim(all_logsum, offset_row, part_rows, 1)
        part_delta = lax.dynamic_slice_in_dim(all_delta, offset_row, part_rows, 1)
        part_segment = segment_of(lengths_row, offset_row + jnp.arange(part_rows, dtype=jnp.int32))
        probs_part = jnp.exp(
            masked_scores(query_part, key_rows, part_segment, own_segment) - part_logsum[..., None]
        )
        context_heads = split_heads(context_part)
        dprob = jnp.einsum(
            "qhe,khe->hqk", context_heads, value_heads, preferred_element_type=jnp.float32
        )
        dscore = (probs_part * (dprob - part_delta[..., None])).astype(jnp.bfloat16)
        new_keys = grad_keys + jnp.einsum(
            "hqk,qhe->khe", dscore, split_heads(query_part), preferred_element_type=jnp.float32
        )
        new_values = grad_values + jnp.einsum(
            "hqk,qhe->khe",
            probs_part.astype(jnp.bfloat16),
            context_heads,
            preferred_element_type=jnp.float32,
        )
        return (new_keys, new_values)

    def spread(running, piece, offset_row):
        return in_blocks(spread_block, running, piece, offset_row)

    empty = jnp.zeros((key_rows.shape[0], HEADS, HEAD), jnp.float32)
    grad_keys, grad_values = spread(
        (empty, empty),
        (
            lax.all_gather(queries, "tok", axis=0, tiled=True),
            lax.all_gather(d_context, "tok", axis=0, tiled=True),
        ),
        jnp.int32(0),
    )
    row_count = key_rows.shape[0]
    return ((grad_keys * HEAD ** (-0.5)).reshape(row_count, -1), grad_values.reshape(row_count, -1))


def layer_backward(
    inbound, upstream, weights, prefix_key_rows, prefix_value_rows, lengths_row, own_segment
):
    queries, key_rows, value_rows = front_part(inbound, weights)
    context, logsum = attention_forward(
        queries, key_rows, value_rows, prefix_key_rows, prefix_value_rows, lengths_row, own_segment
    )
    result, context_low, normal_one_low, pull_one, activation_low, pull_gelu, pull_two = back_part(
        inbound, context, weights
    )
    d_sum, d_gain_two, d_shift_two = pull_two(upstream.astype(jnp.float32))
    d_mixed = d_sum.astype(jnp.bfloat16)
    grad_down = contract_rows(activation_low, d_mixed)
    grad_down_bias = jnp.sum(d_mixed.astype(jnp.float32), axis=0)
    (d_pre,) = pull_gelu(project_back(d_mixed, weights[11]))
    d_pre_low = d_pre.astype(jnp.bfloat16)
    grad_up = contract_rows(normal_one_low, d_pre_low)
    grad_up_bias = jnp.sum(d_pre_low.astype(jnp.float32), axis=0)
    d_resid, d_gain_one, d_shift_one = pull_one(d_sum + project_back(d_pre_low, weights[9]))
    d_attended = d_resid.astype(jnp.bfloat16)
    grad_out = contract_rows(context_low, d_attended)
    grad_out_bias = jnp.sum(d_attended.astype(jnp.float32), axis=0)
    d_context = project_back(d_attended, weights[5]).astype(jnp.bfloat16)
    delta = jnp.sum(split_heads(d_context).astype(jnp.float32) * split_heads(context), axis=2).T
    grad_queries, grad_prefix_keys, grad_prefix_values = query_backward(
        queries,
        d_context,
        logsum,
        delta,
        prefix_key_rows,
        prefix_value_rows,
        key_rows,
        value_rows,
        lengths_row,
        own_segment,
    )
    grad_keys, grad_values = key_backward(
        queries, d_context, logsum, delta, key_rows, value_rows, lengths_row, own_segment
    )
    queries_low = grad_queries.astype(jnp.bfloat16)
    keys_low = grad_keys.astype(jnp.bfloat16)
    values_low = grad_values.astype(jnp.bfloat16)
    grad_query_weight = contract_rows(inbound, queries_low)
    grad_query_bias = jnp.sum(queries_low.astype(jnp.float32), axis=0)
    grad_key_weight = contract_rows(inbound, keys_low)
    grad_value_weight = contract_rows(inbound, values_low)
    grad_value_bias = jnp.sum(values_low.astype(jnp.float32), axis=0)
    d_input = (
        d_resid
        + project_back(queries_low, weights[0])
        + project_back(keys_low, weights[2])
        + project_back(values_low, weights[3])
    )
    grads = (
        grad_query_weight,
        grad_query_bias,
        grad_key_weight,
        grad_value_weight,
        grad_value_bias,
        grad_out,
        grad_out_bias,
        d_gain_one,
        d_shift_one,
        grad_up,
        grad_up_bias,
        grad_down,
        grad_down_bias,
        d_gain_two,
        d_shift_two,
    )
    return (d_input, grads, (grad_prefix_keys, grad_prefix_values))


def sum_each(grads):
    return (
        lax.psum_scatter(grads[0][None], "tok", scatter_dimension=1, tiled=True),
        lax.psum_scatter(grads[1][None], "tok", scatter_dimension=1, tiled=True),
        lax.psum_scatter(grads[2][None], "tok", scatter_dimension=1, tiled=True),
        lax.psum_scatter(grads[3][None], "tok", scatter_dimension=1, tiled=True),
        lax.psum_scatter(grads[4][None], "tok", scatter_dimension=1, tiled=True),
        lax.psum_scatter(grads[5][None], "tok", scatter_dimension=1, tiled=True),
        lax.psum_scatter(grads[6][None], "tok", scatter_dimension=1, tiled=True),
        lax.psum_scatter(grads[7][None], "tok", scatter_dimension=1, tiled=True),
        lax.psum_scatter(grads[8][None], "tok", scatter_dimension=1, tiled=True),
        lax.psum_scatter(grads[9][None], "tok", scatter_dimension=1, tiled=True),
        lax.psum_scatter(grads[10][None], "tok", scatter_dimension=1, tiled=True),
        lax.psum_scatter(grads[11][None], "tok", scatter_dimension=1, tiled=True),
        lax.psum_scatter(grads[12][None], "tok", scatter_dimension=1, tiled=True),
        lax.psum_scatter(grads[13][None], "tok", scatter_dimension=1, tiled=True),
        lax.psum_scatter(grads[14][None], "tok", scatter_dimension=1, tiled=True),
    )


def by_section(listing, is_first, early_first):
    stacked = jnp.stack(listing)
    window_count = len(listing) - 1
    if early_first:
        return jnp.where(is_first, stacked[:window_count], stacked[1:])
    return jnp.where(is_first, stacked[1:], stacked[:window_count])


def local(
    inputs,
    cotangent,
    lengths,
    prefix_keys,
    prefix_values,
    w_query,
    b_query,
    w_key,
    w_value,
    b_value,
    w_out,
    b_out,
    norm1_gain,
    norm1_shift,
    w_up,
    b_up,
    w_down,
    b_down,
    norm2_gain,
    norm2_shift,
):
    micro_count = inputs.shape[0]
    tok_rows = inputs.shape[1]
    model_width = inputs.shape[2]
    section_index = lax.axis_index("section")
    is_first = section_index == 0
    own_positions = lax.axis_index("tok") * tok_rows + jnp.arange(tok_rows, dtype=jnp.int32)
    shard_list = (
        w_query,
        b_query,
        w_key,
        w_value,
        b_value,
        w_out,
        b_out,
        norm1_gain,
        norm1_shift,
        w_up,
        b_up,
        w_down,
        b_down,
        norm2_gain,
        norm2_shift,
    )
    prefix_key_rows = prefix_keys[0]
    prefix_value_rows = prefix_values[0]
    weights = tuple((member[0] for member in gather_weights(shard_list)))
    received = jnp.zeros((tok_rows, model_width), jnp.bfloat16)
    seen_inputs = []
    seen_outputs = []
    seen_context = []
    seen_logsum = []
    for moment in range(micro_count + 1):
        current = jnp.clip(moment - section_index, 0, micro_count - 1)
        lengths_row = lengths[current]
        own_segment = segment_of(lengths_row, own_positions)
        inbound = jnp.where(is_first, inputs[min(moment, micro_count - 1)], received)
        queries, key_rows, value_rows = front_part(inbound, weights)
        context, logsum = attention_forward(
            queries,
            key_rows,
            value_rows,
            prefix_key_rows,
            prefix_value_rows,
            lengths_row,
            own_segment,
        )
        result = back_part(inbound, context, weights)[0].astype(jnp.bfloat16)
        seen_inputs.append(inbound)
        seen_outputs.append(result)
        seen_context.append(context)
        seen_logsum.append(logsum)
        if moment < micro_count:
            received = from_behind(result, "section", 1)
    kept_inputs = by_section(seen_inputs, is_first, True)
    weights = tuple((member[0] for member in gather_weights(shard_list)))
    back_received = jnp.zeros((tok_rows, model_width), jnp.bfloat16)
    grad_shards = tuple((jnp.zeros(member.shape, jnp.float32) for member in shard_list))
    prefix_key_total = jnp.zeros(prefix_key_rows.shape, jnp.float32)
    prefix_value_total = jnp.zeros(prefix_value_rows.shape, jnp.float32)
    seen_grads = []
    for moment in range(micro_count + 1):
        current = moment - 1 + section_index
        is_valid = ((current >= 0) & (current < micro_count)).astype(jnp.float32)
        picked = jnp.clip(current, 0, micro_count - 1)
        lengths_row = lengths[picked]
        own_segment = segment_of(lengths_row, own_positions)
        upstream = jnp.where(is_first, back_received, cotangent[min(moment, micro_count - 1)])
        d_input, grads, prefix_grads = layer_backward(
            kept_inputs[picked],
            upstream,
            weights,
            prefix_key_rows,
            prefix_value_rows,
            lengths_row,
            own_segment,
        )
        d_input_low = d_input.astype(jnp.bfloat16)
        seen_grads.append(d_input_low)
        if moment < micro_count:
            back_received = from_behind(d_input_low, "section", -1)
        grads = tuple((member * is_valid for member in grads))
        prefix_key_total = prefix_key_total + prefix_grads[0] * is_valid
        prefix_value_total = prefix_value_total + prefix_grads[1] * is_valid
        scattered = sum_each(grads)
        grad_shards = tuple((older + newer for older, newer in zip(grad_shards, scattered)))
    layer_outputs = by_section(seen_outputs, is_first, True)[None]
    input_grads = by_section(seen_grads, is_first, False)[None]
    prefix_sums = lax.psum((prefix_key_total, prefix_value_total), "tok")
    return (
        layer_outputs,
        input_grads,
        grad_shards[0],
        grad_shards[1],
        grad_shards[2],
        grad_shards[3],
        grad_shards[4],
        grad_shards[5],
        grad_shards[6],
        grad_shards[7],
        grad_shards[8],
        grad_shards[9],
        grad_shards[10],
        grad_shards[11],
        grad_shards[12],
        grad_shards[13],
        grad_shards[14],
        prefix_sums[0][None],
        prefix_sums[1][None],
    )


MESH = pl.DeviceIdType.MESH
F32 = jnp.float32
BF16 = jnp.bfloat16
ROWS = 64
PIECE = 32
BLOCK = 256
SQRT_HALF = 0.7071067811865476
INV_SQRT_2PI = 0.3989422804014327
AG_X, AG_N, AG_Z, AG_O = range(4)
RS_O, RS_Z, RS_N, RS_X = range(4)


def flip(bit, other):
    return bit + other - 2 * bit * other


def mm(left, right):
    return jnp.dot(left, right, preferred_element_type=F32)


def mm_nt(left, right):
    return lax.dot_general(left, right, (((1,), (1,)), ((), ())), preferred_element_type=F32)


def mm_tn(left, right):
    return lax.dot_general(left, right, (((0,), (0,)), ((), ())), preferred_element_type=F32)


def rows_at(index, size):
    return pl.ds(pl.multiple_of(index * size, size), size)


def remote(src, dst, send, recv, device):
    return pltpu.make_async_remote_copy(
        src_ref=src, dst_ref=dst, send_sem=send, recv_sem=recv, device_id=device, device_id_type=MESH
    )


def local_copy(src, dst, sem):
    return pltpu.make_async_copy(src, dst, sem)


def bytes_of(ref, sem):
    return pltpu.make_async_copy(ref, ref, sem)


class Place:
    def __init__(self):
        self.x = lax.axis_index("section")
        self.t = lax.axis_index("tok")
        z = self.t // 4
        self.y = (self.t // 2) % 2
        self.core = self.t % 2
        self.cube = z // 2
        self.zl = z % 2
        self.chip = self.x * 4 + self.zl * 2 + self.y
        self.tau = self.chip * 2 + self.core

    def device(self, x, cube):
        return (x, cube * 8 + self.zl * 4 + self.y * 2 + self.core)

    def twin(self):
        return self.device(self.x, 1 - self.cube)

    def sibling(self):
        return (self.x, self.t + 1 - 2 * self.core)

    def peer(self, r):
        zl, y = flip(self.zl, (r // 2) % 2), flip(self.y, r % 2)
        return (flip(self.x, r // 4), self.cube * 8 + zl * 4 + y * 2 + self.core)

    def peer_chip(self, r):
        return flip(self.x, r // 4) * 4 + flip(self.zl, (r // 2) % 2) * 2 + flip(self.y, r % 2)

    def pair_rows(self, j):
        return rows_at(flip(self.x, j // 2) * 2 + flip(self.zl, j % 2), BLOCK)


class Gather:
    HOPS = {(1, 0): (2, 3), (1, 1): (2, 3), (2, 0): (4, 6), (2, 1): (4, 6), (4, 0): (1, 5), (4, 1): (1, 5),
            (3, 0): (4, 7), (6, 1): (1, 7)}

    def __init__(self, place, buf, recv, sib, sends):
        self.place, self.buf, self.recv, self.sib, self.sends = place, buf, recv, sib, sends

    def piece(self, r, q, other=0):
        core = flip(self.place.core, other)
        row = (self.place.peer_chip(r) * 2 + core) * ROWS + q * PIECE
        return self.buf.at[pl.ds(pl.multiple_of(row, PIECE), PIECE)]

    def start(self):
        for q in range(2):
            own = self.piece(0, q)
            for r in (4, 2, 1):
                remote(own, own, self.sends.at[0, r, q], self.recv.at[r, q], self.place.peer(r)).start()
            self.to_sibling(0, q).start()

    def to_sibling(self, r, q):
        rows = self.piece(r, q)
        return remote(rows, rows, self.sends.at[1, r, q], self.sib.at[r, q], self.place.sibling())

    def arrive(self, r, q):
        rows = self.piece(r, q)
        bytes_of(rows, self.recv.at[r, q]).wait()
        if (r, q) in self.HOPS:
            self.onward(r, q).start()
        self.to_sibling(r, q).start()

    def onward(self, r, q):
        hop, seen = self.HOPS[(r, q)]
        rows = self.piece(r, q)
        return remote(rows, rows, self.sends.at[2, r, q], self.recv.at[seen, q], self.place.peer(hop))

    def stage(self, number):
        order = ((1, 2, 4), (3, 6, 5), (7,))[number]
        for q in range(2):
            for r in order:
                self.arrive(r, q)

    def ready(self, r):
        for q in range(2):
            bytes_of(self.piece(r, q, 1), self.sib.at[r, q]).wait()

    def pair_ready(self, j):
        self.ready(2 * j)
        self.ready(2 * j + 1)

    def blocks(self, use):
        for j in range(4):
            if j < 3:
                self.stage(j)
            self.pair_ready(j)
            use(j)
        self.drain()

    def drain(self):
        for q in range(2):
            own = self.piece(0, q)
            for r in (4, 2, 1):
                bytes_of(own, self.sends.at[0, r, q]).wait()
            for r in range(8):
                bytes_of(own, self.sends.at[1, r, q]).wait()
        for r, q in self.HOPS:
            bytes_of(self.piece(0, q), self.sends.at[2, r, q]).wait()


class Scatter:
    def __init__(self, place, recv, sends, half, keep, sib_out, sib_in, out, inbox):
        self.place, self.recv, self.sends = place, recv, sends
        self.half, self.keep, self.sib_out, self.sib_in = half, keep, sib_out, sib_in
        self.out, self.inbox = out, inbox

    def pair(self, r):
        return remote(
            self.sib_out.at[r], self.sib_in.at[r], self.sends.at[0, r], self.recv.at[0, r], self.place.sibling()
        )

    def push(self, r):
        return remote(
            self.out.at[r], self.inbox.at[r], self.sends.at[1, r], self.recv.at[1, r], self.place.peer(r)
        )

    def give(self, j, partial):
        for k in range(4):
            self.half[k] = partial[k * ROWS : (k + 1) * ROWS]
        core = self.place.core
        for b in range(2):
            r = 2 * j + flip(self.place.y, b)
            self.keep[r] = self.half[2 * b + core]
            self.sib_out[r] = self.half[2 * b + 1 - core].astype(BF16)
            self.pair(r).start()

    def forward(self, j):
        for k in (1, 0):
            r = 2 * j + k
            self.pair(r).wait_recv()
            total = self.keep[r] + self.sib_in[r].astype(F32)

            @pl.when(r == 0)
            def _():
                self.keep[0] = total

            @pl.when(r != 0)
            def _():
                self.out[r] = total.astype(BF16)
                self.push(r).start()

    def run(self, produce):
        def step(i, carry):
            @pl.when(i < 4)
            def _():
                self.give(3 - i, produce(3 - i))

            @pl.when(i >= 1)
            def _():
                self.forward(4 - i)

            return carry

        lax.fori_loop(0, 5, step, 0)

    def finish(self):
        def collect(r, carry):
            self.push(r).wait_recv()
            self.keep[0] = self.keep[0] + self.inbox[r].astype(F32)
            return carry

        lax.fori_loop(1, 8, collect, 0)

        def drain(r, carry):
            self.pair(r).wait_send()

            @pl.when(r >= 1)
            def _():
                self.push(r).wait_send()

            return carry

        lax.fori_loop(0, 8, drain, 0)
        return self.keep[0]


def norm_forward(value, gain, shift, hat_ref, rstd_ref):
    centred = value - jnp.mean(value, axis=-1, keepdims=True)
    rstd = lax.rsqrt(jnp.mean(centred * centred, axis=-1, keepdims=True) + 1e-05)
    hat = centred * rstd
    hat_ref[...] = hat
    rstd_ref[...] = jnp.broadcast_to(rstd, rstd_ref.shape)
    return hat * gain + shift


def norm_backward(upstream, gain, hat_ref, rstd_ref):
    hat = hat_ref[...]
    scaled = upstream * gain
    mean_one = jnp.mean(scaled, axis=-1, keepdims=True)
    mean_two = jnp.mean(scaled * hat, axis=-1, keepdims=True)
    result = rstd_ref[:, :1] * (scaled - mean_one - hat * mean_two)
    d_gain = jnp.sum(upstream * hat, axis=0, keepdims=True)
    d_shift = jnp.sum(upstream, axis=0, keepdims=True)
    return result, d_gain, d_shift


def column_sum(low):
    return jnp.sum(low.astype(F32), axis=0, keepdims=True)


def kernel(
    lengths, inputs, cotangent, wqkv_src, wup_src, wdn_src, wout_src, pk_src, pv_src,
    out_y, out_dx, got_qkv, got_up, got_dn, got_out, got_prefix, got_rows, got_bias,
    ag_recv, ag_sib, ag_send, rs_recv, rs_send,
    wsend, wown, wtwin, wrelay, psem, xsem, osend, orecv, tsend, trecv, gsend, grecv,
    wqkv, wup, wdn, wout, pre,
    qseg, kseg, xg, ng, dzg, dog, param,
    qs, ks, vs, kt, vt, lse, ctb, ctf,
    hat1, rstd1, hat2, rstd2, act, dact,
    half, keep, sib_out, sib_in, rs_out, inbox,
    own_a, own_b, ystage, dstage,
    dfs, dcb, delta, dqt, dkacc, dvacc, dqkv, dqkvt,
    rowacc, biasacc, g_qkv, g_up, g_dn, g_out, g_prefix,
    t_qkv, t_up, t_dn, t_out, t_prefix,
):
    place = Place()
    x, t, cube, core, tau = place.x, place.t, place.cube, place.core, place.tau
    tokens = qs.shape[1]
    width = xg.shape[2]
    half_rows = 8 * ROWS
    barrier = pltpu.get_barrier_semaphore()

    def greet(i, carry):
        gx, gt = i // 16, i % 16

        @pl.when((gx != x) | (gt != t))
        def _():
            pl.semaphore_signal(barrier, inc=1, device_id=(gx, gt), device_id_type=MESH)

        return carry

    lax.fori_loop(0, 32, greet, 0)
    pl.semaphore_wait(barrier, 31)

    own_rows = rows_at(tau, ROWS)
    x_here = local_copy(inputs.at[cube], xg.at[0, own_rows], xsem.at[0])
    x_there = remote(inputs.at[1 - cube], xg.at[0, own_rows], xsem.at[1], xsem.at[2], place.twin())
    d_here = local_copy(cotangent.at[cube], dstage.at[2], xsem.at[3])
    d_there = remote(cotangent.at[1 - cube], dstage.at[2], xsem.at[4], xsem.at[5], place.twin())

    @pl.when(x == cube)
    def _():
        x_there.start()
        x_here.start()

    def spread_out(kind):
        src_all, dst_all = ((wqkv_src, wqkv), (wup_src, wup))[kind]

        def one(k, carry):
            to = lax.rem(k + tau + 1, 16)
            src, dst = src_all.at[to], dst_all.at[rows_at(x * 16 + t, ROWS)]
            sem = wown.at[kind, x, t % 8]

            @pl.when(to == tau)
            def _():
                local_copy(src, dst, sem).start()

            @pl.when(to != tau)
            def _():
                remote(src, dst, wsend.at[kind], sem, (to // 8, cube * 8 + to % 8)).start()

            return carry

        lax.fori_loop(0, 16, one, 0)

    def slices_out():
        for side in range(2):
            src = wdn_src.at[0, pl.ds(side * 128, 128)]
            dst = wdn.at[x, rows_at(cube, 128)]
            pl.when(x == side)(local_copy(src, dst, wown.at[3, x, 0]).start)
            pl.when(x != side)(remote(src, dst, wsend.at[3], wown.at[3, x, 0], place.device(1 - x, cube)).start)
        src, dst = wout_src.at[0], wout.at[x]
        pl.when(x == cube)(local_copy(src, dst, wown.at[2, x, 0]).start)
        pl.when(x != cube)(remote(src, dst, wsend.at[2], wown.at[2, x, 0], place.device(1 - x, cube)).start)

    def prefix_out():
        for side, index in ((x, 0), (1 - x, 1)):
            for kind, src_all in ((0, pk_src), (1, pv_src)):
                src = src_all.at[0, :, rows_at(side * 4 + place.zl * 2 + place.y, 128)]
                dst = pre.at[x, kind]
                if index == 0:
                    yield local_copy(src, dst, psem.at[0, kind])
                else:
                    yield remote(src, dst, psem.at[1, kind], psem.at[2, kind], place.device(1 - x, cube))

    def twin_copy(kind, l):
        if kind < 2:
            ref = (wqkv, wup)[kind].at[rows_at(l * 2 + cube, half_rows)]
        elif kind == 3:
            ref = wdn.at[l, rows_at(cube, 128)]
        else:
            ref = wout.at[l]
        return remote(ref, ref, wrelay.at[kind, l], wtwin.at[kind, l], place.twin())

    def relay_blocks(kind, l):
        ref_all = (wqkv, wup)[kind]

        def one(k, carry):
            ref = ref_all.at[rows_at((l * 2 + cube) * 8 + k, ROWS)]
            bytes_of(ref, wown.at[kind, l, k]).wait()
            remote(ref, ref, wrelay.at[kind, l], wtwin.at[kind, l], place.twin()).start()
            return carry

        lax.fori_loop(0, 8, one, 0)

    def relay_slices(l):
        dn = wdn.at[l, rows_at(cube, 128)]
        bytes_of(dn, wown.at[3, l, 0]).wait()
        twin_copy(3, l).start()

        @pl.when(x == cube)
        def _():
            bytes_of(wout.at[l], wown.at[2, l, 0]).wait()
            twin_copy(2, l).start()

    def weights_in(kind, l):
        if kind < 2:
            ref = (wqkv, wup)[kind].at[rows_at(l * 2 + 1 - cube, half_rows)]
        elif kind == 3:
            ref = wdn.at[l, rows_at(1 - cube, 128)]
        else:
            ref = wout.at[l]
        wait = bytes_of(ref, wtwin.at[kind, l]).wait
        if kind == 2:
            pl.when(x != cube)(wait)
        else:
            wait()

    def weights_drain():
        for kind, ref in ((0, wqkv), (1, wup)):
            bytes_of(ref.at[pl.ds(0, 15 * ROWS)], wsend.at[kind]).wait()
        bytes_of(wdn.at[0, pl.ds(0, 128)], wsend.at[3]).wait()
        pl.when(x != cube)(bytes_of(wout.at[0], wsend.at[2]).wait)
        for l in range(2):
            for kind in (0, 1, 3):
                twin_copy(kind, l).wait_send()
            pl.when(x == cube)(twin_copy(2, l).wait_send)

    def weight(ref, l):
        return ref[rows_at(l, 16 * ROWS)]

    def own_half(pair):
        return jnp.where(core == 0, pair[:, :64], pair[:, 64:])

    def gather(buf, phase):
        return Gather(place, buf, ag_recv.at[phase], ag_sib.at[phase], ag_send)

    def scatter(phase):
        boxes = phase % 2
        return Scatter(
            place, rs_recv.at[phase], rs_send, half, keep, sib_out, sib_in.at[boxes], rs_out, inbox.at[boxes]
        )

    prefixes = list(prefix_out())
    for copy in prefixes:
        copy.start()

    @pl.when(x == 0)
    def _():
        spread_out(0)

    rowacc[...] = jnp.zeros_like(rowacc)
    biasacc[...] = jnp.zeros_like(biasacc)
    dqt[64:128] = jnp.zeros((64, tokens), F32)
    along = lax.broadcasted_iota(jnp.int32, (8, tokens), 1)
    down = lax.broadcasted_iota(jnp.int32, (tokens, 128), 0)
    segment_q, segment_k = jnp.zeros((8, tokens), jnp.int32), jnp.zeros((tokens, 128), jnp.int32)
    end = jnp.int32(0)
    for j in range(lengths.shape[1]):
        end = end + lengths[cube, j]
        segment_q = segment_q + (along >= end).astype(jnp.int32)
        segment_k = segment_k + (down >= end).astype(jnp.int32)
    qseg[...] = segment_q
    kseg[0:tokens] = segment_k
    kseg[tokens:] = jnp.full((kseg.shape[0] - tokens, 128), -1, jnp.int32)

    pl.when(x != cube)(x_there.wait_recv)
    pl.when(x == cube)(x_here.wait)

    def result_out(stage, out, kind, layer):
        dst = out.at[cube]
        is_self = (layer == x) & (x == cube)
        here = local_copy(stage, dst, orecv.at[kind, cube])
        there = remote(stage, dst, osend.at[kind, layer], orecv.at[kind, cube], place.device(layer, x))
        return is_self, here, there

    def visible(cols):
        key_part = kseg[...]
        keys_two = jnp.concatenate([key_part, key_part], axis=1)
        return (keys_two == qseg[0:1, cols]) | (keys_two < 0)

    def forward_layer(l, carry):
        gather_x = gather(xg.at[l], AG_X)
        gather_x.start()

        @pl.when(l == 0)
        def _():
            @pl.when(x == 0)
            def _():
                spread_out(1)
                slices_out()

            @pl.when(x == cube)
            def _():
                d_there.start()
                d_here.start()

            for number in range(3):
                gather_x.stage(number)
            relay_blocks(0, 0)
            for copy in prefixes[:2]:
                copy.wait()
            for copy in prefixes[2:]:
                copy.wait()

        weights_in(0, l)
        tail = wqkv[rows_at(l, 16 * ROWS), 128:256].astype(F32).T
        param[l] = tail[64:80]
        biases = own_half(param[l, 0:8, rows_at(tau // 2, 128)])[6:8]
        empty = jnp.zeros((1, 64), F32)
        qkv_bias = jnp.concatenate([biases[0:1], empty, biases[1:2], empty], axis=1)
        prefix = jnp.concatenate(
            [own_half(pre[l, 0].astype(F32)), own_half(pre[l, 1].astype(F32))], axis=1
        )
        ks[l, tokens:] = prefix[:, :64].astype(BF16)
        vs[l, tokens:] = prefix[:, 64:].astype(BF16)
        prefix_t = prefix.T
        kt[l, :, tokens:] = prefix_t[:64].astype(BF16)
        vt[l, :, tokens:] = prefix_t[64:].astype(BF16)

        for j in range(4):
            if j < 3:
                @pl.when(l == 1)
                def _():
                    gather_x.stage(j)

            gather_x.pair_ready(j)
            rows = place.pair_rows(j)
            value = mm(xg[l, rows], weight(wqkv, l)) + qkv_bias
            qs[l, rows] = (value[:, :64] * 0.125).astype(BF16)
            ks[l, rows] = value[:, 64:128].astype(BF16)
            vs[l, rows] = value[:, 128:192].astype(BF16)
            value_t = value.T
            kt[l, :, rows] = value_t[64:128].astype(BF16)
            vt[l, :, rows] = value_t[128:192].astype(BF16)
        gather_x.drain()

        @pl.when(l == 0)
        def _():
            relay_slices(0)
            relay_blocks(1, 0)

            @pl.when(x == 1)
            def _():
                spread_out(0)
                slices_out()
                spread_out(1)

        scatter_o = scatter(RS_O)

        def attend(j):
            cols = place.pair_rows(j)
            scores = jnp.where(visible(cols), mm_nt(ks[l], qs[l, cols]), NEGATIVE)
            top = jnp.max(scores, axis=0, keepdims=True)
            grown = jnp.exp(scores - top)
            total = jnp.sum(grown, axis=0, keepdims=True)
            probs = (grown * (1.0 / total)).astype(BF16)
            lse[l, 0:1, cols] = top + jnp.log(total)
            context_t = mm(vt[l], probs)
            ctf[l, :, cols] = context_t
            low = context_t.astype(BF16)
            ctb[l, :, cols] = low
            return mm_tn(low, wout[l])

        pl.when(l == 0)(lambda: weights_in(2, 0))
        pl.when(l == 1)(lambda: weights_in(2, 1))
        scatter_o.run(attend)
        attended = scatter_o.finish() + param[l, 0:1]
        normal = norm_forward(
            xg[l, own_rows].astype(F32) + attended,
            param[l, 1:2], param[l, 2:3], hat1.at[l], rstd1.at[l],
        )
        own_a[...] = normal
        ng[l, own_rows] = normal.astype(BF16)
        gather_n = gather(ng.at[l], AG_N)
        gather_n.start()

        @pl.when(l == 0)
        def _():
            relay_blocks(0, 1)

        weights_in(1, l)
        weights_in(3, l)
        up_part = own_half(param[l, 8:16, rows_at(place.zl * 2 + place.y, 128)])
        up_more = own_half(param[l, 8:16, rows_at(4 + place.zl * 2 + place.y, 128)])
        up_parts = jnp.where(x == 0, up_part[0:2], up_part[2:4])
        up_more = jnp.where(x == 0, up_more[0:2], up_more[2:4])
        up_bias = jnp.concatenate([up_parts[0:1], up_parts[1:2], up_more[0:1], up_more[1:2]], axis=1)
        scatter_z = scatter(RS_Z)

        def feed_block(j):
            rows = place.pair_rows(j)
            value = mm(ng[l, rows], weight(wup, l)) + up_bias
            cdf = 0.5 * (1.0 + lax.erf(value * SQRT_HALF))
            low = (value * cdf).astype(BF16)
            act[l, rows] = low
            dact[l, rows] = cdf + value * (jnp.exp(-0.5 * value * value) * INV_SQRT_2PI)
            scatter_z.give(j, mm(low, wdn[l]))
            if j:
                scatter_z.forward(j - 1)

        gather_n.blocks(feed_block)
        scatter_z.forward(3)

        @pl.when(l == 0)
        def _():
            relay_slices(1)
            relay_blocks(1, 1)

        mixed = scatter_z.finish() + param[l, 3:4]
        result = norm_forward(
            own_a[...] + mixed, param[l, 4:5], param[l, 5:6], hat2.at[l], rstd2.at[l]
        ).astype(BF16)
        ystage[l] = result

        @pl.when(l == 0)
        def _():
            xg[1, own_rows] = result

        is_self, here, there = result_out(ystage.at[l], out_y, 0, l)
        pl.when(is_self)(here.start)
        pl.when(jnp.logical_not(is_self))(there.start)
        return carry

    lax.fori_loop(0, 2, forward_layer, 0)

    pl.when(x != cube)(d_there.wait_recv)
    pl.when(x == cube)(d_here.wait)

    other_half, this_half = 1 - cube, cube

    def twin_parts(kind, l):
        if kind < 2:
            ref, box = ((g_qkv, t_qkv), (g_up, t_up))[kind]
            return ref.at[l, rows_at(other_half, half_rows)], box, ref.at[l, rows_at(this_half, half_rows)]
        if kind == 2:
            return g_prefix.at[l, rows_at(other_half, 32)], t_prefix, g_prefix.at[l, rows_at(this_half, 32)]
        if kind == 3:
            return g_dn.at[l, rows_at(other_half, 128)], t_dn, g_dn.at[l, rows_at(this_half, 128)]
        return g_out.at[l], t_out, g_out.at[l]

    def twin_send(kind, l):
        src, box, own = twin_parts(kind, l)
        return remote(src, box.at[l], tsend.at[kind, l], trecv.at[kind, l], place.twin())

    def twin_start(kind, l):
        copy = twin_send(kind, l)
        if kind == 4:
            pl.when(x != cube)(copy.start)
        else:
            copy.start()

    def owner_copies(kind, l, act_on):
        src, box, own = twin_parts(kind, l)
        mine = x == l
        if kind < 2:
            got = (got_qkv, got_up)[kind]

            def one(k, carry):
                to = lax.rem(k + t + 1, 8)
                src, dst = own.at[rows_at(to, ROWS)], got.at[tau]
                is_self = mine & (to == t % 8)
                act_on(is_self, src, dst, (l, cube * 8 + to))
                return carry

            lax.fori_loop(0, 8, one, 0)
        elif kind == 2:

            def one(k, carry):
                to = lax.rem(k + t + 1, 16)
                act_on(mine & (to == t), own, got_prefix.at[tau, rows_at(this_half, 32)], (l, to))
                return carry

            lax.fori_loop(0, 16, one, 0)
        elif kind == 3:
            act_on(mine, own, got_dn.at[rows_at(x, 128)], place.device(l, cube))
        else:

            @pl.when(x == cube)
            def _():
                act_on(mine, own, got_out, place.device(l, cube))

    def start_on(kind, l):
        def act_on(is_self, src, dst, dev):
            pl.when(is_self)(local_copy(src, dst, grecv.at[kind]).start)
            pl.when(jnp.logical_not(is_self))(remote(src, dst, gsend.at[kind, l], grecv.at[kind], dev).start)

        return act_on

    def owner_start(kind, l):
        src, box, own = twin_parts(kind, l)

        def add():
            twin_send(kind, l).wait_recv()
            own[...] = (own[...].astype(F32) + box[l].astype(F32)).astype(BF16)

        if kind == 4:
            pl.when(x == cube)(add)
        else:
            add()
        owner_copies(kind, l, start_on(kind, l))

    def grads_drain(l):
        for kind in range(5):
            if kind == 4:
                pl.when(x != cube)(twin_send(kind, l).wait_send)
            else:
                twin_send(kind, l).wait_send()
        for kind, ref in ((0, got_qkv), (1, got_up)):
            pl.when(x == l)(bytes_of(ref.at[pl.ds(0, 7)], gsend.at[kind, l]).wait)
            pl.when(x != l)(bytes_of(ref.at[pl.ds(0, 8)], gsend.at[kind, l]).wait)
        for count, condition in ((15, x == l), (16, x != l)):
            pl.when(condition)(bytes_of(got_prefix.at[pl.ds(0, count), pl.ds(0, 32)], gsend.at[2, l]).wait)
            pl.when(condition)(bytes_of(got_rows.at[pl.ds(0, count)], gsend.at[5, l]).wait)
        pl.when(x != l)(bytes_of(g_dn.at[0, pl.ds(0, 128)], gsend.at[3, l]).wait)
        pl.when((x != l) & (x == cube))(bytes_of(g_out.at[0], gsend.at[4, l]).wait)
        for to, src, dst in bias_pairs(l):
            is_self = (x == l) & (cube == to)
            pl.when(jnp.logical_not(is_self))(bytes_of(src, gsend.at[6 + to, l]).wait)

    def rows_start(l):
        def one(k, carry):
            to = lax.rem(k + t + 1, 16)
            src, dst = rowacc.at[l, :, rows_at(to // 2, 128)], got_rows.at[cube * 16 + tau]
            is_self = (x == l) & (to == t)
            pl.when(is_self)(local_copy(src, dst, grecv.at[5]).start)
            pl.when(jnp.logical_not(is_self))(remote(src, dst, gsend.at[5, l], grecv.at[5], (l, to)).start)
            return carry

        lax.fori_loop(0, 16, one, 0)

    def bias_pairs(l):
        for to in range(2):
            yield to, biasacc.at[l], got_bias.at[cube * 2 + x]

    def bias_start(l):
        for to, src, dst in bias_pairs(l):
            is_self = (x == l) & (cube == to)
            pl.when(is_self)(local_copy(src, dst, grecv.at[6]).start)
            pl.when(jnp.logical_not(is_self))(
                remote(src, dst, gsend.at[6 + to, l], grecv.at[6], place.device(l, to)).start
            )

    def backward_layer(step, carry):
        l = 1 - step
        upstream = dstage[l + 1].astype(F32)
        d_sum, d_gain, d_shift = norm_backward(upstream, param[l, 4:5], hat2.at[l], rstd2.at[l])
        own_b[...] = d_sum
        low = d_sum.astype(BF16)
        dzg[own_rows] = low
        gather_z = gather(dzg, AG_Z)
        gather_z.start()
        rowacc[l, 3:4] = d_gain
        rowacc[l, 4:5] = d_shift
        rowacc[l, 5:6] = column_sum(low)
        scatter_n = scatter(RS_N)

        def back_block(j):
            rows = place.pair_rows(j)
            low = (dact[l, rows] * mm_nt(dzg[rows], wdn[l])).astype(BF16)
            dfs[rows] = low
            scatter_n.give(j, mm_nt(low, weight(wup, l)))
            if j:
                scatter_n.forward(j - 1)

        gather_z.blocks(back_block)
        scatter_n.forward(3)
        biasacc[l, 1:2] = column_sum(dfs[...])

        def down_tile(i, carry):
            cols = rows_at(i, 256)
            g_dn[l, :, cols] = mm_tn(act[l], dzg[:, cols]).astype(BF16)
            return carry

        lax.fori_loop(0, width // 256, down_tile, 0)

        def up_tile(i, carry):
            cols = rows_at(i, 256)
            g_up[l, cols] = mm_tn(ng[l, :, cols], dfs[...]).astype(BF16)
            return carry

        lax.fori_loop(0, width // 256, up_tile, 0)
        twin_start(3, l)
        twin_start(1, l)

        @pl.when(step == 1)
        def _():
            owner_start(0, 1)
            owner_start(4, 1)

        d_normal = own_b[...] + scatter_n.finish()
        d_sum, d_gain, d_shift = norm_backward(d_normal, param[l, 1:2], hat1.at[l], rstd1.at[l])
        own_a[...] = d_sum
        low = d_sum.astype(BF16)
        dog[own_rows] = low
        gather_o = gather(dog, AG_O)
        gather_o.start()
        rowacc[l, 0:1] = d_gain
        rowacc[l, 1:2] = d_shift
        rowacc[l, 2:3] = column_sum(low)
        rows_start(l)
        dkacc[...] = jnp.zeros_like(dkacc)
        dvacc[...] = jnp.zeros_like(dvacc)

        def attend_back(j):
            cols = place.pair_rows(j)
            d_context = mm_nt(dog[cols], wout[l]).astype(BF16)
            dcb[cols] = d_context
            d_context_t = mm_nt(wout[l], dog[cols]).astype(BF16).astype(F32)
            sums = jnp.sum(d_context_t * ctf[l, :, cols], axis=0, keepdims=True)
            scores = jnp.where(visible(cols), mm_nt(ks[l], qs[l, cols]), NEGATIVE)
            probs = jnp.exp(scores - lse[l, 0:1, cols])
            d_probs = mm_nt(vs[l], d_context)
            d_scores = (probs * (d_probs - sums)).astype(BF16)
            dvacc[...] += mm(probs.astype(BF16), d_context)
            dkacc[...] += mm(d_scores, qs[l, cols])
            dqt[0:64, cols] = mm(kt[l], d_scores) * 0.125

        gather_o.blocks(attend_back)
        g_prefix[l] = jnp.concatenate([dkacc[tokens:], dvacc[tokens:]], axis=1).astype(BF16)
        twin_start(2, l)
        scatter_x = scatter(RS_X)

        def assemble(j):
            rows = place.pair_rows(j)
            d_query = dqt[:, rows].T[:, :64]
            value = jnp.concatenate(
                [d_query, dkacc[rows], dvacc[rows], jnp.zeros((BLOCK, 64), F32)], axis=1
            )
            low = value.astype(BF16)
            dqkv[rows] = low
            dqkvt[:, rows] = value.T.astype(BF16)
            return mm_nt(low, weight(wqkv, l))

        scatter_x.run(assemble)
        biasacc[l, 0:1] = column_sum(dqkv[...])
        bias_start(l)

        def qkv_tile(i, carry):
            cols = rows_at(i, 256)
            g_qkv[l, cols] = mm(dqkvt[...], xg[l, :, cols]).T.astype(BF16)
            return carry

        lax.fori_loop(0, width // 256, qkv_tile, 0)
        twin_start(0, l)
        g_out[l] = mm(ctb[l], dog[...]).astype(BF16)
        twin_start(4, l)
        for kind in (3, 1, 2):
            owner_start(kind, l)

        dstage[l] = (own_a[...] + scatter_x.finish()).astype(BF16)
        is_self, here, there = result_out(dstage.at[l], out_dx, 1, l)
        pl.when(is_self)(here.start)
        pl.when(jnp.logical_not(is_self))(there.start)
        return carry

    lax.fori_loop(0, 2, backward_layer, 0)
    owner_start(0, 0)
    owner_start(4, 0)

    @pl.when(x == cube)
    def _():
        x_there.wait_send()
        d_there.wait_send()

    weights_drain()
    for l in range(2):
        grads_drain(l)
        for kind, stage, out in ((0, ystage.at[l], out_y), (1, dstage.at[l], out_dx)):
            is_self, here, there = result_out(stage, out, kind, l)
            pl.when(jnp.logical_not(is_self))(there.wait_send)
    for kind, out in ((0, out_y), (1, out_dx)):
        for m in range(2):
            bytes_of(out.at[m], orecv.at[kind, m]).wait()
    for kind, ref in enumerate((got_qkv, got_up, got_prefix, got_dn, got_out, got_rows, got_bias)):
        bytes_of(ref, grecv.at[kind]).wait()


def cube_local(
    inputs, cotangent, lengths, prefix_keys, prefix_values,
    w_query, b_query, w_key, w_value, b_value, w_out, b_out, norm1_gain, norm1_shift,
    w_up, b_up, w_down, b_down, norm2_gain, norm2_shift,
):
    t = lax.axis_index("tok")
    rows, width = w_query.shape[1], w_query.shape[2]
    heads = width // HEAD
    tokens = inputs.shape[1] * lax.axis_size("tok")
    prefix = prefix_keys.shape[1]
    keys = tokens + prefix
    hidden = b_up.shape[1]

    def by_head(value):
        return value[0].reshape(rows, heads, HEAD).transpose(1, 0, 2)

    vectors = jnp.concatenate(
        [b_out, norm1_gain, norm1_shift, b_down, norm2_gain, norm2_shift, b_query, b_value,
         b_up.reshape(4, HEAD), jnp.zeros((HEAD - 12, HEAD), BF16)], axis=0,
    ).T
    wqkv_src = jnp.concatenate(
        [by_head(w_query), by_head(w_key), by_head(w_value),
         jnp.broadcast_to(vectors[None], (heads, rows, HEAD))], axis=-1,
    )
    wup_src = w_up[0].reshape(rows, 2, 8, 2, 128).transpose(3, 2, 0, 1, 4).reshape(heads, rows, 256)
    anywhere = pl.BlockSpec(memory_space=pl.ANY)
    smem = pl.BlockSpec(memory_space=pltpu.SMEM)
    dma = pltpu.SemaphoreType.DMA
    V = pltpu.VMEM
    L = 2
    shape = jax.ShapeDtypeStruct
    results = pl.pallas_call(
        kernel,
        out_shape=(
            shape((2, ROWS, width), BF16), shape((2, ROWS, width), BF16),
            shape((16, ROWS, 256), BF16), shape((16, ROWS, 256), BF16),
            shape((hidden, width), BF16), shape((ROWS, width), BF16),
            shape((16, prefix, 128), BF16), shape((32, 8, 128), F32), shape((4, 8, 256), F32),
        ),
        in_specs=[smem] + [anywhere] * 8,
        out_specs=[anywhere] * 9,
        scratch_shapes=[
            dma((4, 8, 2)), dma((4, 8, 2)), dma((3, 8, 2)), dma((4, 2, 8)), dma((2, 8)),
            dma((4,)), dma((4, 2, 8)), dma((4, 2)), dma((4, 2)), dma((3, 2)), dma((6,)),
            dma((2, 2)), dma((2, 2)), dma((5, 2)), dma((5, 2)), dma((8, 2)), dma((7,)),
            V((L * 1024, 256), BF16), V((L * 1024, 256), BF16), V((L, hidden, width), BF16),
            V((L, ROWS, width), BF16), V((L, 2, prefix, 128), BF16),
            V((8, tokens), jnp.int32), V((keys, 128), jnp.int32),
            V((L, tokens, width), BF16), V((L, tokens, width), BF16),
            V((tokens, width), BF16), V((tokens, width), BF16), V((L, 16, width), F32),
            V((L, tokens, HEAD), BF16), V((L, keys, HEAD), BF16), V((L, keys, HEAD), BF16),
            V((L, HEAD, keys), BF16), V((L, HEAD, keys), BF16),
            V((L, 8, tokens), F32), V((L, HEAD, tokens), BF16), V((L, HEAD, tokens), F32),
            V((L, ROWS, width), F32), V((L, ROWS, 128), F32), V((L, ROWS, width), F32), V((L, ROWS, 128), F32),
            V((L, tokens, hidden), BF16), V((L, tokens, hidden), F32),
            V((4, ROWS, width), F32), V((8, ROWS, width), F32), V((8, ROWS, width), BF16),
            V((2, 8, ROWS, width), BF16), V((8, ROWS, width), BF16), V((2, 8, ROWS, width), BF16),
            V((ROWS, width), F32), V((ROWS, width), F32), V((L, ROWS, width), BF16), V((L + 1, ROWS, width), BF16),
            V((tokens, hidden), BF16), V((tokens, HEAD), BF16), V((8, tokens), F32), V((128, tokens), F32),
            V((keys, HEAD), F32), V((keys, HEAD), F32), V((tokens, 256), BF16), V((256, tokens), BF16),
            V((L, 8, width), F32), V((L, 8, 256), F32),
            V((L, width, 256), BF16), V((L, width, 256), BF16), V((L, hidden, width), BF16),
            V((L, ROWS, width), BF16), V((L, prefix, 128), BF16),
            V((L, width // 2, 256), BF16), V((L, width // 2, 256), BF16), V((L, hidden // 2, width), BF16),
            V((L, ROWS, width), BF16), V((L, prefix // 2, 128), BF16),
        ],
        compiler_params=pltpu.CompilerParams(
            collective_id=0, has_side_effects=True, vmem_limit_bytes=60 * 2**20
        ),
    )(lengths, inputs, cotangent, wqkv_src, wup_src, w_down, w_out, prefix_keys, prefix_values)
    out_y, out_dx, got_qkv, got_up, got_dn, got_out, got_prefix, got_rows, got_bias = results

    def side_by_side(value):
        return value.astype(F32).transpose(1, 0, 2).reshape(1, value.shape[1], -1)

    up = got_up.reshape(2, 8, rows, 2, 128).transpose(2, 3, 1, 0, 4).astype(F32)
    row_sum = lax.dynamic_slice_in_dim(jnp.sum(got_rows, axis=0), (t % 2) * 64, 64, 1)
    side = t // 8
    bias = got_bias[:2] + got_bias[2:]
    bias_up = lax.dynamic_slice_in_dim(bias[:, 1], side * 128, 128, 1).reshape(1, hidden)
    bias_qkv = lax.dynamic_index_in_dim(bias[:, 0], side, 0, keepdims=True)
    return (
        out_y[None],
        out_dx[None],
        side_by_side(got_qkv[:, :, :64]),
        bias_qkv[:, 0:64],
        side_by_side(got_qkv[:, :, 64:128]),
        side_by_side(got_qkv[:, :, 128:192]),
        bias_qkv[:, 128:192],
        got_out[None].astype(F32),
        row_sum[2:3],
        row_sum[0:1],
        row_sum[1:2],
        up.reshape(1, rows, -1),
        bias_up,
        got_dn[None].astype(F32),
        row_sum[5:6],
        row_sum[3:4],
        row_sum[4:5],
        side_by_side(got_prefix[:, :, :64]),
        side_by_side(got_prefix[:, :, 64:]),
    )


def solution(mesh):
    placed = (
        P(None, "tok", None),
        P(None, "tok", None),
        P(),
        P("section", None, None),
        P("section", None, None),
        P("section", "tok", None),
        P("section", "tok"),
        P("section", "tok", None),
        P("section", "tok", None),
        P("section", "tok"),
        P("section", "tok", None),
        P("section", "tok"),
        P("section", "tok"),
        P("section", "tok"),
        P("section", "tok", None),
        P("section", "tok"),
        P("section", "tok", None),
        P("section", "tok"),
        P("section", "tok"),
        P("section", "tok"),
    )
    return jax.shard_map(
        cube_local if mesh.shape["tok"] == HEADS else local,
        mesh=mesh,
        in_specs=placed,
        out_specs=(
            P("section", None, "tok", None),
            P("section", None, "tok", None),
            P("section", "tok", None),
            P("section", "tok"),
            P("section", "tok", None),
            P("section", "tok", None),
            P("section", "tok"),
            P("section", "tok", None),
            P("section", "tok"),
            P("section", "tok"),
            P("section", "tok"),
            P("section", "tok", None),
            P("section", "tok"),
            P("section", "tok", None),
            P("section", "tok"),
            P("section", "tok"),
            P("section", "tok"),
            P("section", None, None),
            P("section", None, None),
        ),
        check_vma=False,
    )
```

```python
import jax
import jax.numpy as jnp
from jax import lax
from jax.experimental import pallas as pl
from jax.experimental.pallas import tpu as pltpu
from jax.sharding import PartitionSpec as P

HEADS = 16
HEAD = 64


NEGATIVE = -1e30


def from_behind(block, axis, distance):
    devices = range(lax.axis_size(axis))
    route = [(i - distance, i) for i in devices if i - distance in devices]
    return lax.ppermute(block, axis, route)


def segment_of(lengths_row, positions):
    ends = jnp.cumsum(lengths_row, dtype=jnp.int32)
    return jnp.sum((positions[:, None] >= ends[None, :]).astype(jnp.int32), axis=1, dtype=jnp.int32)


def normalize(value, gain, shift):
    centred = value - jnp.mean(value, axis=-1, keepdims=True)
    spread = jnp.mean(centred * centred, axis=-1, keepdims=True)
    return centred * lax.rsqrt(spread + 1e-05) * gain + shift


def gelu_exact(value):
    return jax.nn.gelu(value, approximate=False)


def project(left, right):
    return jnp.dot(left, right, preferred_element_type=jnp.float32)


def project_back(left, weight):
    return jnp.einsum("tf,df->td", left, weight, preferred_element_type=jnp.float32)


def contract_rows(left, right):
    return jnp.einsum("tf,td->fd", left, right, preferred_element_type=jnp.float32)


def split_heads(value):
    return value.reshape(value.shape[0], HEADS, HEAD)


def in_blocks(step_fn, running, arrays, offset_row):
    total_rows = arrays[0].shape[0]
    block_rows = 1024 if total_rows > 1024 and total_rows % 1024 == 0 else total_rows
    if block_rows == total_rows:
        return step_fn(running, arrays, offset_row)
    stacked = tuple(
        (
            member.reshape((total_rows // block_rows, block_rows) + member.shape[1:])
            for member in arrays
        )
    )
    offsets = offset_row + block_rows * jnp.arange(total_rows // block_rows, dtype=jnp.int32)

    def scan_step(inner, packet):
        return (step_fn(inner, packet[0], packet[1]), None)

    result, unused = lax.scan(scan_step, running, (stacked, offsets))
    return result


def masked_scores(query_part, key_part, query_segment, key_segment):
    raw_scores = jnp.einsum(
        "qhe,khe->hqk",
        split_heads(query_part),
        split_heads(key_part),
        preferred_element_type=jnp.float32,
    ) * HEAD ** (-0.5)
    return jnp.where((query_segment[:, None] == key_segment[None, :])[None], raw_scores, NEGATIVE)


def prefix_scores(queries, prefix_key_rows):
    return jnp.einsum(
        "qhe,khe->hqk",
        split_heads(queries),
        split_heads(prefix_key_rows),
        preferred_element_type=jnp.float32,
    ) * HEAD ** (-0.5)


def gather_weights(shards):
    return (
        lax.all_gather(shards[0], "tok", axis=1, tiled=True),
        lax.all_gather(shards[1], "tok", axis=1, tiled=True),
        lax.all_gather(shards[2], "tok", axis=1, tiled=True),
        lax.all_gather(shards[3], "tok", axis=1, tiled=True),
        lax.all_gather(shards[4], "tok", axis=1, tiled=True),
        lax.all_gather(shards[5], "tok", axis=1, tiled=True),
        lax.all_gather(shards[6], "tok", axis=1, tiled=True),
        lax.all_gather(shards[7], "tok", axis=1, tiled=True),
        lax.all_gather(shards[8], "tok", axis=1, tiled=True),
        lax.all_gather(shards[9], "tok", axis=1, tiled=True),
        lax.all_gather(shards[10], "tok", axis=1, tiled=True),
        lax.all_gather(shards[11], "tok", axis=1, tiled=True),
        lax.all_gather(shards[12], "tok", axis=1, tiled=True),
        lax.all_gather(shards[13], "tok", axis=1, tiled=True),
        lax.all_gather(shards[14], "tok", axis=1, tiled=True),
    )


def front_part(inbound, weights):
    queries = (project(inbound, weights[0]) + weights[1].astype(jnp.float32)).astype(jnp.bfloat16)
    key_rows = project(inbound, weights[2]).astype(jnp.bfloat16)
    value_rows = (project(inbound, weights[3]) + weights[4].astype(jnp.float32)).astype(
        jnp.bfloat16
    )
    return (queries, key_rows, value_rows)


def attention_forward(
    queries, key_rows, value_rows, prefix_key_rows, prefix_value_rows, lengths_row, own_segment
):
    first_scores = prefix_scores(queries, prefix_key_rows)
    highest = jnp.max(first_scores, axis=2)
    denominator = jnp.sum(jnp.exp(first_scores - highest[..., None]), axis=2)

    def total_block(state, piece, offset_row):
        old_high, old_denominator = state
        key_part = piece[0]
        key_segment = segment_of(
            lengths_row, offset_row + jnp.arange(key_part.shape[0], dtype=jnp.int32)
        )
        raw_scores = masked_scores(queries, key_part, own_segment, key_segment)
        new_high = jnp.maximum(old_high, jnp.max(raw_scores, axis=2))
        new_denominator = old_denominator * jnp.exp(old_high - new_high) + jnp.sum(
            jnp.exp(raw_scores - new_high[..., None]), axis=2
        )
        return (new_high, new_denominator)

    highest, denominator = in_blocks(
        total_block,
        (highest, denominator),
        (lax.all_gather(key_rows, "tok", axis=0, tiled=True),),
        jnp.int32(0),
    )
    logsum = highest + jnp.log(denominator)
    summed = jnp.einsum(
        "hqk,khe->qhe",
        jnp.exp(first_scores - logsum[..., None]).astype(jnp.bfloat16),
        split_heads(prefix_value_rows),
        preferred_element_type=jnp.float32,
    )

    def absorb_block(running, piece, offset_row):
        key_part, value_part = piece
        key_segment = segment_of(
            lengths_row, offset_row + jnp.arange(key_part.shape[0], dtype=jnp.int32)
        )
        probs_part = jnp.exp(
            masked_scores(queries, key_part, own_segment, key_segment) - logsum[..., None]
        )
        return running + jnp.einsum(
            "hqk,khe->qhe",
            probs_part.astype(jnp.bfloat16),
            split_heads(value_part),
            preferred_element_type=jnp.float32,
        )

    summed = in_blocks(
        absorb_block,
        summed,
        (
            lax.all_gather(key_rows, "tok", axis=0, tiled=True),
            lax.all_gather(value_rows, "tok", axis=0, tiled=True),
        ),
        jnp.int32(0),
    )
    context = summed.reshape(queries.shape[0], -1)
    return (context, logsum)


def back_part(inbound, context, weights):
    context_low = context.astype(jnp.bfloat16)
    attended = project(context_low, weights[5]) + weights[6].astype(jnp.float32)
    normal_one, pull_one = jax.vjp(
        normalize,
        inbound.astype(jnp.float32) + attended,
        weights[7].astype(jnp.float32),
        weights[8].astype(jnp.float32),
    )
    normal_one_low = normal_one.astype(jnp.bfloat16)
    activation, pull_gelu = jax.vjp(
        gelu_exact, project(normal_one_low, weights[9]) + weights[10].astype(jnp.float32)
    )
    activation_low = activation.astype(jnp.bfloat16)
    mixed = project(activation_low, weights[11]) + weights[12].astype(jnp.float32)
    result, pull_two = jax.vjp(
        normalize,
        normal_one + mixed,
        weights[13].astype(jnp.float32),
        weights[14].astype(jnp.float32),
    )
    return (result, context_low, normal_one_low, pull_one, activation_low, pull_gelu, pull_two)


def query_backward(
    queries,
    d_context,
    logsum,
    delta,
    prefix_key_rows,
    prefix_value_rows,
    key_rows,
    value_rows,
    lengths_row,
    own_segment,
):
    context_heads = split_heads(d_context)
    query_heads = split_heads(queries)
    prefix_prob = jnp.exp(prefix_scores(queries, prefix_key_rows) - logsum[..., None])
    prefix_dprob = jnp.einsum(
        "qhe,khe->hqk",
        context_heads,
        split_heads(prefix_value_rows),
        preferred_element_type=jnp.float32,
    )
    prefix_dscore = (prefix_prob * (prefix_dprob - delta[..., None])).astype(jnp.bfloat16)
    grad_prefix_keys = jnp.einsum(
        "hqk,qhe->khe", prefix_dscore, query_heads, preferred_element_type=jnp.float32
    ) * HEAD ** (-0.5)
    grad_prefix_values = jnp.einsum(
        "hqk,qhe->khe",
        prefix_prob.astype(jnp.bfloat16),
        context_heads,
        preferred_element_type=jnp.float32,
    )
    grad_start = jnp.einsum(
        "hqk,khe->qhe",
        prefix_dscore,
        split_heads(prefix_key_rows),
        preferred_element_type=jnp.float32,
    )

    def pull_block(running, piece, offset_row):
        key_part, value_part = piece
        key_segment = segment_of(
            lengths_row, offset_row + jnp.arange(key_part.shape[0], dtype=jnp.int32)
        )
        probs_part = jnp.exp(
            masked_scores(queries, key_part, own_segment, key_segment) - logsum[..., None]
        )
        dprob = jnp.einsum(
            "qhe,khe->hqk",
            context_heads,
            split_heads(value_part),
            preferred_element_type=jnp.float32,
        )
        dscore = (probs_part * (dprob - delta[..., None])).astype(jnp.bfloat16)
        return running + jnp.einsum(
            "hqk,khe->qhe", dscore, split_heads(key_part), preferred_element_type=jnp.float32
        )

    grad_queries = in_blocks(
        pull_block,
        grad_start,
        (
            lax.all_gather(key_rows, "tok", axis=0, tiled=True),
            lax.all_gather(value_rows, "tok", axis=0, tiled=True),
        ),
        jnp.int32(0),
    )
    row_count = queries.shape[0]
    return (
        (grad_queries * HEAD ** (-0.5)).reshape(row_count, -1),
        grad_prefix_keys.reshape(prefix_key_rows.shape),
        grad_prefix_values.reshape(prefix_value_rows.shape),
    )


def key_backward(queries, d_context, logsum, delta, key_rows, value_rows, lengths_row, own_segment):
    all_logsum, all_delta = (
        lax.all_gather(logsum, "tok", axis=1, tiled=True),
        lax.all_gather(delta, "tok", axis=1, tiled=True),
    )
    value_heads = split_heads(value_rows)

    def spread_block(running, piece, offset_row):
        grad_keys, grad_values = running
        query_part, context_part = piece
        part_rows = query_part.shape[0]
        part_logsum = lax.dynamic_slice_in_dim(all_logsum, offset_row, part_rows, 1)
        part_delta = lax.dynamic_slice_in_dim(all_delta, offset_row, part_rows, 1)
        part_segment = segment_of(lengths_row, offset_row + jnp.arange(part_rows, dtype=jnp.int32))
        probs_part = jnp.exp(
            masked_scores(query_part, key_rows, part_segment, own_segment) - part_logsum[..., None]
        )
        context_heads = split_heads(context_part)
        dprob = jnp.einsum(
            "qhe,khe->hqk", context_heads, value_heads, preferred_element_type=jnp.float32
        )
        dscore = (probs_part * (dprob - part_delta[..., None])).astype(jnp.bfloat16)
        new_keys = grad_keys + jnp.einsum(
            "hqk,qhe->khe", dscore, split_heads(query_part), preferred_element_type=jnp.float32
        )
        new_values = grad_values + jnp.einsum(
            "hqk,qhe->khe",
            probs_part.astype(jnp.bfloat16),
            context_heads,
            preferred_element_type=jnp.float32,
        )
        return (new_keys, new_values)

    def spread(running, piece, offset_row):
        return in_blocks(spread_block, running, piece, offset_row)

    empty = jnp.zeros((key_rows.shape[0], HEADS, HEAD), jnp.float32)
    grad_keys, grad_values = spread(
        (empty, empty),
        (
            lax.all_gather(queries, "tok", axis=0, tiled=True),
            lax.all_gather(d_context, "tok", axis=0, tiled=True),
        ),
        jnp.int32(0),
    )
    row_count = key_rows.shape[0]
    return ((grad_keys * HEAD ** (-0.5)).reshape(row_count, -1), grad_values.reshape(row_count, -1))


def layer_backward(
    inbound, upstream, weights, prefix_key_rows, prefix_value_rows, lengths_row, own_segment
):
    queries, key_rows, value_rows = front_part(inbound, weights)
    context, logsum = attention_forward(
        queries, key_rows, value_rows, prefix_key_rows, prefix_value_rows, lengths_row, own_segment
    )
    result, context_low, normal_one_low, pull_one, activation_low, pull_gelu, pull_two = back_part(
        inbound, context, weights
    )
    d_sum, d_gain_two, d_shift_two = pull_two(upstream.astype(jnp.float32))
    d_mixed = d_sum.astype(jnp.bfloat16)
    grad_down = contract_rows(activation_low, d_mixed)
    grad_down_bias = jnp.sum(d_mixed.astype(jnp.float32), axis=0)
    (d_pre,) = pull_gelu(project_back(d_mixed, weights[11]))
    d_pre_low = d_pre.astype(jnp.bfloat16)
    grad_up = contract_rows(normal_one_low, d_pre_low)
    grad_up_bias = jnp.sum(d_pre_low.astype(jnp.float32), axis=0)
    d_resid, d_gain_one, d_shift_one = pull_one(d_sum + project_back(d_pre_low, weights[9]))
    d_attended = d_resid.astype(jnp.bfloat16)
    grad_out = contract_rows(context_low, d_attended)
    grad_out_bias = jnp.sum(d_attended.astype(jnp.float32), axis=0)
    d_context = project_back(d_attended, weights[5]).astype(jnp.bfloat16)
    delta = jnp.sum(split_heads(d_context).astype(jnp.float32) * split_heads(context), axis=2).T
    grad_queries, grad_prefix_keys, grad_prefix_values = query_backward(
        queries,
        d_context,
        logsum,
        delta,
        prefix_key_rows,
        prefix_value_rows,
        key_rows,
        value_rows,
        lengths_row,
        own_segment,
    )
    grad_keys, grad_values = key_backward(
        queries, d_context, logsum, delta, key_rows, value_rows, lengths_row, own_segment
    )
    queries_low = grad_queries.astype(jnp.bfloat16)
    keys_low = grad_keys.astype(jnp.bfloat16)
    values_low = grad_values.astype(jnp.bfloat16)
    grad_query_weight = contract_rows(inbound, queries_low)
    grad_query_bias = jnp.sum(queries_low.astype(jnp.float32), axis=0)
    grad_key_weight = contract_rows(inbound, keys_low)
    grad_value_weight = contract_rows(inbound, values_low)
    grad_value_bias = jnp.sum(values_low.astype(jnp.float32), axis=0)
    d_input = (
        d_resid
        + project_back(queries_low, weights[0])
        + project_back(keys_low, weights[2])
        + project_back(values_low, weights[3])
    )
    grads = (
        grad_query_weight,
        grad_query_bias,
        grad_key_weight,
        grad_value_weight,
        grad_value_bias,
        grad_out,
        grad_out_bias,
        d_gain_one,
        d_shift_one,
        grad_up,
        grad_up_bias,
        grad_down,
        grad_down_bias,
        d_gain_two,
        d_shift_two,
    )
    return (d_input, grads, (grad_prefix_keys, grad_prefix_values))


def sum_each(grads):
    return (
        lax.psum_scatter(grads[0][None], "tok", scatter_dimension=1, tiled=True),
        lax.psum_scatter(grads[1][None], "tok", scatter_dimension=1, tiled=True),
        lax.psum_scatter(grads[2][None], "tok", scatter_dimension=1, tiled=True),
        lax.psum_scatter(grads[3][None], "tok", scatter_dimension=1, tiled=True),
        lax.psum_scatter(grads[4][None], "tok", scatter_dimension=1, tiled=True),
        lax.psum_scatter(grads[5][None], "tok", scatter_dimension=1, tiled=True),
        lax.psum_scatter(grads[6][None], "tok", scatter_dimension=1, tiled=True),
        lax.psum_scatter(grads[7][None], "tok", scatter_dimension=1, tiled=True),
        lax.psum_scatter(grads[8][None], "tok", scatter_dimension=1, tiled=True),
        lax.psum_scatter(grads[9][None], "tok", scatter_dimension=1, tiled=True),
        lax.psum_scatter(grads[10][None], "tok", scatter_dimension=1, tiled=True),
        lax.psum_scatter(grads[11][None], "tok", scatter_dimension=1, tiled=True),
        lax.psum_scatter(grads[12][None], "tok", scatter_dimension=1, tiled=True),
        lax.psum_scatter(grads[13][None], "tok", scatter_dimension=1, tiled=True),
        lax.psum_scatter(grads[14][None], "tok", scatter_dimension=1, tiled=True),
    )


def by_section(listing, is_first, early_first):
    stacked = jnp.stack(listing)
    window_count = len(listing) - 1
    if early_first:
        return jnp.where(is_first, stacked[:window_count], stacked[1:])
    return jnp.where(is_first, stacked[1:], stacked[:window_count])


def local(
    inputs,
    cotangent,
    lengths,
    prefix_keys,
    prefix_values,
    w_query,
    b_query,
    w_key,
    w_value,
    b_value,
    w_out,
    b_out,
    norm1_gain,
    norm1_shift,
    w_up,
    b_up,
    w_down,
    b_down,
    norm2_gain,
    norm2_shift,
):
    micro_count = inputs.shape[0]
    tok_rows = inputs.shape[1]
    model_width = inputs.shape[2]
    section_index = lax.axis_index("section")
    is_first = section_index == 0
    own_positions = lax.axis_index("tok") * tok_rows + jnp.arange(tok_rows, dtype=jnp.int32)
    shard_list = (
        w_query,
        b_query,
        w_key,
        w_value,
        b_value,
        w_out,
        b_out,
        norm1_gain,
        norm1_shift,
        w_up,
        b_up,
        w_down,
        b_down,
        norm2_gain,
        norm2_shift,
    )
    prefix_key_rows = prefix_keys[0]
    prefix_value_rows = prefix_values[0]
    weights = tuple((member[0] for member in gather_weights(shard_list)))
    received = jnp.zeros((tok_rows, model_width), jnp.bfloat16)
    seen_inputs = []
    seen_outputs = []
    seen_context = []
    seen_logsum = []
    for moment in range(micro_count + 1):
        current = jnp.clip(moment - section_index, 0, micro_count - 1)
        lengths_row = lengths[current]
        own_segment = segment_of(lengths_row, own_positions)
        inbound = jnp.where(is_first, inputs[min(moment, micro_count - 1)], received)
        queries, key_rows, value_rows = front_part(inbound, weights)
        context, logsum = attention_forward(
            queries,
            key_rows,
            value_rows,
            prefix_key_rows,
            prefix_value_rows,
            lengths_row,
            own_segment,
        )
        result = back_part(inbound, context, weights)[0].astype(jnp.bfloat16)
        seen_inputs.append(inbound)
        seen_outputs.append(result)
        seen_context.append(context)
        seen_logsum.append(logsum)
        if moment < micro_count:
            received = from_behind(result, "section", 1)
    kept_inputs = by_section(seen_inputs, is_first, True)
    weights = tuple((member[0] for member in gather_weights(shard_list)))
    back_received = jnp.zeros((tok_rows, model_width), jnp.bfloat16)
    grad_shards = tuple((jnp.zeros(member.shape, jnp.float32) for member in shard_list))
    prefix_key_total = jnp.zeros(prefix_key_rows.shape, jnp.float32)
    prefix_value_total = jnp.zeros(prefix_value_rows.shape, jnp.float32)
    seen_grads = []
    for moment in range(micro_count + 1):
        current = moment - 1 + section_index
        is_valid = ((current >= 0) & (current < micro_count)).astype(jnp.float32)
        picked = jnp.clip(current, 0, micro_count - 1)
        lengths_row = lengths[picked]
        own_segment = segment_of(lengths_row, own_positions)
        upstream = jnp.where(is_first, back_received, cotangent[min(moment, micro_count - 1)])
        d_input, grads, prefix_grads = layer_backward(
            kept_inputs[picked],
            upstream,
            weights,
            prefix_key_rows,
            prefix_value_rows,
            lengths_row,
            own_segment,
        )
        d_input_low = d_input.astype(jnp.bfloat16)
        seen_grads.append(d_input_low)
        if moment < micro_count:
            back_received = from_behind(d_input_low, "section", -1)
        grads = tuple((member * is_valid for member in grads))
        prefix_key_total = prefix_key_total + prefix_grads[0] * is_valid
        prefix_value_total = prefix_value_total + prefix_grads[1] * is_valid
        scattered = sum_each(grads)
        grad_shards = tuple((older + newer for older, newer in zip(grad_shards, scattered)))
    layer_outputs = by_section(seen_outputs, is_first, True)[None]
    input_grads = by_section(seen_grads, is_first, False)[None]
    prefix_sums = lax.psum((prefix_key_total, prefix_value_total), "tok")
    return (
        layer_outputs,
        input_grads,
        grad_shards[0],
        grad_shards[1],
        grad_shards[2],
        grad_shards[3],
        grad_shards[4],
        grad_shards[5],
        grad_shards[6],
        grad_shards[7],
        grad_shards[8],
        grad_shards[9],
        grad_shards[10],
        grad_shards[11],
        grad_shards[12],
        grad_shards[13],
        grad_shards[14],
        prefix_sums[0][None],
        prefix_sums[1][None],
    )


MESH = pl.DeviceIdType.MESH
F32 = jnp.float32
BF16 = jnp.bfloat16
ROWS = 64
PIECE = 16
PIECES = ROWS // PIECE
BLOCK = 256
SQRT_HALF = 0.7071067811865476
INV_SQRT_2PI = 0.3989422804014327
AG_X, AG_N, AG_Z, AG_O = range(4)
RS_O, RS_Z, RS_N, RS_X = range(4)


def flip(bit, other):
    return bit + other - 2 * bit * other


def mm(left, right):
    return jnp.dot(left, right, preferred_element_type=F32)


def mm_nt(left, right):
    return lax.dot_general(left, right, (((1,), (1,)), ((), ())), preferred_element_type=F32)


def mm_tn(left, right):
    return lax.dot_general(left, right, (((0,), (0,)), ((), ())), preferred_element_type=F32)


def rows_at(index, size):
    return pl.ds(pl.multiple_of(index * size, size), size)


def remote(src, dst, send, recv, device):
    return pltpu.make_async_remote_copy(
        src_ref=src, dst_ref=dst, send_sem=send, recv_sem=recv, device_id=device, device_id_type=MESH
    )


def local_copy(src, dst, sem):
    return pltpu.make_async_copy(src, dst, sem)


def bytes_of(ref, sem):
    return pltpu.make_async_copy(ref, ref, sem)


class Place:
    def __init__(self):
        self.x = lax.axis_index("section")
        self.t = lax.axis_index("tok")
        z = self.t // 4
        self.y = (self.t // 2) % 2
        self.core = self.t % 2
        self.cube = z // 2
        self.zl = z % 2
        self.chip = self.x * 4 + self.zl * 2 + self.y
        self.tau = self.chip * 2 + self.core

    def device(self, x, cube):
        return (x, cube * 8 + self.zl * 4 + self.y * 2 + self.core)

    def twin(self):
        return self.device(self.x, 1 - self.cube)

    def sibling(self):
        return (self.x, self.t + 1 - 2 * self.core)

    def peer(self, r):
        zl, y = flip(self.zl, (r // 2) % 2), flip(self.y, r % 2)
        return (flip(self.x, r // 4), self.cube * 8 + zl * 4 + y * 2 + self.core)

    def peer_chip(self, r):
        return flip(self.x, r // 4) * 4 + flip(self.zl, (r // 2) % 2) * 2 + flip(self.y, r % 2)

    def pair_rows(self, j):
        return rows_at(flip(self.x, j // 2) * 2 + flip(self.zl, j % 2), BLOCK)


def hops_of(first, last):
    hops = {(r, q): hop for q in range(PIECES) for r, hop in first}
    for q, (via, step, seen) in enumerate(last):
        hops[(via, q)] = (step, seen)
    return hops


class Pump:
    def __init__(self, rate=3):
        self.waiting = []
        self.rate = rate

    def add(self, starts):
        self.waiting += starts

    def go(self, count=None):
        count = self.rate if count is None else count
        for start in self.waiting[:count]:
            start()
        del self.waiting[:count]


class Gather:
    CUBE = (
        (4, 2, 1), ((1, 2, 4), (3, 6, 5), (7,)), (0, 2, 1, 3),
        hops_of(((1, (2, 3)), (2, (4, 6)), (4, (1, 5))), ((3, 4, 7), (6, 1, 7), (5, 2, 7), (3, 4, 7))),
    )
    FACE = ((2, 1), ((1, 2), (3,)), (0, 1), hops_of((), ((1, 2, 3), (2, 1, 3), (1, 2, 3), (2, 1, 3))))

    def __init__(self, place, buf, recv, sib, sends, face=False):
        self.place, self.buf, self.recv, self.sib, self.sends = place, buf, recv, sib, sends
        self.near, self.stages, self.order, self.hops = self.FACE if face else self.CUBE
        self.pump = Pump()

    def piece(self, r, q, other=0):
        core = flip(self.place.core, other)
        row = (self.place.peer_chip(r) * 2 + core) * ROWS + q * PIECE
        return self.buf.at[pl.ds(pl.multiple_of(row, PIECE), PIECE)]

    def start(self):
        for q in range(PIECES):
            own = self.piece(0, q)
            for r in self.near:
                remote(own, own, self.sends.at[0, r, q], self.recv.at[r, q], self.place.peer(r)).start()
            self.to_sibling(0, q).start()

    def to_sibling(self, r, q):
        rows = self.piece(r, q)
        return remote(rows, rows, self.sends.at[1, r, q], self.sib.at[r, q], self.place.sibling())

    def arrive(self, r, q):
        rows = self.piece(r, q)
        bytes_of(rows, self.recv.at[r, q]).wait()
        if (r, q) in self.hops:
            hop, seen = self.hops[(r, q)]
            remote(rows, rows, self.sends.at[2, r, q], self.recv.at[seen, q], self.place.peer(hop)).start()
        self.to_sibling(r, q).start()

    def stage(self, number):
        for q in range(PIECES):
            for r in self.stages[number]:
                self.arrive(r, q)
            self.pump.go()

    def pair_ready(self, j):
        for r in (2 * j, 2 * j + 1):
            for q in range(PIECES):
                bytes_of(self.piece(r, q, 1), self.sib.at[r, q]).wait()

    def blocks(self, use):
        before = None
        for i, j in enumerate(self.order):
            if i < len(self.stages):
                self.stage(i)
            self.pair_ready(j)
            use(j, before)
            before = j
        self.drain()

    def drain(self):
        own = self.piece(0, 0)
        for q in range(PIECES):
            for r in self.near:
                bytes_of(own, self.sends.at[0, r, q]).wait()
            for r in range(2 * len(self.order)):
                bytes_of(own, self.sends.at[1, r, q]).wait()
        for r, q in self.hops:
            bytes_of(own, self.sends.at[2, r, q]).wait()


class Scatter:
    WAY = {3: (2, (7, 0)), 6: (4, (7, 1)), 5: (1, None), 1: (1, 3), 2: (2, 6), 4: (4, 5)}

    def __init__(self, place, recv, sends, half, keep, sib_out, sib_in, out, inbox):
        self.place, self.recv, self.sends = place, recv, sends
        self.half, self.keep, self.sib_out, self.sib_in = half, keep, sib_out, sib_in
        self.out, self.inbox = out, inbox
        self.pump = Pump()

    def pair(self, r):
        return remote(
            self.sib_out.at[r], self.sib_in.at[r], self.sends.at[0, r], self.recv.at[0, r], self.place.sibling()
        )

    def push(self, r):
        step = self.WAY[r][0]
        return remote(
            self.out.at[r], self.inbox.at[r], self.sends.at[1, r], self.recv.at[1, r], self.place.peer(step)
        )

    def part(self, q):
        rows, slot = pl.ds(q * 32, 32), (7, 0)[q]
        return remote(
            self.out.at[7, rows], self.inbox.at[7, rows], self.sends.at[1, slot], self.recv.at[1, slot],
            self.place.peer((4, 1)[q]),
        )

    def give(self, j, partial):
        for k in range(4):
            self.half[k] = partial[k * ROWS : (k + 1) * ROWS]
        core = self.place.core
        for b in range(2):
            r = 2 * j + flip(self.place.y, b)
            self.keep[r] = self.half[2 * b + core]
            self.sib_out[r] = self.half[2 * b + 1 - core].astype(BF16)
            self.pair(r).start()

    def forward(self, r):
        self.pair(r).wait_recv()
        if r == 7:
            self.out[7] = (self.keep[7] + self.sib_in[7].astype(F32)).astype(BF16)
            self.part(0).start()
            self.part(1).start()
            return
        more = self.WAY[r][1]
        if more is None:
            self.out[r] = (self.keep[r] + self.sib_in[r].astype(F32)).astype(BF16)
        elif isinstance(more, int):
            self.push(more).wait_recv()
            self.out[r] = (self.keep[r] + self.sib_in[r].astype(F32) + self.inbox[more].astype(F32)).astype(BF16)
        else:
            q = more[1]
            self.part(q).wait_recv()
            for k in range(2):
                rows = pl.ds(k * 32, 32)
                total = self.keep[r, rows] + self.sib_in[r, rows].astype(F32)
                if k == q:
                    total = total + self.inbox[7, rows].astype(F32)
                self.out[r, rows] = total.astype(BF16)
        self.push(r).start()

    def run(self, produce):
        def step(i, carry):
            @pl.when(i < 4)
            def _():
                self.give(3 - i, produce(3 - i))

            for when, steps in ((1, (7,)), (2, (5,)), (3, (3, 6)), (4, (1, 2, 4))):
                @pl.when(i == when)
                def _():
                    for r in steps:
                        self.forward(r)
                    self.pump.go()

            return carry

        lax.fori_loop(0, 5, step, 0)

    def rest(self):
        for r in (7, 3, 6, 1, 2, 4):
            self.forward(r)

    def finish(self):
        self.pair(0).wait_recv()
        self.keep[0] = self.keep[0] + self.sib_in[0].astype(F32)
        for r in (1, 2, 4):
            self.push(r).wait_recv()
            self.keep[0] = self.keep[0] + self.inbox[r].astype(F32)
        for r in range(8):
            self.pair(r).wait_send()
        for r in self.WAY:
            self.push(r).wait_send()
        for q in range(2):
            self.part(q).wait_send()
        return self.keep[0]


def norm_forward(value, gain, shift, hat_ref, rstd_ref):
    centred = value - jnp.mean(value, axis=-1, keepdims=True)
    rstd = lax.rsqrt(jnp.mean(centred * centred, axis=-1, keepdims=True) + 1e-05)
    hat = centred * rstd
    hat_ref[...] = hat
    rstd_ref[...] = jnp.broadcast_to(rstd, rstd_ref.shape)
    return hat * gain + shift


def norm_backward(upstream, gain, hat_ref, rstd_ref):
    hat = hat_ref[...]
    scaled = upstream * gain
    mean_one = jnp.mean(scaled, axis=-1, keepdims=True)
    mean_two = jnp.mean(scaled * hat, axis=-1, keepdims=True)
    result = rstd_ref[:, :1] * (scaled - mean_one - hat * mean_two)
    d_gain = jnp.sum(upstream * hat, axis=0, keepdims=True)
    d_shift = jnp.sum(upstream, axis=0, keepdims=True)
    return result, d_gain, d_shift


def column_sum(low):
    return jnp.sum(low.astype(F32), axis=0, keepdims=True)


def kernel(
    lengths, inputs, cotangent, wq_src, wk_src, wv_src, wup_src, wdn_src, wout_src, pk_src, pv_src,
    v0, v1, v2, v3, v4, v5, v6, v7, v8,
    out_y, out_dx, got_qkv, got_up, got_dn, got_out, got_prefix, got_rows, got_bias,
    ag_recv, ag_sib, ag_send, rs_recv, rs_send,
    wsend, wown, wtwin, wrelay, psem, xsem, osend, orecv, tsend, trecv, gsend, grecv, rsem,
    raw_qkv, raw_up, pack_qkv, pack_up, vrows, u0, u1, u2, u3, u4, u5, u6, u7, u8,
    wqkv, wup, wdn, wout, pre,
    qseg, kseg, xg, ng, dzg, dog, param,
    qs, ks, vs, kt, vt, lse, ctb, ctf,
    hat1, rstd1, hat2, rstd2, act, dact,
    half, keep, sib_out, sib_in, rs_out, inbox,
    own_a, own_b, ystage, dstage,
    dfs, dcb, delta, dqt, dkacc, dvacc, dqkv, dqkvt,
    rowacc, biasacc, g_qkv, g_up, g_dn, g_out, g_prefix,
    t_qkv, t_up, t_dn, t_out, t_prefix,
):
    place = Place()
    x, t, cube, core, tau = place.x, place.t, place.cube, place.core, place.tau
    tokens = qs.shape[1]
    width = xg.shape[2]
    half_rows = 8 * ROWS
    barrier = pltpu.get_barrier_semaphore()

    def greet(i, carry):
        gx, gt = i // 16, i % 16

        @pl.when((gx != x) | (gt != t))
        def _():
            pl.semaphore_signal(barrier, inc=1, device_id=(gx, gt), device_id_type=MESH)

        return carry

    lax.fori_loop(0, 32, greet, 0)

    raw = [local_copy(src.at[0], raw_qkv.at[i], rsem.at[i]) for i, src in enumerate((wq_src, wk_src, wv_src))]
    raw.append(local_copy(wup_src.at[0], raw_up, rsem.at[3]))
    vectors = (u0, u1, u2, u3, u4, u5, u6, u7, u8)
    for i, (src, dst) in enumerate(zip((v0, v1, v2, v3, v4, v5, v6, v7, v8), vectors)):
        raw.append(local_copy(src, dst, rsem.at[4 + i]))
    for copy in raw:
        copy.start()
    vrows[...] = jnp.zeros_like(vrows)
    for copy in raw:
        copy.wait()
    for i in range(8):
        vrows[i : i + 1, 0:64] = vectors[i][...].astype(F32)
    up_row = u8[...].astype(F32)
    for i in range(4):
        vrows[8 + i : 9 + i, 0:64] = up_row[:, i * 64 : (i + 1) * 64]
    vector_columns = vrows[...].T[0:64]

    def pack_heads(h, carry):
        cols = rows_at(h, 128)
        parts = [raw_qkv[i, :, cols].astype(F32) for i in range(3)]
        for s in range(2):
            sides = [part[:, s * 64 : (s + 1) * 64] for part in parts]
            pack_qkv[2 * h + s] = jnp.concatenate(sides + [vector_columns], axis=1).astype(BF16)
        return carry

    lax.fori_loop(0, 8, pack_heads, 0)
    for side in range(2):
        for rest in range(8):
            for zhi in range(2):
                start = (zhi * 8 + rest) * 256 + side * 128
                pack_up[side * 8 + rest, :, zhi * 128 : (zhi + 1) * 128] = raw_up[:, start : start + 128]

    pl.semaphore_wait(barrier, 31)

    own_rows = rows_at(tau, ROWS)
    first, last = pl.ds(0, 32), pl.ds(32, 32)
    diagonal = place.device(1 - x, 1 - cube)
    neighbour = place.device(1 - x, cube)

    def shares(source, target, far, sem):
        here = local_copy(source.at[cube], target, xsem.at[sem])
        to_twin = remote(source.at[1 - cube, first], target.at[first], xsem.at[sem + 1], xsem.at[sem + 2], place.twin())
        to_diagonal = remote(source.at[1 - cube, last], far.at[last], xsem.at[sem + 1], xsem.at[sem + 3], diagonal)

        def start():
            @pl.when(x == cube)
            def _():
                to_twin.start()
                here.start()

            pl.when(x != cube)(to_diagonal.start)

        def arrived():
            @pl.when(x != cube)
            def _():
                to_twin.wait_recv()
                to_diagonal.wait_recv()

            pl.when(x == cube)(here.wait)

        def sent():
            pl.when(x == cube)(to_twin.wait_send)
            pl.when(x != cube)(to_diagonal.wait_send)

        return start, arrived, sent

    x_start, x_arrived, x_sent = shares(inputs, xg.at[0, own_rows], xg.at[0, rows_at(tau + 8 - 16 * x, ROWS)], 0)
    d_start, d_arrived, d_sent = shares(cotangent, dstage.at[2], dstage.at[2], 4)
    x_start()

    def spread_pushes(kind):
        src_all, dst_all = (pack_qkv, pack_up)[kind], (wqkv, wup)[kind]
        dst, sem = dst_all.at[rows_at(x * 16 + t, ROWS)], wown.at[kind, x, t % 8]
        for k in range(16):
            to = lax.rem(k + tau + 1, 16)

            def go(to=to):
                src = src_all.at[to]
                pl.when(to == tau)(local_copy(src, dst, sem).start)
                pl.when(to != tau)(remote(src, dst, wsend.at[kind], sem, (to // 8, cube * 8 + to % 8)).start)

            yield go

    def slice_pushes():
        neighbour = place.device(1 - x, cube)

        def give_out():
            src, dst = wout_src.at[0], wout.at[x]
            pl.when(x == cube)(local_copy(src, dst, wown.at[2, x, 0]).start)
            pl.when(x != cube)(remote(src, dst, wsend.at[2], wown.at[2, x, 0], neighbour).start)

        def give_down():
            for side in range(2):
                src = wdn_src.at[0, pl.ds(side * 128, 128)]
                dst = wdn.at[x, rows_at(cube, 128)]
                pl.when(x == side)(local_copy(src, dst, wown.at[3, x, 0]).start)
                pl.when(x != side)(remote(src, dst, wsend.at[3], wown.at[3, x, 0], neighbour).start)

        return give_out, give_down

    def prefix_out():
        for side, index in ((x, 0), (1 - x, 1)):
            for kind, src_all in ((0, pk_src), (1, pv_src)):
                src = src_all.at[0, :, rows_at(side * 4 + place.zl * 2 + place.y, 128)]
                dst = pre.at[x, kind]
                if index == 0:
                    yield local_copy(src, dst, psem.at[0, kind])
                else:
                    yield remote(src, dst, psem.at[1, kind], psem.at[2, kind], place.device(1 - x, cube))

    def slice_ref(kind, l, zhi):
        if kind < 2:
            return (wqkv, wup)[kind].at[rows_at(l * 2 + zhi, half_rows)]
        if kind == 3:
            return wdn.at[l, rows_at(zhi, 128)]
        return wout.at[l]

    def to_twin(ref, kind, l):
        return remote(ref, ref, wrelay.at[kind, l], wtwin.at[kind, l], place.twin())

    def relay_blocks(kind, l):
        def one(i, carry):
            k = lax.rem(jnp.where(x == l, tau, 0) + 7 - i, 8)
            ref = (wqkv, wup)[kind].at[rows_at((l * 2 + cube) * 8 + k, ROWS)]
            bytes_of(ref, wown.at[kind, l, k]).wait()
            to_twin(ref, kind, l).start()
            return carry

        lax.fori_loop(0, 8, one, 0)

    def relay_out(l):
        @pl.when(x == cube)
        def _():
            bytes_of(wout.at[l], wown.at[2, l, 0]).wait()
            to_twin(wout.at[l], 2, l).start()

    def relay_down(l):
        dn = slice_ref(3, l, cube)
        bytes_of(dn, wown.at[3, l, 0]).wait()
        to_twin(dn, 3, l).start()

    def weights_in(kind, l):
        wait = bytes_of(slice_ref(kind, l, 1 - cube), wtwin.at[kind, l]).wait
        if kind == 2:
            pl.when(x != cube)(wait)
        else:
            wait()

    def weights_drain():
        for kind, ref in ((0, pack_qkv), (1, pack_up)):
            bytes_of(ref.at[pl.ds(0, 15)], wsend.at[kind]).wait()
        bytes_of(wdn.at[0, pl.ds(0, 128)], wsend.at[3]).wait()
        pl.when(x != cube)(bytes_of(wout.at[0], wsend.at[2]).wait)
        for l in range(2):
            for kind in (0, 1, 3):
                to_twin(slice_ref(kind, l, cube), kind, l).wait_send()
            pl.when(x == cube)(to_twin(wout.at[l], 2, l).wait_send)

    def weight(ref, l):
        return ref[rows_at(l, 16 * ROWS)]

    def own_half(pair):
        return jnp.where(core == 0, pair[:, :64], pair[:, 64:])

    def gather(buf, phase):
        return Gather(place, buf, ag_recv.at[phase], ag_sib.at[phase], ag_send)

    def scatter(phase):
        boxes = phase % 2
        return Scatter(
            place, rs_recv.at[phase], rs_send, half, keep, sib_out, sib_in.at[boxes], rs_out, inbox.at[boxes],
        )

    prefixes = list(prefix_out())
    for copy in prefixes:
        copy.start()

    @pl.when(x == 0)
    def _():
        for start in spread_pushes(0):
            start()

    rowacc[...] = jnp.zeros_like(rowacc)
    biasacc[...] = jnp.zeros_like(biasacc)
    dqt[64:128] = jnp.zeros((64, tokens), F32)
    along = lax.broadcasted_iota(jnp.int32, (8, tokens), 1)
    down = lax.broadcasted_iota(jnp.int32, (tokens, 128), 0)
    segment_q, segment_k = jnp.zeros((8, tokens), jnp.int32), jnp.zeros((tokens, 128), jnp.int32)
    end = jnp.int32(0)
    for j in range(lengths.shape[1]):
        end = end + lengths[cube, j]
        segment_q = segment_q + (along >= end).astype(jnp.int32)
        segment_k = segment_k + (down >= end).astype(jnp.int32)
    qseg[...] = segment_q
    kseg[0:tokens] = segment_k
    kseg[tokens:] = jnp.full((kseg.shape[0] - tokens, 128), -1, jnp.int32)

    relay_blocks(0, 0)
    x_arrived()

    def result_out(stage, out, kind, layer):
        dst = out.at[cube]
        is_self = (layer == x) & (x == cube)
        here = local_copy(stage, dst, orecv.at[kind, cube])
        there = remote(stage, dst, osend.at[kind, layer], orecv.at[kind, cube], place.device(layer, x))
        return is_self, here, there

    def visible(cols):
        key_part = kseg[...]
        keys_two = jnp.concatenate([key_part, key_part], axis=1)
        return (keys_two == qseg[0:1, cols]) | (keys_two < 0)

    def forward_layer(l, carry):
        gather_x = gather(xg.at[l], AG_X)
        gather_x.start()

        @pl.when(l == 0)
        def _():
            def first_layer(start):
                return lambda: pl.when(x == 0)(start)

            give_out, give_down = slice_pushes()
            gather_x.pump.add([first_layer(start) for start in (give_out, *spread_pushes(1), give_down)])
            gather_x.stage(0)
            gather_x.pump.go(1)
            relay_out(0)
            gather_x.stage(1)
            relay_blocks(1, 0)
            gather_x.pump.go(len(gather_x.pump.waiting))
            gather_x.stage(2)
            relay_down(0)
            d_start()
            for copy in prefixes[:2]:
                copy.wait()
            for copy in prefixes[2:]:
                copy.wait()

        weights_in(0, l)
        tail = wqkv[rows_at(l, 16 * ROWS), 128:256].astype(F32).T
        param[l] = tail[64:80]
        biases = own_half(param[l, 0:8, rows_at(tau // 2, 128)])[6:8]
        empty = jnp.zeros((1, 64), F32)
        qkv_bias = jnp.concatenate([biases[0:1], empty, biases[1:2], empty], axis=1)
        prefix = jnp.concatenate(
            [own_half(pre[l, 0].astype(F32)), own_half(pre[l, 1].astype(F32))], axis=1
        )
        ks[l, tokens:] = prefix[:, :64].astype(BF16)
        vs[l, tokens:] = prefix[:, 64:].astype(BF16)
        prefix_t = prefix.T
        kt[l, :, tokens:] = prefix_t[:64].astype(BF16)
        vt[l, :, tokens:] = prefix_t[64:].astype(BF16)

        for i, j in enumerate(gather_x.order):
            if i < 3:
                @pl.when(l == 1)
                def _():
                    gather_x.stage(i)

            gather_x.pair_ready(j)
            rows = place.pair_rows(j)
            value = mm(xg[l, rows], weight(wqkv, l)) + qkv_bias
            qs[l, rows] = (value[:, :64] * 0.125).astype(BF16)
            ks[l, rows] = value[:, 64:128].astype(BF16)
            vs[l, rows] = value[:, 128:192].astype(BF16)
            value_t = value.T
            kt[l, :, rows] = value_t[64:128].astype(BF16)
            vt[l, :, rows] = value_t[128:192].astype(BF16)
        gather_x.drain()

        def second_layer(start):
            return lambda: pl.when((l == 0) & (x == 1))(start)

        give_out, give_down = slice_pushes()
        scatter_o = scatter(RS_O)
        scatter_o.pump = Pump(9)
        scatter_o.pump.add(
            [second_layer(start) for start in (*spread_pushes(0), give_out, give_down, *spread_pushes(1))]
        )

        def attend(j):
            cols = place.pair_rows(j)
            scores = jnp.where(visible(cols), mm_nt(ks[l], qs[l, cols]), NEGATIVE)
            top = jnp.max(scores, axis=0, keepdims=True)
            grown = jnp.exp(scores - top)
            total = jnp.sum(grown, axis=0, keepdims=True)
            probs = (grown * (1.0 / total)).astype(BF16)
            lse[l, 0:1, cols] = top + jnp.log(total)
            context_t = mm(vt[l], probs)
            ctf[l, :, cols] = context_t
            low = context_t.astype(BF16)
            ctb[l, :, cols] = low
            return mm_tn(low, wout[l])

        pl.when(l == 0)(lambda: weights_in(2, 0))
        pl.when(l == 1)(lambda: weights_in(2, 1))
        scatter_o.run(attend)
        attended = scatter_o.finish() + param[l, 0:1]
        normal = norm_forward(
            xg[l, own_rows].astype(F32) + attended,
            param[l, 1:2], param[l, 2:3], hat1.at[l], rstd1.at[l],
        )
        own_a[...] = normal
        ng[l, own_rows] = normal.astype(BF16)
        gather_n = gather(ng.at[l], AG_N)
        gather_n.start()

        @pl.when(l == 0)
        def _():
            relay_blocks(0, 1)

        weights_in(1, l)
        weights_in(3, l)
        up_part = own_half(param[l, 8:16, rows_at(place.zl * 2 + place.y, 128)])
        up_more = own_half(param[l, 8:16, rows_at(4 + place.zl * 2 + place.y, 128)])
        up_parts = jnp.where(x == 0, up_part[0:2], up_part[2:4])
        up_more = jnp.where(x == 0, up_more[0:2], up_more[2:4])
        up_bias = jnp.concatenate([up_parts[0:1], up_parts[1:2], up_more[0:1], up_more[1:2]], axis=1)
        scatter_z = scatter(RS_Z)

        def feed_block(j, before):
            rows = place.pair_rows(j)
            value = mm(ng[l, rows], weight(wup, l)) + up_bias
            cdf = 0.5 * (1.0 + lax.erf(value * SQRT_HALF))
            low = (value * cdf).astype(BF16)
            act[l, rows] = low
            dact[l, rows] = cdf + value * (jnp.exp(-0.5 * value * value) * INV_SQRT_2PI)
            scatter_z.give(j, mm(low, wdn[l]))
            if j == 1:
                scatter_z.forward(5)

        gather_n.blocks(feed_block)
        scatter_z.rest()

        @pl.when(l == 0)
        def _():
            relay_out(1)
            relay_blocks(1, 1)
            relay_down(1)

        mixed = scatter_z.finish() + param[l, 3:4]
        result = norm_forward(
            own_a[...] + mixed, param[l, 4:5], param[l, 5:6], hat2.at[l], rstd2.at[l]
        ).astype(BF16)
        ystage[l] = result

        @pl.when(l == 0)
        def _():
            xg[1, own_rows] = result

        is_self, here, there = result_out(ystage.at[l], out_y, 0, l)
        pl.when(is_self)(here.start)
        pl.when(jnp.logical_not(is_self))(there.start)
        return carry

    lax.fori_loop(0, 2, forward_layer, 0)

    d_arrived()

    other_half, this_half = 1 - cube, cube

    def twin_parts(kind, l):
        if kind == 0:
            return g_qkv.at[l, rows_at(other_half, half_rows)], t_qkv, g_qkv.at[l, rows_at(this_half, half_rows)]
        if kind == 1:
            return g_up.at[l, rows_at(other_half, half_rows)], t_up, g_up.at[l, rows_at(this_half, half_rows)]
        if kind == 2:
            return g_prefix.at[l, rows_at(other_half, 32)], t_prefix, g_prefix.at[l, rows_at(this_half, 32)]
        if kind == 3:
            return g_dn.at[l, rows_at(other_half, 128)], t_dn, g_dn.at[l, rows_at(this_half, 128)]
        return g_out.at[l], t_out, g_out.at[l]

    def twin_send(kind, l):
        src, box, own = twin_parts(kind, l)
        return remote(src, box.at[l], tsend.at[kind, l], trecv.at[kind, l], place.twin())

    def twin_chunks(kind, l):
        src, box, own = twin_parts(kind, l)
        rows = ROWS if kind < 2 else 16
        for k in range(src.shape[0] // rows):
            part = pl.ds(k * rows, rows)
            yield remote(
                src.at[part], box.at[l, part], tsend.at[kind, l], trecv.at[kind, l], place.twin()
            ).start

    def twin_start(kind, l):
        copy = twin_send(kind, l)
        if kind == 4:
            pl.when(x != cube)(copy.start)
        else:
            copy.start()

    def owner_pushes(kind, l):
        src, box, own = twin_parts(kind, l)
        mine = x == l

        def start(is_self, part, dst, dev, condition=None):
            def go():
                pl.when(is_self)(local_copy(part, dst, grecv.at[kind]).start)
                pl.when(jnp.logical_not(is_self))(
                    remote(part, dst, gsend.at[kind, l], grecv.at[kind], dev).start
                )

            return go if condition is None else lambda: pl.when(condition)(go)

        if kind < 2:
            got = (got_qkv, got_up)[kind]
            for k in range(8):
                to = lax.rem(k + t + 1, 8)
                yield start(mine & (to == t % 8), own.at[rows_at(to, ROWS)], got.at[tau], (l, cube * 8 + to))
        elif kind == 2:
            for k in range(16):
                to = lax.rem(k + t + 1, 16)
                yield start(mine & (to == t), own, got_prefix.at[tau, rows_at(this_half, 32)], (l, to))
        elif kind == 3:
            yield start(mine, own, got_dn.at[rows_at(x, 128)], place.device(l, cube))
        else:
            yield start(mine, own, got_out, place.device(l, cube), x == cube)

    def owner_add(kind, l):
        src, box, own = twin_parts(kind, l)

        def add():
            twin_send(kind, l).wait_recv()
            own[...] = (own[...].astype(F32) + box[l].astype(F32)).astype(BF16)

        if kind == 4:
            pl.when(x == cube)(add)
        else:
            add()

    def owner_start(kind, l):
        owner_add(kind, l)
        for start in owner_pushes(kind, l):
            start()

    def grads_drain(l):
        for kind in range(5):
            if kind == 4:
                pl.when(x != cube)(twin_send(kind, l).wait_send)
            else:
                twin_send(kind, l).wait_send()
        for kind, ref in ((0, got_qkv), (1, got_up)):
            pl.when(x == l)(bytes_of(ref.at[pl.ds(0, 7)], gsend.at[kind, l]).wait)
            pl.when(x != l)(bytes_of(ref.at[pl.ds(0, 8)], gsend.at[kind, l]).wait)
        for count, condition in ((15, x == l), (16, x != l)):
            pl.when(condition)(bytes_of(got_prefix.at[pl.ds(0, count), pl.ds(0, 32)], gsend.at[2, l]).wait)
            pl.when(condition)(bytes_of(got_rows.at[pl.ds(0, count)], gsend.at[5, l]).wait)
        pl.when(x != l)(bytes_of(g_dn.at[0, pl.ds(0, 128)], gsend.at[3, l]).wait)
        pl.when((x != l) & (x == cube))(bytes_of(g_out.at[0], gsend.at[4, l]).wait)
        for to, src, dst in bias_pairs(l):
            is_self = (x == l) & (cube == to)
            pl.when(jnp.logical_not(is_self))(bytes_of(src, gsend.at[6 + to, l]).wait)

    def rows_start(l):
        def one(k, carry):
            to = lax.rem(k + t + 1, 16)
            src, dst = rowacc.at[l, :, rows_at(to // 2, 128)], got_rows.at[cube * 16 + tau]
            is_self = (x == l) & (to == t)
            pl.when(is_self)(local_copy(src, dst, grecv.at[5]).start)
            pl.when(jnp.logical_not(is_self))(remote(src, dst, gsend.at[5, l], grecv.at[5], (l, to)).start)
            return carry

        lax.fori_loop(0, 16, one, 0)

    def bias_pairs(l):
        for to in range(2):
            yield to, biasacc.at[l], got_bias.at[cube * 2 + x]

    def bias_start(l):
        for to, src, dst in bias_pairs(l):
            is_self = (x == l) & (cube == to)
            pl.when(is_self)(local_copy(src, dst, grecv.at[6]).start)
            pl.when(jnp.logical_not(is_self))(
                remote(src, dst, gsend.at[6 + to, l], grecv.at[6], place.device(l, to)).start
            )

    def backward_layer(step, carry):
        l = 1 - step
        upstream = dstage[l + 1].astype(F32)
        d_sum, d_gain, d_shift = norm_backward(upstream, param[l, 4:5], hat2.at[l], rstd2.at[l])
        own_b[...] = d_sum
        low = d_sum.astype(BF16)
        dzg[own_rows] = low
        gather_z = gather(dzg, AG_Z)
        gather_z.start()
        rowacc[l, 3:4] = d_gain
        rowacc[l, 4:5] = d_shift
        rowacc[l, 5:6] = column_sum(low)
        scatter_n = scatter(RS_N)

        def back_block(j, before):
            rows = place.pair_rows(j)
            low = (dact[l, rows] * mm_nt(dzg[rows], wdn[l])).astype(BF16)
            dfs[rows] = low
            scatter_n.give(j, mm_nt(low, weight(wup, l)))
            if j == 1:
                scatter_n.forward(5)

        gather_z.blocks(back_block)
        scatter_n.rest()
        biasacc[l, 1:2] = column_sum(dfs[...])

        def down_tile(i, carry):
            cols = rows_at(i, 256)
            g_dn[l, :, cols] = mm_tn(act[l], dzg[:, cols]).astype(BF16)
            return carry

        lax.fori_loop(0, width // 256, down_tile, 0)

        def up_tile(i, carry):
            cols = rows_at(i, 256)
            g_up[l, cols] = mm_tn(ng[l, :, cols], dfs[...]).astype(BF16)
            return carry

        lax.fori_loop(0, width // 256, up_tile, 0)
        @pl.when(l == 0)
        def _():
            for kind in (3, 1, 2, 4, 0):
                owner_add(kind, 1)

        def older(start):
            return lambda: pl.when(l == 0)(start)

        pump = Pump()
        twins = [*twin_chunks(3, l), *twin_chunks(1, l)]
        olds = [older(start) for kind in (3, 1, 4, 0, 2) for start in owner_pushes(kind, 1)]
        for k in range(17):
            pump.add(twins[k : k + 1] + olds[2 * k : 2 * k + 2])
        pump.go(3)

        d_normal = own_b[...] + scatter_n.finish()
        d_sum, d_gain, d_shift = norm_backward(d_normal, param[l, 1:2], hat1.at[l], rstd1.at[l])
        own_a[...] = d_sum
        low = d_sum.astype(BF16)
        dog[own_rows] = low
        gather_o = gather(dog, AG_O)
        gather_o.pump = pump
        gather_o.start()
        rowacc[l, 0:1] = d_gain
        rowacc[l, 1:2] = d_shift
        rowacc[l, 2:3] = column_sum(low)
        rows_start(l)


        dkacc[...] = jnp.zeros_like(dkacc)
        dvacc[...] = jnp.zeros_like(dvacc)

        def attend_back(j, before):
            cols = place.pair_rows(j)
            d_context = mm_nt(dog[cols], wout[l]).astype(BF16)
            dcb[cols] = d_context
            d_context_t = mm_nt(wout[l], dog[cols]).astype(BF16).astype(F32)
            sums = jnp.sum(d_context_t * ctf[l, :, cols], axis=0, keepdims=True)
            scores = jnp.where(visible(cols), mm_nt(ks[l], qs[l, cols]), NEGATIVE)
            probs = jnp.exp(scores - lse[l, 0:1, cols])
            d_probs = mm_nt(vs[l], d_context)
            d_scores = (probs * (d_probs - sums)).astype(BF16)
            dvacc[...] += mm(probs.astype(BF16), d_context)
            dkacc[...] += mm(d_scores, qs[l, cols])
            dqt[0:64, cols] = mm(kt[l], d_scores) * 0.125
            pump.go(3)

        gather_o.blocks(attend_back)
        g_prefix[l] = jnp.concatenate([dkacc[tokens:], dvacc[tokens:]], axis=1).astype(BF16)
        twin_start(2, l)
        g_out[l] = mm(ctb[l], dog[...]).astype(BF16)
        twin_start(4, l)

        def assemble(i, carry):
            rows = rows_at(i, BLOCK)
            d_query = dqt[:, rows].T[:, :64]
            value = jnp.concatenate(
                [d_query, dkacc[rows], dvacc[rows], jnp.zeros((BLOCK, 64), F32)], axis=1
            )
            dqkv[rows] = value.astype(BF16)
            dqkvt[:, rows] = value.T.astype(BF16)
            return carry

        lax.fori_loop(0, tokens // BLOCK, assemble, 0)

        def qkv_tile(i, carry):
            cols = rows_at(i, 256)
            g_qkv[l, cols] = mm(dqkvt[...], xg[l, :, cols]).T.astype(BF16)
            return carry

        lax.fori_loop(other_half * 2, other_half * 2 + 2, qkv_tile, 0)
        pump.add(list(twin_chunks(0, l)))
        pump.go(2)
        scatter_x = scatter(RS_X)
        scatter_x.pump = pump
        pump.rate = 2
        scatter_x.run(lambda j: mm_nt(dqkv[place.pair_rows(j)], weight(wqkv, l)))
        biasacc[l, 0:1, 0:256] = column_sum(dqkv[...])
        bias_start(l)
        lax.fori_loop(this_half * 2, this_half * 2 + 2, qkv_tile, 0)
        pump.go(len(pump.waiting))

        @pl.when(l == 0)
        def _():
            for kind in (3, 1):
                owner_start(kind, 0)

        dstage[l] = (own_a[...] + scatter_x.finish()).astype(BF16)
        is_self, here, there = result_out(dstage.at[l], out_dx, 1, l)
        pl.when(is_self)(here.start)
        pl.when(jnp.logical_not(is_self))(there.start)
        return carry

    lax.fori_loop(0, 2, backward_layer, 0)
    for kind in (2, 4, 0):
        owner_start(kind, 0)

    x_sent()
    d_sent()
    weights_drain()
    for l in range(2):
        grads_drain(l)
        for kind, stage, out in ((0, ystage.at[l], out_y), (1, dstage.at[l], out_dx)):
            is_self, here, there = result_out(stage, out, kind, l)
            pl.when(jnp.logical_not(is_self))(there.wait_send)
    for kind, out in ((0, out_y), (1, out_dx)):
        for m in range(2):
            bytes_of(out.at[m], orecv.at[kind, m]).wait()
    for kind, ref in enumerate((got_qkv, got_up, got_prefix, got_dn, got_out, got_rows, got_bias)):
        bytes_of(ref, grecv.at[kind]).wait()


def cube_local(
    inputs, cotangent, lengths, prefix_keys, prefix_values,
    w_query, b_query, w_key, w_value, b_value, w_out, b_out, norm1_gain, norm1_shift,
    w_up, b_up, w_down, b_down, norm2_gain, norm2_shift,
):
    t = lax.axis_index("tok")
    rows, width = w_query.shape[1], w_query.shape[2]
    heads = width // HEAD
    tokens = inputs.shape[1] * lax.axis_size("tok")
    prefix = prefix_keys.shape[1]
    keys = tokens + prefix
    hidden = b_up.shape[1]

    anywhere = pl.BlockSpec(memory_space=pl.ANY)
    smem = pl.BlockSpec(memory_space=pltpu.SMEM)
    dma = pltpu.SemaphoreType.DMA
    V = pltpu.VMEM
    L = 2
    shape = jax.ShapeDtypeStruct
    results = pl.pallas_call(
        kernel,
        out_shape=(
            shape((2, ROWS, width), BF16), shape((2, ROWS, width), BF16),
            shape((16, ROWS, 256), BF16), shape((16, ROWS, 256), BF16),
            shape((hidden, width), BF16), shape((ROWS, width), BF16),
            shape((16, prefix, 128), BF16), shape((32, 8, 128), F32), shape((4, 8, hidden), F32),
        ),
        in_specs=[smem] + [anywhere] * 19,
        out_specs=[anywhere] * 9,
        scratch_shapes=[
            dma((4, 8, PIECES)), dma((4, 8, PIECES)), dma((3, 8, PIECES)), dma((4, 2, 8)), dma((2, 8)),
            dma((4,)), dma((4, 2, 8)), dma((4, 2)), dma((4, 2)), dma((3, 2)), dma((8,)),
            dma((2, 2)), dma((2, 2)), dma((5, 2)), dma((5, 2)), dma((8, 2)), dma((7,)), dma((13,)),
            V((3, rows, width), BF16), V((rows, 4 * width), BF16), V((heads, rows, 256), BF16), V((heads, rows, 256), BF16),
            V((64, 128), F32),
            *[V((1, rows), BF16)] * 8, V((1, hidden), BF16),
            V((L * 1024, 256), BF16), V((L * 1024, 256), BF16), V((L, hidden, width), BF16),
            V((L, ROWS, width), BF16), V((L, 2, prefix, 128), BF16),
            V((8, tokens), jnp.int32), V((keys, 128), jnp.int32),
            V((L, tokens, width), BF16), V((L, tokens, width), BF16),
            V((tokens, width), BF16), V((tokens, width), BF16), V((L, 16, width), F32),
            V((L, tokens, HEAD), BF16), V((L, keys, HEAD), BF16), V((L, keys, HEAD), BF16),
            V((L, HEAD, keys), BF16), V((L, HEAD, keys), BF16),
            V((L, 8, tokens), F32), V((L, HEAD, tokens), BF16), V((L, HEAD, tokens), F32),
            V((L, ROWS, width), F32), V((L, ROWS, 128), F32), V((L, ROWS, width), F32), V((L, ROWS, 128), F32),
            V((L, tokens, hidden), BF16), V((L, tokens, hidden), F32),
            V((4, ROWS, width), F32), V((8, ROWS, width), F32), V((8, ROWS, width), BF16),
            V((2, 8, ROWS, width), BF16), V((8, ROWS, width), BF16), V((2, 8, ROWS, width), BF16),
            V((ROWS, width), F32), V((ROWS, width), F32), V((L, ROWS, width), BF16), V((L + 1, ROWS, width), BF16),
            V((tokens, hidden), BF16), V((tokens, HEAD), BF16), V((8, tokens), F32), V((128, tokens), F32),
            V((keys, HEAD), F32), V((keys, HEAD), F32), V((tokens, 256), BF16), V((256, tokens), BF16),
            V((L, 8, width), F32), V((L, 8, hidden), F32),
            V((L, width, 256), BF16), V((L, width, hidden), BF16), V((L, hidden, width), BF16),
            V((L, ROWS, width), BF16), V((L, prefix, 128), BF16),
            V((L, width // 2, 256), BF16), V((L, width // 2, 256), BF16), V((L, hidden // 2, width), BF16),
            V((L, ROWS, width), BF16), V((L, prefix // 2, 128), BF16),
        ],
        compiler_params=pltpu.CompilerParams(
            collective_id=0, has_side_effects=True, vmem_limit_bytes=60 * 2**20
        ),
    )(
        lengths, inputs, cotangent, w_query, w_key, w_value, w_up, w_down, w_out, prefix_keys, prefix_values,
        b_out, norm1_gain, norm1_shift, b_down, norm2_gain, norm2_shift, b_query, b_value, b_up,
    )
    out_y, out_dx, got_qkv, got_up, got_dn, got_out, got_prefix, got_rows, got_bias = results

    def side_by_side(value):
        return value.astype(F32).transpose(1, 0, 2).reshape(1, value.shape[1], -1)

    up = got_up.reshape(2, 8, rows, 2, 128).transpose(2, 3, 1, 0, 4).astype(F32)
    row_sum = lax.dynamic_slice_in_dim(jnp.sum(got_rows, axis=0), (t % 2) * 64, 64, 1)
    side = t // 8
    bias_up = (got_bias[:2, 1] + got_bias[2:, 1]).reshape(2, 2, 128)
    bias_up = lax.dynamic_index_in_dim(bias_up, side, 1, keepdims=False).reshape(1, hidden)
    bias_qkv = lax.dynamic_index_in_dim(got_bias[:2, 0] + got_bias[2:, 0], side, 0, keepdims=True)
    return (
        out_y[None],
        out_dx[None],
        side_by_side(got_qkv[:, :, :64]),
        bias_qkv[:, 0:64],
        side_by_side(got_qkv[:, :, 64:128]),
        side_by_side(got_qkv[:, :, 128:192]),
        bias_qkv[:, 128:192],
        got_out[None].astype(F32),
        row_sum[2:3],
        row_sum[0:1],
        row_sum[1:2],
        up.reshape(1, rows, -1),
        bias_up,
        got_dn[None].astype(F32),
        row_sum[5:6],
        row_sum[3:4],
        row_sum[4:5],
        side_by_side(got_prefix[:, :, :64]),
        side_by_side(got_prefix[:, :, 64:]),
    )


def solution(mesh):
    placed = (
        P(None, "tok", None),
        P(None, "tok", None),
        P(),
        P("section", None, None),
        P("section", None, None),
        P("section", "tok", None),
        P("section", "tok"),
        P("section", "tok", None),
        P("section", "tok", None),
        P("section", "tok"),
        P("section", "tok", None),
        P("section", "tok"),
        P("section", "tok"),
        P("section", "tok"),
        P("section", "tok", None),
        P("section", "tok"),
        P("section", "tok", None),
        P("section", "tok"),
        P("section", "tok"),
        P("section", "tok"),
    )
    return jax.shard_map(
        cube_local if mesh.shape["tok"] == HEADS else local,
        mesh=mesh,
        in_specs=placed,
        out_specs=(
            P("section", None, "tok", None),
            P("section", None, "tok", None),
            P("section", "tok", None),
            P("section", "tok"),
            P("section", "tok", None),
            P("section", "tok", None),
            P("section", "tok"),
            P("section", "tok", None),
            P("section", "tok"),
            P("section", "tok"),
            P("section", "tok"),
            P("section", "tok", None),
            P("section", "tok"),
            P("section", "tok", None),
            P("section", "tok"),
            P("section", "tok"),
            P("section", "tok"),
            P("section", None, None),
            P("section", None, None),
        ),
        check_vma=False,
    )
```

```python
import jax
import jax.numpy as jnp
from jax import lax
from jax.experimental import pallas as pl
from jax.experimental.pallas import tpu as pltpu
from jax.sharding import PartitionSpec as P

HEADS = 16
HEAD = 64


NEGATIVE = -1e30


def from_behind(block, axis, distance):
    devices = range(lax.axis_size(axis))
    route = [(i - distance, i) for i in devices if i - distance in devices]
    return lax.ppermute(block, axis, route)


def segment_of(lengths_row, positions):
    ends = jnp.cumsum(lengths_row, dtype=jnp.int32)
    return jnp.sum((positions[:, None] >= ends[None, :]).astype(jnp.int32), axis=1, dtype=jnp.int32)


def normalize(value, gain, shift):
    centred = value - jnp.mean(value, axis=-1, keepdims=True)
    spread = jnp.mean(centred * centred, axis=-1, keepdims=True)
    return centred * lax.rsqrt(spread + 1e-05) * gain + shift


def gelu_exact(value):
    return jax.nn.gelu(value, approximate=False)


def project(left, right):
    return jnp.dot(left, right, preferred_element_type=jnp.float32)


def project_back(left, weight):
    return jnp.einsum("tf,df->td", left, weight, preferred_element_type=jnp.float32)


def contract_rows(left, right):
    return jnp.einsum("tf,td->fd", left, right, preferred_element_type=jnp.float32)


def split_heads(value):
    return value.reshape(value.shape[0], HEADS, HEAD)


def in_blocks(step_fn, running, arrays, offset_row):
    total_rows = arrays[0].shape[0]
    block_rows = 1024 if total_rows > 1024 and total_rows % 1024 == 0 else total_rows
    if block_rows == total_rows:
        return step_fn(running, arrays, offset_row)
    stacked = tuple(
        (
            member.reshape((total_rows // block_rows, block_rows) + member.shape[1:])
            for member in arrays
        )
    )
    offsets = offset_row + block_rows * jnp.arange(total_rows // block_rows, dtype=jnp.int32)

    def scan_step(inner, packet):
        return (step_fn(inner, packet[0], packet[1]), None)

    result, unused = lax.scan(scan_step, running, (stacked, offsets))
    return result


def masked_scores(query_part, key_part, query_segment, key_segment):
    raw_scores = jnp.einsum(
        "qhe,khe->hqk",
        split_heads(query_part),
        split_heads(key_part),
        preferred_element_type=jnp.float32,
    ) * HEAD ** (-0.5)
    return jnp.where((query_segment[:, None] == key_segment[None, :])[None], raw_scores, NEGATIVE)


def prefix_scores(queries, prefix_key_rows):
    return jnp.einsum(
        "qhe,khe->hqk",
        split_heads(queries),
        split_heads(prefix_key_rows),
        preferred_element_type=jnp.float32,
    ) * HEAD ** (-0.5)


def gather_weights(shards):
    return (
        lax.all_gather(shards[0], "tok", axis=1, tiled=True),
        lax.all_gather(shards[1], "tok", axis=1, tiled=True),
        lax.all_gather(shards[2], "tok", axis=1, tiled=True),
        lax.all_gather(shards[3], "tok", axis=1, tiled=True),
        lax.all_gather(shards[4], "tok", axis=1, tiled=True),
        lax.all_gather(shards[5], "tok", axis=1, tiled=True),
        lax.all_gather(shards[6], "tok", axis=1, tiled=True),
        lax.all_gather(shards[7], "tok", axis=1, tiled=True),
        lax.all_gather(shards[8], "tok", axis=1, tiled=True),
        lax.all_gather(shards[9], "tok", axis=1, tiled=True),
        lax.all_gather(shards[10], "tok", axis=1, tiled=True),
        lax.all_gather(shards[11], "tok", axis=1, tiled=True),
        lax.all_gather(shards[12], "tok", axis=1, tiled=True),
        lax.all_gather(shards[13], "tok", axis=1, tiled=True),
        lax.all_gather(shards[14], "tok", axis=1, tiled=True),
    )


def front_part(inbound, weights):
    queries = (project(inbound, weights[0]) + weights[1].astype(jnp.float32)).astype(jnp.bfloat16)
    key_rows = project(inbound, weights[2]).astype(jnp.bfloat16)
    value_rows = (project(inbound, weights[3]) + weights[4].astype(jnp.float32)).astype(
        jnp.bfloat16
    )
    return (queries, key_rows, value_rows)


def attention_forward(
    queries, key_rows, value_rows, prefix_key_rows, prefix_value_rows, lengths_row, own_segment
):
    first_scores = prefix_scores(queries, prefix_key_rows)
    highest = jnp.max(first_scores, axis=2)
    denominator = jnp.sum(jnp.exp(first_scores - highest[..., None]), axis=2)

    def total_block(state, piece, offset_row):
        old_high, old_denominator = state
        key_part = piece[0]
        key_segment = segment_of(
            lengths_row, offset_row + jnp.arange(key_part.shape[0], dtype=jnp.int32)
        )
        raw_scores = masked_scores(queries, key_part, own_segment, key_segment)
        new_high = jnp.maximum(old_high, jnp.max(raw_scores, axis=2))
        new_denominator = old_denominator * jnp.exp(old_high - new_high) + jnp.sum(
            jnp.exp(raw_scores - new_high[..., None]), axis=2
        )
        return (new_high, new_denominator)

    highest, denominator = in_blocks(
        total_block,
        (highest, denominator),
        (lax.all_gather(key_rows, "tok", axis=0, tiled=True),),
        jnp.int32(0),
    )
    logsum = highest + jnp.log(denominator)
    summed = jnp.einsum(
        "hqk,khe->qhe",
        jnp.exp(first_scores - logsum[..., None]).astype(jnp.bfloat16),
        split_heads(prefix_value_rows),
        preferred_element_type=jnp.float32,
    )

    def absorb_block(running, piece, offset_row):
        key_part, value_part = piece
        key_segment = segment_of(
            lengths_row, offset_row + jnp.arange(key_part.shape[0], dtype=jnp.int32)
        )
        probs_part = jnp.exp(
            masked_scores(queries, key_part, own_segment, key_segment) - logsum[..., None]
        )
        return running + jnp.einsum(
            "hqk,khe->qhe",
            probs_part.astype(jnp.bfloat16),
            split_heads(value_part),
            preferred_element_type=jnp.float32,
        )

    summed = in_blocks(
        absorb_block,
        summed,
        (
            lax.all_gather(key_rows, "tok", axis=0, tiled=True),
            lax.all_gather(value_rows, "tok", axis=0, tiled=True),
        ),
        jnp.int32(0),
    )
    context = summed.reshape(queries.shape[0], -1)
    return (context, logsum)


def back_part(inbound, context, weights):
    context_low = context.astype(jnp.bfloat16)
    attended = project(context_low, weights[5]) + weights[6].astype(jnp.float32)
    normal_one, pull_one = jax.vjp(
        normalize,
        inbound.astype(jnp.float32) + attended,
        weights[7].astype(jnp.float32),
        weights[8].astype(jnp.float32),
    )
    normal_one_low = normal_one.astype(jnp.bfloat16)
    activation, pull_gelu = jax.vjp(
        gelu_exact, project(normal_one_low, weights[9]) + weights[10].astype(jnp.float32)
    )
    activation_low = activation.astype(jnp.bfloat16)
    mixed = project(activation_low, weights[11]) + weights[12].astype(jnp.float32)
    result, pull_two = jax.vjp(
        normalize,
        normal_one + mixed,
        weights[13].astype(jnp.float32),
        weights[14].astype(jnp.float32),
    )
    return (result, context_low, normal_one_low, pull_one, activation_low, pull_gelu, pull_two)


def query_backward(
    queries,
    d_context,
    logsum,
    delta,
    prefix_key_rows,
    prefix_value_rows,
    key_rows,
    value_rows,
    lengths_row,
    own_segment,
):
    context_heads = split_heads(d_context)
    query_heads = split_heads(queries)
    prefix_prob = jnp.exp(prefix_scores(queries, prefix_key_rows) - logsum[..., None])
    prefix_dprob = jnp.einsum(
        "qhe,khe->hqk",
        context_heads,
        split_heads(prefix_value_rows),
        preferred_element_type=jnp.float32,
    )
    prefix_dscore = (prefix_prob * (prefix_dprob - delta[..., None])).astype(jnp.bfloat16)
    grad_prefix_keys = jnp.einsum(
        "hqk,qhe->khe", prefix_dscore, query_heads, preferred_element_type=jnp.float32
    ) * HEAD ** (-0.5)
    grad_prefix_values = jnp.einsum(
        "hqk,qhe->khe",
        prefix_prob.astype(jnp.bfloat16),
        context_heads,
        preferred_element_type=jnp.float32,
    )
    grad_start = jnp.einsum(
        "hqk,khe->qhe",
        prefix_dscore,
        split_heads(prefix_key_rows),
        preferred_element_type=jnp.float32,
    )

    def pull_block(running, piece, offset_row):
        key_part, value_part = piece
        key_segment = segment_of(
            lengths_row, offset_row + jnp.arange(key_part.shape[0], dtype=jnp.int32)
        )
        probs_part = jnp.exp(
            masked_scores(queries, key_part, own_segment, key_segment) - logsum[..., None]
        )
        dprob = jnp.einsum(
            "qhe,khe->hqk",
            context_heads,
            split_heads(value_part),
            preferred_element_type=jnp.float32,
        )
        dscore = (probs_part * (dprob - delta[..., None])).astype(jnp.bfloat16)
        return running + jnp.einsum(
            "hqk,khe->qhe", dscore, split_heads(key_part), preferred_element_type=jnp.float32
        )

    grad_queries = in_blocks(
        pull_block,
        grad_start,
        (
            lax.all_gather(key_rows, "tok", axis=0, tiled=True),
            lax.all_gather(value_rows, "tok", axis=0, tiled=True),
        ),
        jnp.int32(0),
    )
    row_count = queries.shape[0]
    return (
        (grad_queries * HEAD ** (-0.5)).reshape(row_count, -1),
        grad_prefix_keys.reshape(prefix_key_rows.shape),
        grad_prefix_values.reshape(prefix_value_rows.shape),
    )


def key_backward(queries, d_context, logsum, delta, key_rows, value_rows, lengths_row, own_segment):
    all_logsum, all_delta = (
        lax.all_gather(logsum, "tok", axis=1, tiled=True),
        lax.all_gather(delta, "tok", axis=1, tiled=True),
    )
    value_heads = split_heads(value_rows)

    def spread_block(running, piece, offset_row):
        grad_keys, grad_values = running
        query_part, context_part = piece
        part_rows = query_part.shape[0]
        part_logsum = lax.dynamic_slice_in_dim(all_logsum, offset_row, part_rows, 1)
        part_delta = lax.dynamic_slice_in_dim(all_delta, offset_row, part_rows, 1)
        part_segment = segment_of(lengths_row, offset_row + jnp.arange(part_rows, dtype=jnp.int32))
        probs_part = jnp.exp(
            masked_scores(query_part, key_rows, part_segment, own_segment) - part_logsum[..., None]
        )
        context_heads = split_heads(context_part)
        dprob = jnp.einsum(
            "qhe,khe->hqk", context_heads, value_heads, preferred_element_type=jnp.float32
        )
        dscore = (probs_part * (dprob - part_delta[..., None])).astype(jnp.bfloat16)
        new_keys = grad_keys + jnp.einsum(
            "hqk,qhe->khe", dscore, split_heads(query_part), preferred_element_type=jnp.float32
        )
        new_values = grad_values + jnp.einsum(
            "hqk,qhe->khe",
            probs_part.astype(jnp.bfloat16),
            context_heads,
            preferred_element_type=jnp.float32,
        )
        return (new_keys, new_values)

    def spread(running, piece, offset_row):
        return in_blocks(spread_block, running, piece, offset_row)

    empty = jnp.zeros((key_rows.shape[0], HEADS, HEAD), jnp.float32)
    grad_keys, grad_values = spread(
        (empty, empty),
        (
            lax.all_gather(queries, "tok", axis=0, tiled=True),
            lax.all_gather(d_context, "tok", axis=0, tiled=True),
        ),
        jnp.int32(0),
    )
    row_count = key_rows.shape[0]
    return ((grad_keys * HEAD ** (-0.5)).reshape(row_count, -1), grad_values.reshape(row_count, -1))


def layer_backward(
    inbound, upstream, weights, prefix_key_rows, prefix_value_rows, lengths_row, own_segment
):
    queries, key_rows, value_rows = front_part(inbound, weights)
    context, logsum = attention_forward(
        queries, key_rows, value_rows, prefix_key_rows, prefix_value_rows, lengths_row, own_segment
    )
    result, context_low, normal_one_low, pull_one, activation_low, pull_gelu, pull_two = back_part(
        inbound, context, weights
    )
    d_sum, d_gain_two, d_shift_two = pull_two(upstream.astype(jnp.float32))
    d_mixed = d_sum.astype(jnp.bfloat16)
    grad_down = contract_rows(activation_low, d_mixed)
    grad_down_bias = jnp.sum(d_mixed.astype(jnp.float32), axis=0)
    (d_pre,) = pull_gelu(project_back(d_mixed, weights[11]))
    d_pre_low = d_pre.astype(jnp.bfloat16)
    grad_up = contract_rows(normal_one_low, d_pre_low)
    grad_up_bias = jnp.sum(d_pre_low.astype(jnp.float32), axis=0)
    d_resid, d_gain_one, d_shift_one = pull_one(d_sum + project_back(d_pre_low, weights[9]))
    d_attended = d_resid.astype(jnp.bfloat16)
    grad_out = contract_rows(context_low, d_attended)
    grad_out_bias = jnp.sum(d_attended.astype(jnp.float32), axis=0)
    d_context = project_back(d_attended, weights[5]).astype(jnp.bfloat16)
    delta = jnp.sum(split_heads(d_context).astype(jnp.float32) * split_heads(context), axis=2).T
    grad_queries, grad_prefix_keys, grad_prefix_values = query_backward(
        queries,
        d_context,
        logsum,
        delta,
        prefix_key_rows,
        prefix_value_rows,
        key_rows,
        value_rows,
        lengths_row,
        own_segment,
    )
    grad_keys, grad_values = key_backward(
        queries, d_context, logsum, delta, key_rows, value_rows, lengths_row, own_segment
    )
    queries_low = grad_queries.astype(jnp.bfloat16)
    keys_low = grad_keys.astype(jnp.bfloat16)
    values_low = grad_values.astype(jnp.bfloat16)
    grad_query_weight = contract_rows(inbound, queries_low)
    grad_query_bias = jnp.sum(queries_low.astype(jnp.float32), axis=0)
    grad_key_weight = contract_rows(inbound, keys_low)
    grad_value_weight = contract_rows(inbound, values_low)
    grad_value_bias = jnp.sum(values_low.astype(jnp.float32), axis=0)
    d_input = (
        d_resid
        + project_back(queries_low, weights[0])
        + project_back(keys_low, weights[2])
        + project_back(values_low, weights[3])
    )
    grads = (
        grad_query_weight,
        grad_query_bias,
        grad_key_weight,
        grad_value_weight,
        grad_value_bias,
        grad_out,
        grad_out_bias,
        d_gain_one,
        d_shift_one,
        grad_up,
        grad_up_bias,
        grad_down,
        grad_down_bias,
        d_gain_two,
        d_shift_two,
    )
    return (d_input, grads, (grad_prefix_keys, grad_prefix_values))


def sum_each(grads):
    return (
        lax.psum_scatter(grads[0][None], "tok", scatter_dimension=1, tiled=True),
        lax.psum_scatter(grads[1][None], "tok", scatter_dimension=1, tiled=True),
        lax.psum_scatter(grads[2][None], "tok", scatter_dimension=1, tiled=True),
        lax.psum_scatter(grads[3][None], "tok", scatter_dimension=1, tiled=True),
        lax.psum_scatter(grads[4][None], "tok", scatter_dimension=1, tiled=True),
        lax.psum_scatter(grads[5][None], "tok", scatter_dimension=1, tiled=True),
        lax.psum_scatter(grads[6][None], "tok", scatter_dimension=1, tiled=True),
        lax.psum_scatter(grads[7][None], "tok", scatter_dimension=1, tiled=True),
        lax.psum_scatter(grads[8][None], "tok", scatter_dimension=1, tiled=True),
        lax.psum_scatter(grads[9][None], "tok", scatter_dimension=1, tiled=True),
        lax.psum_scatter(grads[10][None], "tok", scatter_dimension=1, tiled=True),
        lax.psum_scatter(grads[11][None], "tok", scatter_dimension=1, tiled=True),
        lax.psum_scatter(grads[12][None], "tok", scatter_dimension=1, tiled=True),
        lax.psum_scatter(grads[13][None], "tok", scatter_dimension=1, tiled=True),
        lax.psum_scatter(grads[14][None], "tok", scatter_dimension=1, tiled=True),
    )


def by_section(listing, is_first, early_first):
    stacked = jnp.stack(listing)
    window_count = len(listing) - 1
    if early_first:
        return jnp.where(is_first, stacked[:window_count], stacked[1:])
    return jnp.where(is_first, stacked[1:], stacked[:window_count])


def local(
    inputs,
    cotangent,
    lengths,
    prefix_keys,
    prefix_values,
    w_query,
    b_query,
    w_key,
    w_value,
    b_value,
    w_out,
    b_out,
    norm1_gain,
    norm1_shift,
    w_up,
    b_up,
    w_down,
    b_down,
    norm2_gain,
    norm2_shift,
):
    micro_count = inputs.shape[0]
    tok_rows = inputs.shape[1]
    model_width = inputs.shape[2]
    section_index = lax.axis_index("section")
    is_first = section_index == 0
    own_positions = lax.axis_index("tok") * tok_rows + jnp.arange(tok_rows, dtype=jnp.int32)
    shard_list = (
        w_query,
        b_query,
        w_key,
        w_value,
        b_value,
        w_out,
        b_out,
        norm1_gain,
        norm1_shift,
        w_up,
        b_up,
        w_down,
        b_down,
        norm2_gain,
        norm2_shift,
    )
    prefix_key_rows = prefix_keys[0]
    prefix_value_rows = prefix_values[0]
    weights = tuple((member[0] for member in gather_weights(shard_list)))
    received = jnp.zeros((tok_rows, model_width), jnp.bfloat16)
    seen_inputs = []
    seen_outputs = []
    seen_context = []
    seen_logsum = []
    for moment in range(micro_count + 1):
        current = jnp.clip(moment - section_index, 0, micro_count - 1)
        lengths_row = lengths[current]
        own_segment = segment_of(lengths_row, own_positions)
        inbound = jnp.where(is_first, inputs[min(moment, micro_count - 1)], received)
        queries, key_rows, value_rows = front_part(inbound, weights)
        context, logsum = attention_forward(
            queries,
            key_rows,
            value_rows,
            prefix_key_rows,
            prefix_value_rows,
            lengths_row,
            own_segment,
        )
        result = back_part(inbound, context, weights)[0].astype(jnp.bfloat16)
        seen_inputs.append(inbound)
        seen_outputs.append(result)
        seen_context.append(context)
        seen_logsum.append(logsum)
        if moment < micro_count:
            received = from_behind(result, "section", 1)
    kept_inputs = by_section(seen_inputs, is_first, True)
    weights = tuple((member[0] for member in gather_weights(shard_list)))
    back_received = jnp.zeros((tok_rows, model_width), jnp.bfloat16)
    grad_shards = tuple((jnp.zeros(member.shape, jnp.float32) for member in shard_list))
    prefix_key_total = jnp.zeros(prefix_key_rows.shape, jnp.float32)
    prefix_value_total = jnp.zeros(prefix_value_rows.shape, jnp.float32)
    seen_grads = []
    for moment in range(micro_count + 1):
        current = moment - 1 + section_index
        is_valid = ((current >= 0) & (current < micro_count)).astype(jnp.float32)
        picked = jnp.clip(current, 0, micro_count - 1)
        lengths_row = lengths[picked]
        own_segment = segment_of(lengths_row, own_positions)
        upstream = jnp.where(is_first, back_received, cotangent[min(moment, micro_count - 1)])
        d_input, grads, prefix_grads = layer_backward(
            kept_inputs[picked],
            upstream,
            weights,
            prefix_key_rows,
            prefix_value_rows,
            lengths_row,
            own_segment,
        )
        d_input_low = d_input.astype(jnp.bfloat16)
        seen_grads.append(d_input_low)
        if moment < micro_count:
            back_received = from_behind(d_input_low, "section", -1)
        grads = tuple((member * is_valid for member in grads))
        prefix_key_total = prefix_key_total + prefix_grads[0] * is_valid
        prefix_value_total = prefix_value_total + prefix_grads[1] * is_valid
        scattered = sum_each(grads)
        grad_shards = tuple((older + newer for older, newer in zip(grad_shards, scattered)))
    layer_outputs = by_section(seen_outputs, is_first, True)[None]
    input_grads = by_section(seen_grads, is_first, False)[None]
    prefix_sums = lax.psum((prefix_key_total, prefix_value_total), "tok")
    return (
        layer_outputs,
        input_grads,
        grad_shards[0],
        grad_shards[1],
        grad_shards[2],
        grad_shards[3],
        grad_shards[4],
        grad_shards[5],
        grad_shards[6],
        grad_shards[7],
        grad_shards[8],
        grad_shards[9],
        grad_shards[10],
        grad_shards[11],
        grad_shards[12],
        grad_shards[13],
        grad_shards[14],
        prefix_sums[0][None],
        prefix_sums[1][None],
    )


MESH = pl.DeviceIdType.MESH
F32 = jnp.float32
BF16 = jnp.bfloat16
ROWS = 64
PIECE = 16
PIECES = ROWS // PIECE
BLOCK = 256
SQRT_HALF = 0.7071067811865476
INV_SQRT_2PI = 0.3989422804014327
AG_X, AG_N, AG_Z, AG_O = range(4)
RS_O, RS_Z, RS_N, RS_X = range(4)


def flip(bit, other):
    return bit + other - 2 * bit * other


def mm(left, right):
    return jnp.dot(left, right, preferred_element_type=F32)


def mm_nt(left, right):
    return lax.dot_general(left, right, (((1,), (1,)), ((), ())), preferred_element_type=F32)


def mm_tn(left, right):
    return lax.dot_general(left, right, (((0,), (0,)), ((), ())), preferred_element_type=F32)


def rows_at(index, size):
    return pl.ds(pl.multiple_of(index * size, size), size)


def remote(src, dst, send, recv, device):
    return pltpu.make_async_remote_copy(
        src_ref=src, dst_ref=dst, send_sem=send, recv_sem=recv, device_id=device, device_id_type=MESH
    )


def local_copy(src, dst, sem):
    return pltpu.make_async_copy(src, dst, sem)


def bytes_of(ref, sem):
    return pltpu.make_async_copy(ref, ref, sem)


class Place:
    def __init__(self):
        self.x = lax.axis_index("section")
        self.t = lax.axis_index("tok")
        z = self.t // 4
        self.y = (self.t // 2) % 2
        self.core = self.t % 2
        self.cube = z // 2
        self.zl = z % 2
        self.chip = self.x * 4 + self.zl * 2 + self.y
        self.tau = self.chip * 2 + self.core

    def device(self, x, cube):
        return (x, cube * 8 + self.zl * 4 + self.y * 2 + self.core)

    def twin(self):
        return self.device(self.x, 1 - self.cube)

    def sibling(self):
        return (self.x, self.t + 1 - 2 * self.core)

    def peer(self, r):
        zl, y = flip(self.zl, (r // 2) % 2), flip(self.y, r % 2)
        return (flip(self.x, r // 4), self.cube * 8 + zl * 4 + y * 2 + self.core)

    def peer_chip(self, r):
        return flip(self.x, r // 4) * 4 + flip(self.zl, (r // 2) % 2) * 2 + flip(self.y, r % 2)

    def pair_rows(self, j):
        return rows_at(flip(self.x, j // 2) * 2 + flip(self.zl, j % 2), BLOCK)


def hops_of(first, last):
    hops = {(r, q): hop for q in range(PIECES) for r, hop in first}
    for q, (via, step, seen) in enumerate(last):
        hops[(via, q)] = (step, seen)
    return hops


class Pump:
    def __init__(self, rate=2):
        self.waiting = []
        self.rate = rate

    def add(self, starts):
        self.waiting += starts

    def go(self, count=None):
        count = self.rate if count is None else count
        for start in self.waiting[:count]:
            start()
        del self.waiting[:count]


class Gather:
    CUBE = (
        (4, 2, 1), ((1, 2, 4), (3, 6, 5), (7,)), (0, 2, 1, 3),
        hops_of(((1, (2, 3)), (2, (4, 6)), (4, (1, 5))), ((3, 4, 7), (6, 1, 7), (5, 2, 7), (3, 4, 7))),
    )

    def __init__(self, place, buf, recv, sib, sends):
        self.place, self.buf, self.recv, self.sib, self.sends = place, buf, recv, sib, sends
        self.near, self.stages, self.order, self.hops = self.CUBE
        self.pump = Pump()

    def piece(self, r, q, other=0):
        core = flip(self.place.core, other)
        row = (self.place.peer_chip(r) * 2 + core) * ROWS + q * PIECE
        return self.buf.at[pl.ds(pl.multiple_of(row, PIECE), PIECE)]

    def start(self):
        for q in range(PIECES):
            own = self.piece(0, q)
            for r in self.near:
                remote(own, own, self.sends.at[0, r, q], self.recv.at[r, q], self.place.peer(r)).start()
            self.to_sibling(0, q).start()

    def to_sibling(self, r, q):
        rows = self.piece(r, q)
        return remote(rows, rows, self.sends.at[1, r, q], self.sib.at[r, q], self.place.sibling())

    def arrive(self, r, q):
        rows = self.piece(r, q)
        bytes_of(rows, self.recv.at[r, q]).wait()
        if (r, q) in self.hops:
            hop, seen = self.hops[(r, q)]
            remote(rows, rows, self.sends.at[2, r, q], self.recv.at[seen, q], self.place.peer(hop)).start()
        self.to_sibling(r, q).start()

    def stage(self, number):
        for q in range(PIECES):
            for r in self.stages[number]:
                self.arrive(r, q)
            self.pump.go()

    def pair_ready(self, j):
        for r in (2 * j, 2 * j + 1):
            for q in range(PIECES):
                bytes_of(self.piece(r, q, 1), self.sib.at[r, q]).wait()

    def blocks(self, use):
        before = None
        for i, j in enumerate(self.order):
            if i < len(self.stages):
                self.stage(i)
            self.pair_ready(j)
            use(j, before)
            before = j
        self.drain()

    def drain(self):
        own = self.piece(0, 0)
        for q in range(PIECES):
            for r in self.near:
                bytes_of(own, self.sends.at[0, r, q]).wait()
            for r in range(2 * len(self.order)):
                bytes_of(own, self.sends.at[1, r, q]).wait()
        for r, q in self.hops:
            bytes_of(own, self.sends.at[2, r, q]).wait()


class Scatter:
    WAY = {3: (2, (7, 0)), 6: (4, (7, 1)), 5: (1, None), 1: (1, 3), 2: (2, 6), 4: (4, 5)}

    def __init__(self, place, recv, sends, half, keep, sib_out, sib_in, out, inbox):
        self.place, self.recv, self.sends = place, recv, sends
        self.half, self.keep, self.sib_out, self.sib_in = half, keep, sib_out, sib_in
        self.out, self.inbox = out, inbox
        self.pump = Pump()

    def pair(self, r):
        return remote(
            self.sib_out.at[r], self.sib_in.at[r], self.sends.at[0, r], self.recv.at[0, r], self.place.sibling()
        )

    def push(self, r):
        step = self.WAY[r][0]
        return remote(
            self.out.at[r], self.inbox.at[r], self.sends.at[1, r], self.recv.at[1, r], self.place.peer(step)
        )

    def part(self, q):
        rows, slot = pl.ds(q * 32, 32), (7, 0)[q]
        return remote(
            self.out.at[7, rows], self.inbox.at[7, rows], self.sends.at[1, slot], self.recv.at[1, slot],
            self.place.peer((4, 1)[q]),
        )

    def give(self, j, partial):
        for k in range(4):
            self.half[k] = partial[k * ROWS : (k + 1) * ROWS]
        core = self.place.core
        for b in range(2):
            r = 2 * j + flip(self.place.y, b)
            self.keep[r] = self.half[2 * b + core]
            self.sib_out[r] = self.half[2 * b + 1 - core].astype(BF16)
            self.pair(r).start()

    def forward(self, r):
        self.pair(r).wait_recv()
        if r == 7:
            self.out[7] = (self.keep[7] + self.sib_in[7].astype(F32)).astype(BF16)
            self.part(0).start()
            self.part(1).start()
            return
        more = self.WAY[r][1]
        if more is None:
            self.out[r] = (self.keep[r] + self.sib_in[r].astype(F32)).astype(BF16)
        elif isinstance(more, int):
            self.push(more).wait_recv()
            self.out[r] = (self.keep[r] + self.sib_in[r].astype(F32) + self.inbox[more].astype(F32)).astype(BF16)
        else:
            q = more[1]
            self.part(q).wait_recv()
            for k in range(2):
                rows = pl.ds(k * 32, 32)
                total = self.keep[r, rows] + self.sib_in[r, rows].astype(F32)
                if k == q:
                    total = total + self.inbox[7, rows].astype(F32)
                self.out[r, rows] = total.astype(BF16)
        self.push(r).start()

    def run(self, produce):
        def step(i, carry):
            @pl.when(i < 4)
            def _():
                self.give(3 - i, produce(3 - i))

            for when, steps in ((1, (7,)), (2, (5,)), (3, (3, 6)), (4, (1, 2, 4))):
                @pl.when(i == when)
                def _():
                    for r in steps:
                        self.forward(r)
                    self.pump.go()

            return carry

        lax.fori_loop(0, 5, step, 0)

    def rest(self):
        for r in (7, 3, 6, 1, 2, 4):
            self.forward(r)

    def finish(self):
        self.pair(0).wait_recv()
        self.keep[0] = self.keep[0] + self.sib_in[0].astype(F32)
        for r in (1, 2, 4):
            self.push(r).wait_recv()
            self.keep[0] = self.keep[0] + self.inbox[r].astype(F32)
        for r in range(8):
            self.pair(r).wait_send()
        for r in self.WAY:
            self.push(r).wait_send()
        for q in range(2):
            self.part(q).wait_send()
        return self.keep[0]


def norm_forward(value, gain, shift, hat_ref, rstd_ref):
    centred = value - jnp.mean(value, axis=-1, keepdims=True)
    rstd = lax.rsqrt(jnp.mean(centred * centred, axis=-1, keepdims=True) + 1e-05)
    hat = centred * rstd
    hat_ref[...] = hat
    rstd_ref[...] = jnp.broadcast_to(rstd, rstd_ref.shape)
    return hat * gain + shift


def norm_backward(upstream, gain, hat_ref, rstd_ref):
    hat = hat_ref[...]
    scaled = upstream * gain
    mean_one = jnp.mean(scaled, axis=-1, keepdims=True)
    mean_two = jnp.mean(scaled * hat, axis=-1, keepdims=True)
    result = rstd_ref[:, :1] * (scaled - mean_one - hat * mean_two)
    d_gain = jnp.sum(upstream * hat, axis=0, keepdims=True)
    d_shift = jnp.sum(upstream, axis=0, keepdims=True)
    return result, d_gain, d_shift


def column_sum(low):
    return jnp.sum(low.astype(F32), axis=0, keepdims=True)


def kernel(
    lengths, inputs, cotangent, wq_src, wk_src, wv_src, wup_src, wdn_src, wout_src, pk_src, pv_src,
    v0, v1, v2, v3, v4, v5, v6, v7, v8,
    out_y, out_dx, out_q, out_k, out_v, out_o, out_up, out_dn, out_pk, out_pv, got_rows, got_bias,
    ag_recv, ag_sib, ag_send, rs_recv, rs_send,
    wsend, wown, wtwin, wrelay, psem, xsem, osend, orecv, tsend, trecv, gsend, grecv, rsem,
    raw_qkv, raw_up, pack_qkv, pack_up, vrows, u0, u1, u2, u3, u4, u5, u6, u7, u8,
    wqkv, wup, wdn, wout, pre,
    qseg, kseg, xg, ng, dzg, dog, param,
    qs, ks, vs, kt, vt, lse, ctb, ctf,
    hat1, rstd1, hat2, rstd2, act, dact,
    half, keep, sib_out, sib_in, rs_out, inbox,
    own_a, own_b, ystage, dstage,
    dfs, dcb, delta, dqt, dkacc, dvacc, dqkv, dqkvt,
    rowacc, biasacc, g_qkv, g_up, g_dn, g_out, g_prefix,
    t_qkv, t_up, t_dn, t_out, t_prefix,
    got_qkv, got_up, got_dn, got_out, got_prefix,
):
    place = Place()
    x, t, cube, core, tau = place.x, place.t, place.cube, place.core, place.tau
    tokens = qs.shape[1]
    width = xg.shape[2]
    half_rows = 8 * ROWS
    barrier = pltpu.get_barrier_semaphore()

    def greet(i, carry):
        gx, gt = i // 16, i % 16

        @pl.when((gx != x) | (gt != t))
        def _():
            pl.semaphore_signal(barrier, inc=1, device_id=(gx, gt), device_id_type=MESH)

        return carry

    lax.fori_loop(0, 32, greet, 0)

    raw = [local_copy(src.at[0], raw_qkv.at[i], rsem.at[i]) for i, src in enumerate((wq_src, wk_src, wv_src))]
    raw.append(local_copy(wup_src.at[0], raw_up, rsem.at[3]))
    vectors = (u0, u1, u2, u3, u4, u5, u6, u7, u8)
    for i, (src, dst) in enumerate(zip((v0, v1, v2, v3, v4, v5, v6, v7, v8), vectors)):
        raw.append(local_copy(src, dst, rsem.at[4 + i]))
    for copy in raw:
        copy.start()
    vrows[...] = jnp.zeros_like(vrows)
    for copy in raw:
        copy.wait()
    for i in range(8):
        vrows[i : i + 1, 0:64] = vectors[i][...].astype(F32)
    up_row = u8[...].astype(F32)
    for i in range(4):
        vrows[8 + i : 9 + i, 0:64] = up_row[:, i * 64 : (i + 1) * 64]
    vector_columns = vrows[...].T[0:64]

    def pack_heads(h, carry):
        cols = rows_at(h, 128)
        parts = [raw_qkv[i, :, cols].astype(F32) for i in range(3)]
        for s in range(2):
            sides = [part[:, s * 64 : (s + 1) * 64] for part in parts]
            pack_qkv[2 * h + s] = jnp.concatenate(sides + [vector_columns], axis=1).astype(BF16)
        return carry

    lax.fori_loop(0, 8, pack_heads, 0)
    for side in range(2):
        for rest in range(8):
            for zhi in range(2):
                start = (zhi * 8 + rest) * 256 + side * 128
                pack_up[side * 8 + rest, :, zhi * 128 : (zhi + 1) * 128] = raw_up[:, start : start + 128]

    pl.semaphore_wait(barrier, 31)

    own_rows = rows_at(tau, ROWS)
    first, last = pl.ds(0, 32), pl.ds(32, 32)
    diagonal = place.device(1 - x, 1 - cube)
    neighbour = place.device(1 - x, cube)

    def shares(source, target, far, sem):
        here = local_copy(source.at[cube], target, xsem.at[sem])
        to_twin = remote(source.at[1 - cube, first], target.at[first], xsem.at[sem + 1], xsem.at[sem + 2], place.twin())
        to_diagonal = remote(source.at[1 - cube, last], far.at[last], xsem.at[sem + 1], xsem.at[sem + 3], diagonal)

        def start():
            @pl.when(x == cube)
            def _():
                to_twin.start()
                here.start()

            pl.when(x != cube)(to_diagonal.start)

        def arrived():
            @pl.when(x != cube)
            def _():
                to_twin.wait_recv()
                to_diagonal.wait_recv()

            pl.when(x == cube)(here.wait)

        def sent():
            pl.when(x == cube)(to_twin.wait_send)
            pl.when(x != cube)(to_diagonal.wait_send)

        return start, arrived, sent

    x_start, x_arrived, x_sent = shares(inputs, xg.at[0, own_rows], xg.at[0, rows_at(tau + 8 - 16 * x, ROWS)], 0)
    d_start, d_arrived, d_sent = shares(cotangent, dstage.at[2], dstage.at[2], 4)
    x_start()

    def spread_pushes(kind):
        src_all, dst_all = (pack_qkv, pack_up)[kind], (wqkv, wup)[kind]
        dst, sem = dst_all.at[rows_at(x * 16 + t, ROWS)], wown.at[kind, x, t % 8]
        for k in range(16):
            to = lax.rem(k + tau + 1, 16)

            def go(to=to):
                src = src_all.at[to]
                pl.when(to == tau)(local_copy(src, dst, sem).start)
                pl.when(to != tau)(remote(src, dst, wsend.at[kind], sem, (to // 8, cube * 8 + to % 8)).start)

            yield go

    def slice_pushes():
        neighbour = place.device(1 - x, cube)

        def give_out():
            src, dst = wout_src.at[0], wout.at[x]
            pl.when(x == cube)(local_copy(src, dst, wown.at[2, x, 0]).start)
            pl.when(x != cube)(remote(src, dst, wsend.at[2], wown.at[2, x, 0], neighbour).start)

        def give_down():
            for side in range(2):
                src = wdn_src.at[0, pl.ds(side * 128, 128)]
                dst = wdn.at[x, rows_at(cube, 128)]
                pl.when(x == side)(local_copy(src, dst, wown.at[3, x, 0]).start)
                pl.when(x != side)(remote(src, dst, wsend.at[3], wown.at[3, x, 0], neighbour).start)

        return give_out, give_down

    def prefix_out():
        for side, index in ((x, 0), (1 - x, 1)):
            for kind, src_all in ((0, pk_src), (1, pv_src)):
                src = src_all.at[0, :, rows_at(side * 4 + place.zl * 2 + place.y, 128)]
                dst = pre.at[x, kind]
                if index == 0:
                    yield local_copy(src, dst, psem.at[0, kind])
                else:
                    yield remote(src, dst, psem.at[1, kind], psem.at[2, kind], place.device(1 - x, cube))

    def slice_ref(kind, l, zhi):
        if kind < 2:
            return (wqkv, wup)[kind].at[rows_at(l * 2 + zhi, half_rows)]
        if kind == 3:
            return wdn.at[l, rows_at(zhi, 128)]
        return wout.at[l]

    def to_twin(ref, kind, l):
        return remote(ref, ref, wrelay.at[kind, l], wtwin.at[kind, l], place.twin())

    def relay_blocks(kind, l):
        def one(i, carry):
            k = lax.rem(jnp.where(x == l, tau, 0) + 7 - i, 8)
            ref = (wqkv, wup)[kind].at[rows_at((l * 2 + cube) * 8 + k, ROWS)]
            bytes_of(ref, wown.at[kind, l, k]).wait()
            to_twin(ref, kind, l).start()
            return carry

        lax.fori_loop(0, 8, one, 0)

    def relay_out(l):
        @pl.when(x == cube)
        def _():
            bytes_of(wout.at[l], wown.at[2, l, 0]).wait()
            to_twin(wout.at[l], 2, l).start()

    def relay_down(l):
        dn = slice_ref(3, l, cube)
        bytes_of(dn, wown.at[3, l, 0]).wait()
        to_twin(dn, 3, l).start()

    def weights_in(kind, l):
        wait = bytes_of(slice_ref(kind, l, 1 - cube), wtwin.at[kind, l]).wait
        if kind == 2:
            pl.when(x != cube)(wait)
        else:
            wait()

    def weights_drain():
        for kind, ref in ((0, pack_qkv), (1, pack_up)):
            bytes_of(ref.at[pl.ds(0, 15)], wsend.at[kind]).wait()
        bytes_of(wdn.at[0, pl.ds(0, 128)], wsend.at[3]).wait()
        pl.when(x != cube)(bytes_of(wout.at[0], wsend.at[2]).wait)
        for l in range(2):
            for kind in (0, 1, 3):
                to_twin(slice_ref(kind, l, cube), kind, l).wait_send()
            pl.when(x == cube)(to_twin(wout.at[l], 2, l).wait_send)

    def weight(ref, l):
        return ref[rows_at(l, 16 * ROWS)]

    def own_half(pair):
        return jnp.where(core == 0, pair[:, :64], pair[:, 64:])

    def gather(buf, phase):
        return Gather(place, buf, ag_recv.at[phase], ag_sib.at[phase], ag_send)

    def scatter(phase):
        boxes = phase % 2
        return Scatter(
            place, rs_recv.at[phase], rs_send, half, keep, sib_out, sib_in.at[boxes], rs_out, inbox.at[boxes],
        )

    prefixes = list(prefix_out())
    for copy in prefixes:
        copy.start()

    @pl.when(x == 0)
    def _():
        for start in spread_pushes(0):
            start()

    rowacc[...] = jnp.zeros_like(rowacc)
    biasacc[...] = jnp.zeros_like(biasacc)
    dqt[64:128] = jnp.zeros((64, tokens), F32)
    along = lax.broadcasted_iota(jnp.int32, (8, tokens), 1)
    down = lax.broadcasted_iota(jnp.int32, (tokens, 128), 0)
    segment_q, segment_k = jnp.zeros((8, tokens), jnp.int32), jnp.zeros((tokens, 128), jnp.int32)
    end = jnp.int32(0)
    for j in range(lengths.shape[1]):
        end = end + lengths[cube, j]
        segment_q = segment_q + (along >= end).astype(jnp.int32)
        segment_k = segment_k + (down >= end).astype(jnp.int32)
    qseg[...] = segment_q
    kseg[0:tokens] = segment_k
    kseg[tokens:] = jnp.full((kseg.shape[0] - tokens, 128), -1, jnp.int32)

    relay_blocks(0, 0)
    x_arrived()

    def result_out(stage, out, kind, layer):
        dst = out.at[cube]
        is_self = (layer == x) & (x == cube)
        here = local_copy(stage, dst, orecv.at[kind, cube])
        there = remote(stage, dst, osend.at[kind, layer], orecv.at[kind, cube], place.device(layer, x))
        return is_self, here, there

    def visible(cols):
        key_part = kseg[...]
        keys_two = jnp.concatenate([key_part, key_part], axis=1)
        return (keys_two == qseg[0:1, cols]) | (keys_two < 0)

    def forward_layer(l, carry):
        gather_x = gather(xg.at[l], AG_X)
        gather_x.start()

        @pl.when(l == 0)
        def _():
            def first_layer(start):
                return lambda: pl.when(x == 0)(start)

            give_out, give_down = slice_pushes()
            gather_x.pump.add([first_layer(start) for start in (give_out, *spread_pushes(1), give_down)])
            gather_x.stage(0)
            gather_x.pump.go(1)
            relay_out(0)
            gather_x.stage(1)
            gather_x.pump.go(len(gather_x.pump.waiting))
            relay_blocks(1, 0)
            gather_x.stage(2)
            relay_down(0)
            d_start()
            for copy in prefixes[:2]:
                copy.wait()
            for copy in prefixes[2:]:
                copy.wait()

        weights_in(0, l)
        tail = wqkv[rows_at(l, 16 * ROWS), 128:256].astype(F32).T
        param[l] = tail[64:80]
        biases = own_half(param[l, 0:8, rows_at(tau // 2, 128)])[6:8]
        empty = jnp.zeros((1, 64), F32)
        qkv_bias = jnp.concatenate([biases[0:1], empty, biases[1:2], empty], axis=1)
        prefix = jnp.concatenate(
            [own_half(pre[l, 0].astype(F32)), own_half(pre[l, 1].astype(F32))], axis=1
        )
        ks[l, tokens:] = prefix[:, :64].astype(BF16)
        vs[l, tokens:] = prefix[:, 64:].astype(BF16)
        prefix_t = prefix.T
        kt[l, :, tokens:] = prefix_t[:64].astype(BF16)
        vt[l, :, tokens:] = prefix_t[64:].astype(BF16)

        for i, j in enumerate(gather_x.order):
            if i < 3:
                @pl.when(l == 1)
                def _():
                    gather_x.stage(i)

            gather_x.pair_ready(j)
            rows = place.pair_rows(j)
            value = mm(xg[l, rows], weight(wqkv, l)) + qkv_bias
            qs[l, rows] = (value[:, :64] * 0.125).astype(BF16)
            ks[l, rows] = value[:, 64:128].astype(BF16)
            vs[l, rows] = value[:, 128:192].astype(BF16)
            value_t = value.T
            kt[l, :, rows] = value_t[64:128].astype(BF16)
            vt[l, :, rows] = value_t[128:192].astype(BF16)
        gather_x.drain()

        def second_layer(start):
            return lambda: pl.when((l == 0) & (x == 1))(start)

        give_out, give_down = slice_pushes()
        scatter_o = scatter(RS_O)
        scatter_o.pump = Pump(5)
        scatter_o.pump.add(
            [second_layer(start) for start in (*spread_pushes(0), give_out, give_down, *spread_pushes(1))]
        )

        def attend(j):
            cols = place.pair_rows(j)
            scores = jnp.where(visible(cols), mm_nt(ks[l], qs[l, cols]), NEGATIVE)
            top = jnp.max(scores, axis=0, keepdims=True)
            grown = jnp.exp(scores - top)
            total = jnp.sum(grown, axis=0, keepdims=True)
            probs = (grown * (1.0 / total)).astype(BF16)
            lse[l, 0:1, cols] = top + jnp.log(total)
            context_t = mm(vt[l], probs)
            ctf[l, :, cols] = context_t
            low = context_t.astype(BF16)
            ctb[l, :, cols] = low
            return mm_tn(low, wout[l])

        pl.when(l == 0)(lambda: weights_in(2, 0))
        pl.when(l == 1)(lambda: weights_in(2, 1))
        scatter_o.run(attend)
        scatter_o.pump.go(len(scatter_o.pump.waiting))
        attended = scatter_o.finish() + param[l, 0:1]
        normal = norm_forward(
            xg[l, own_rows].astype(F32) + attended,
            param[l, 1:2], param[l, 2:3], hat1.at[l], rstd1.at[l],
        )
        own_a[...] = normal
        ng[l, own_rows] = normal.astype(BF16)
        gather_n = gather(ng.at[l], AG_N)
        gather_n.start()

        @pl.when(l == 0)
        def _():
            relay_blocks(0, 1)

        weights_in(1, l)
        weights_in(3, l)
        up_part = own_half(param[l, 8:16, rows_at(place.zl * 2 + place.y, 128)])
        up_more = own_half(param[l, 8:16, rows_at(4 + place.zl * 2 + place.y, 128)])
        up_parts = jnp.where(x == 0, up_part[0:2], up_part[2:4])
        up_more = jnp.where(x == 0, up_more[0:2], up_more[2:4])
        up_bias = jnp.concatenate([up_parts[0:1], up_parts[1:2], up_more[0:1], up_more[1:2]], axis=1)
        scatter_z = scatter(RS_Z)

        def feed_block(j, before):
            rows = place.pair_rows(j)
            value = mm(ng[l, rows], weight(wup, l)) + up_bias
            cdf = 0.5 * (1.0 + lax.erf(value * SQRT_HALF))
            low = (value * cdf).astype(BF16)
            act[l, rows] = low
            dact[l, rows] = cdf + value * (jnp.exp(-0.5 * value * value) * INV_SQRT_2PI)
            scatter_z.give(j, mm(low, wdn[l]))
            if j == 1:
                scatter_z.forward(5)

        gather_n.blocks(feed_block)
        scatter_z.rest()

        @pl.when(l == 0)
        def _():
            relay_out(1)
            relay_blocks(1, 1)
            relay_down(1)

        mixed = scatter_z.finish() + param[l, 3:4]
        result = norm_forward(
            own_a[...] + mixed, param[l, 4:5], param[l, 5:6], hat2.at[l], rstd2.at[l]
        ).astype(BF16)
        ystage[l] = result

        @pl.when(l == 0)
        def _():
            xg[1, own_rows] = result

        is_self, here, there = result_out(ystage.at[l], out_y, 0, l)
        pl.when(is_self)(here.start)
        pl.when(jnp.logical_not(is_self))(there.start)
        return carry

    lax.fori_loop(0, 2, forward_layer, 0)

    d_arrived()

    other_half, this_half = 1 - cube, cube

    def twin_parts(kind, l):
        if kind == 0:
            return g_qkv.at[l, rows_at(other_half, half_rows)], t_qkv, g_qkv.at[l, rows_at(this_half, half_rows)]
        if kind == 1:
            return g_up.at[l, rows_at(other_half, half_rows)], t_up, g_up.at[l, rows_at(this_half, half_rows)]
        if kind == 2:
            return g_prefix.at[l, rows_at(other_half, 32)], t_prefix, g_prefix.at[l, rows_at(this_half, 32)]
        if kind == 3:
            return g_dn.at[l, rows_at(other_half, 128)], t_dn, g_dn.at[l, rows_at(this_half, 128)]
        return g_out.at[l], t_out, g_out.at[l]

    def twin_send(kind, l):
        src, box, own = twin_parts(kind, l)
        return remote(src, box.at[l], tsend.at[kind, l], trecv.at[kind, l], place.twin())

    def twin_chunks(kind, l):
        src, box, own = twin_parts(kind, l)
        rows = ROWS if kind < 2 else 16
        for k in range(src.shape[0] // rows):
            part = pl.ds(k * rows, rows)
            yield remote(
                src.at[part], box.at[l, part], tsend.at[kind, l], trecv.at[kind, l], place.twin()
            ).start

    def twin_start(kind, l):
        copy = twin_send(kind, l)
        if kind == 4:
            pl.when(x != cube)(copy.start)
        else:
            copy.start()

    def owner_pushes(kind, l):
        src, box, own = twin_parts(kind, l)
        mine = x == l

        def start(is_self, part, dst, dev, condition=None):
            def go():
                pl.when(is_self)(local_copy(part, dst, grecv.at[kind]).start)
                pl.when(jnp.logical_not(is_self))(
                    remote(part, dst, gsend.at[kind, l], grecv.at[kind], dev).start
                )

            return go if condition is None else lambda: pl.when(condition)(go)

        if kind < 2:
            got = (got_qkv, got_up)[kind]
            for k in range(8):
                to = lax.rem(k + t + 1, 8)
                yield start(mine & (to == t % 8), own.at[rows_at(to, ROWS)], got.at[tau], (l, cube * 8 + to))
        elif kind == 2:
            for k in range(16):
                to = lax.rem(k + t + 1, 16)
                yield start(mine & (to == t), own, got_prefix.at[tau, rows_at(this_half, 32)], (l, to))
        elif kind == 3:
            yield start(mine, own, got_dn.at[rows_at(x, 128)], place.device(l, cube))
        else:
            yield start(mine, own, got_out, place.device(l, cube), x == cube)

    def owner_add(kind, l):
        src, box, own = twin_parts(kind, l)

        def add():
            twin_send(kind, l).wait_recv()
            own[...] = (own[...].astype(F32) + box[l].astype(F32)).astype(BF16)

        if kind == 4:
            pl.when(x == cube)(add)
        else:
            add()

    def owner_start(kind, l):
        owner_add(kind, l)
        for start in owner_pushes(kind, l):
            start()

    def grads_drain(l):
        for kind in range(5):
            if kind == 4:
                pl.when(x != cube)(twin_send(kind, l).wait_send)
            else:
                twin_send(kind, l).wait_send()
        for kind, ref in ((0, got_qkv), (1, got_up)):
            pl.when(x == l)(bytes_of(ref.at[pl.ds(0, 7)], gsend.at[kind, l]).wait)
            pl.when(x != l)(bytes_of(ref.at[pl.ds(0, 8)], gsend.at[kind, l]).wait)
        for count, condition in ((15, x == l), (16, x != l)):
            pl.when(condition)(bytes_of(got_prefix.at[pl.ds(0, count), pl.ds(0, 32)], gsend.at[2, l]).wait)
            pl.when(condition)(bytes_of(got_rows.at[pl.ds(0, count)], gsend.at[5, l]).wait)
        pl.when(x != l)(bytes_of(g_dn.at[0, pl.ds(0, 128)], gsend.at[3, l]).wait)
        pl.when((x != l) & (x == cube))(bytes_of(g_out.at[0], gsend.at[4, l]).wait)
        for to, src, dst in bias_pairs(l):
            is_self = (x == l) & (cube == to)
            pl.when(jnp.logical_not(is_self))(bytes_of(src, gsend.at[6 + to, l]).wait)

    def rows_start(l):
        def one(k, carry):
            to = lax.rem(k + t + 1, 16)
            src, dst = rowacc.at[l, :, rows_at(to // 2, 128)], got_rows.at[cube * 16 + tau]
            is_self = (x == l) & (to == t)
            pl.when(is_self)(local_copy(src, dst, grecv.at[5]).start)
            pl.when(jnp.logical_not(is_self))(remote(src, dst, gsend.at[5, l], grecv.at[5], (l, to)).start)
            return carry

        lax.fori_loop(0, 16, one, 0)

    def bias_pairs(l):
        for to in range(2):
            yield to, biasacc.at[l], got_bias.at[cube * 2 + x]

    def bias_start(l):
        for to, src, dst in bias_pairs(l):
            is_self = (x == l) & (cube == to)
            pl.when(is_self)(local_copy(src, dst, grecv.at[6]).start)
            pl.when(jnp.logical_not(is_self))(
                remote(src, dst, gsend.at[6 + to, l], grecv.at[6], place.device(l, to)).start
            )

    def backward_layer(step, carry):
        l = 1 - step
        upstream = dstage[l + 1].astype(F32)
        d_sum, d_gain, d_shift = norm_backward(upstream, param[l, 4:5], hat2.at[l], rstd2.at[l])
        own_b[...] = d_sum
        low = d_sum.astype(BF16)
        dzg[own_rows] = low
        gather_z = gather(dzg, AG_Z)
        gather_z.start()
        rowacc[l, 3:4] = d_gain
        rowacc[l, 4:5] = d_shift
        rowacc[l, 5:6] = column_sum(low)
        scatter_n = scatter(RS_N)

        def back_block(j, before):
            rows = place.pair_rows(j)
            low = (dact[l, rows] * mm_nt(dzg[rows], wdn[l])).astype(BF16)
            dfs[rows] = low
            scatter_n.give(j, mm_nt(low, weight(wup, l)))
            if j == 1:
                scatter_n.forward(5)

        gather_z.blocks(back_block)
        scatter_n.rest()
        biasacc[l, 1:2] = column_sum(dfs[...])

        def down_tile(i, carry):
            cols = rows_at(i, 256)
            g_dn[l, :, cols] = mm_tn(act[l], dzg[:, cols]).astype(BF16)
            return carry

        lax.fori_loop(0, width // 256, down_tile, 0)

        def up_tile(i, carry):
            cols = rows_at(i, 256)
            g_up[l, cols] = mm_tn(ng[l, :, cols], dfs[...]).astype(BF16)
            return carry

        lax.fori_loop(0, width // 256, up_tile, 0)
        @pl.when(l == 0)
        def _():
            for kind in (3, 1, 2, 4, 0):
                owner_add(kind, 1)

        def older(start):
            return lambda: pl.when(l == 0)(start)

        pump = Pump(1)
        twins = [*twin_chunks(3, l), *twin_chunks(1, l)]
        olds = [older(start) for kind in (3, 1, 4, 0, 2) for start in owner_pushes(kind, 1)]
        for k in range(17):
            pump.add(twins[k : k + 1] + olds[2 * k : 2 * k + 2])
        pump.go(3)

        d_normal = own_b[...] + scatter_n.finish()
        d_sum, d_gain, d_shift = norm_backward(d_normal, param[l, 1:2], hat1.at[l], rstd1.at[l])
        own_a[...] = d_sum
        low = d_sum.astype(BF16)
        dog[own_rows] = low
        gather_o = gather(dog, AG_O)
        gather_o.pump = pump
        gather_o.start()
        rowacc[l, 0:1] = d_gain
        rowacc[l, 1:2] = d_shift
        rowacc[l, 2:3] = column_sum(low)
        rows_start(l)


        dkacc[...] = jnp.zeros_like(dkacc)
        dvacc[...] = jnp.zeros_like(dvacc)

        def attend_back(j, before):
            cols = place.pair_rows(j)
            d_context = mm_nt(dog[cols], wout[l]).astype(BF16)
            dcb[cols] = d_context
            d_context_t = mm_nt(wout[l], dog[cols]).astype(BF16).astype(F32)
            sums = jnp.sum(d_context_t * ctf[l, :, cols], axis=0, keepdims=True)
            scores = jnp.where(visible(cols), mm_nt(ks[l], qs[l, cols]), NEGATIVE)
            probs = jnp.exp(scores - lse[l, 0:1, cols])
            d_probs = mm_nt(vs[l], d_context)
            d_scores = (probs * (d_probs - sums)).astype(BF16)
            dvacc[...] += mm(probs.astype(BF16), d_context)
            dkacc[...] += mm(d_scores, qs[l, cols])
            dqt[0:64, cols] = mm(kt[l], d_scores) * 0.125
            pump.go(3)

        gather_o.blocks(attend_back)
        g_prefix[l] = jnp.concatenate([dkacc[tokens:], dvacc[tokens:]], axis=1).astype(BF16)
        twin_start(2, l)
        g_out[l] = mm(ctb[l], dog[...]).astype(BF16)
        twin_start(4, l)

        def assemble(i, carry):
            rows = rows_at(i, BLOCK)
            d_query = dqt[:, rows].T[:, :64]
            value = jnp.concatenate(
                [d_query, dkacc[rows], dvacc[rows], jnp.zeros((BLOCK, 64), F32)], axis=1
            )
            dqkv[rows] = value.astype(BF16)
            dqkvt[:, rows] = value.T.astype(BF16)
            return carry

        lax.fori_loop(0, tokens // BLOCK, assemble, 0)

        def qkv_tile(i, carry):
            cols = rows_at(i, 256)
            g_qkv[l, cols] = mm(dqkvt[...], xg[l, :, cols]).T.astype(BF16)
            return carry

        lax.fori_loop(other_half * 2, other_half * 2 + 2, qkv_tile, 0)
        pump.add(list(twin_chunks(0, l)))
        pump.go(2)
        scatter_x = scatter(RS_X)
        scatter_x.pump = pump
        pump.rate = 2
        scatter_x.run(lambda j: mm_nt(dqkv[place.pair_rows(j)], weight(wqkv, l)))
        biasacc[l, 0:1, 0:256] = column_sum(dqkv[...])
        bias_start(l)
        lax.fori_loop(this_half * 2, this_half * 2 + 2, qkv_tile, 0)
        pump.go(len(pump.waiting))

        @pl.when(l == 0)
        def _():
            for kind in (3, 1):
                owner_start(kind, 0)

        dstage[l] = (own_a[...] + scatter_x.finish()).astype(BF16)
        is_self, here, there = result_out(dstage.at[l], out_dx, 1, l)
        pl.when(is_self)(here.start)
        pl.when(jnp.logical_not(is_self))(there.start)
        return carry

    lax.fori_loop(0, 2, backward_layer, 0)
    for kind in (2, 4, 0):
        owner_start(kind, 0)

    x_sent()
    d_sent()
    weights_drain()
    for l in range(2):
        grads_drain(l)
        for kind, stage, out in ((0, ystage.at[l], out_y), (1, dstage.at[l], out_dx)):
            is_self, here, there = result_out(stage, out, kind, l)
            pl.when(jnp.logical_not(is_self))(there.wait_send)
    for kind, out in ((0, out_y), (1, out_dx)):
        for m in range(2):
            bytes_of(out.at[m], orecv.at[kind, m]).wait()

    def landed(kind):
        ref = (got_qkv, got_up, got_prefix, got_dn, got_out, got_rows, got_bias)[kind]
        bytes_of(ref, grecv.at[kind]).wait()

    landed(3)
    out_dn[0] = got_dn[...].astype(F32)
    landed(1)
    for side in range(2):
        for rest in range(8):
            for zhi in range(2):
                start = (zhi * 8 + rest) * 256 + side * 128
                part = got_up[side * 8 + rest, :, zhi * 128 : (zhi + 1) * 128]
                out_up[0, :, start : start + 128] = part.astype(F32)
    landed(4)
    out_o[0] = got_out[...].astype(F32)

    def heads_together(got, outs):
        for h in range(8):
            pair = [got[2 * h].astype(F32), got[2 * h + 1].astype(F32)]
            for i, out in enumerate(outs):
                sides = [value[:, i * 64 : (i + 1) * 64] for value in pair]
                out[0, :, h * 128 : (h + 1) * 128] = jnp.concatenate(sides, axis=1)

    landed(2)
    heads_together(got_prefix, (out_pk, out_pv))
    landed(0)
    heads_together(got_qkv, (out_q, out_k, out_v))
    landed(5)
    landed(6)


def cube_local(
    inputs, cotangent, lengths, prefix_keys, prefix_values,
    w_query, b_query, w_key, w_value, b_value, w_out, b_out, norm1_gain, norm1_shift,
    w_up, b_up, w_down, b_down, norm2_gain, norm2_shift,
):
    t = lax.axis_index("tok")
    rows, width = w_query.shape[1], w_query.shape[2]
    heads = width // HEAD
    tokens = inputs.shape[1] * lax.axis_size("tok")
    prefix = prefix_keys.shape[1]
    keys = tokens + prefix
    hidden = b_up.shape[1]

    anywhere = pl.BlockSpec(memory_space=pl.ANY)
    smem = pl.BlockSpec(memory_space=pltpu.SMEM)
    dma = pltpu.SemaphoreType.DMA
    V = pltpu.VMEM
    L = 2
    shape = jax.ShapeDtypeStruct
    results = pl.pallas_call(
        kernel,
        out_shape=(
            shape((2, ROWS, width), BF16), shape((2, ROWS, width), BF16),
            shape((1, rows, width), F32), shape((1, rows, width), F32), shape((1, rows, width), F32),
            shape((1, rows, width), F32), shape((1, rows, 4 * width), F32), shape((1, hidden, width), F32),
            shape((1, prefix, width), F32), shape((1, prefix, width), F32),
            shape((32, 8, 128), F32), shape((4, 8, hidden), F32),
        ),
        in_specs=[smem] + [anywhere] * 19,
        out_specs=[anywhere] * 2 + [pl.BlockSpec(memory_space=pltpu.VMEM)] * 8 + [anywhere] * 2,
        scratch_shapes=[
            dma((4, 8, PIECES)), dma((4, 8, PIECES)), dma((3, 8, PIECES)), dma((4, 2, 8)), dma((2, 8)),
            dma((4,)), dma((4, 2, 8)), dma((4, 2)), dma((4, 2)), dma((3, 2)), dma((8,)),
            dma((2, 2)), dma((2, 2)), dma((5, 2)), dma((5, 2)), dma((8, 2)), dma((7,)), dma((13,)),
            V((3, rows, width), BF16), V((rows, 4 * width), BF16), V((heads, rows, 256), BF16), V((heads, rows, 256), BF16),
            V((64, 128), F32),
            *[V((1, rows), BF16)] * 8, V((1, hidden), BF16),
            V((L * 1024, 256), BF16), V((L * 1024, 256), BF16), V((L, hidden, width), BF16),
            V((L, ROWS, width), BF16), V((L, 2, prefix, 128), BF16),
            V((8, tokens), jnp.int32), V((keys, 128), jnp.int32),
            V((L, tokens, width), BF16), V((L, tokens, width), BF16),
            V((tokens, width), BF16), V((tokens, width), BF16), V((L, 16, width), F32),
            V((L, tokens, HEAD), BF16), V((L, keys, HEAD), BF16), V((L, keys, HEAD), BF16),
            V((L, HEAD, keys), BF16), V((L, HEAD, keys), BF16),
            V((L, 8, tokens), F32), V((L, HEAD, tokens), BF16), V((L, HEAD, tokens), F32),
            V((L, ROWS, width), F32), V((L, ROWS, 128), F32), V((L, ROWS, width), F32), V((L, ROWS, 128), F32),
            V((L, tokens, hidden), BF16), V((L, tokens, hidden), F32),
            V((4, ROWS, width), F32), V((8, ROWS, width), F32), V((8, ROWS, width), BF16),
            V((2, 8, ROWS, width), BF16), V((8, ROWS, width), BF16), V((2, 8, ROWS, width), BF16),
            V((ROWS, width), F32), V((ROWS, width), F32), V((L, ROWS, width), BF16), V((L + 1, ROWS, width), BF16),
            V((tokens, hidden), BF16), V((tokens, HEAD), BF16), V((8, tokens), F32), V((128, tokens), F32),
            V((keys, HEAD), F32), V((keys, HEAD), F32), V((tokens, 256), BF16), V((256, tokens), BF16),
            V((L, 8, width), F32), V((L, 8, hidden), F32),
            V((L, width, 256), BF16), V((L, width, hidden), BF16), V((L, hidden, width), BF16),
            V((L, ROWS, width), BF16), V((L, prefix, 128), BF16),
            V((L, width // 2, 256), BF16), V((L, width // 2, 256), BF16), V((L, hidden // 2, width), BF16),
            V((L, ROWS, width), BF16), V((L, prefix // 2, 128), BF16),
            V((16, ROWS, 256), BF16), V((16, ROWS, 256), BF16), V((hidden, width), BF16), V((ROWS, width), BF16),
            V((16, prefix, 128), BF16),
        ],
        compiler_params=pltpu.CompilerParams(
            collective_id=0, has_side_effects=True, vmem_limit_bytes=60 * 2**20
        ),
    )(
        lengths, inputs, cotangent, w_query, w_key, w_value, w_up, w_down, w_out, prefix_keys, prefix_values,
        b_out, norm1_gain, norm1_shift, b_down, norm2_gain, norm2_shift, b_query, b_value, b_up,
    )
    out_y, out_dx, out_q, out_k, out_v, out_o, out_up, out_dn, out_pk, out_pv, got_rows, got_bias = results
    row_sum = lax.dynamic_slice_in_dim(jnp.sum(got_rows, axis=0), (t % 2) * 64, 64, 1)
    side = t // 8
    bias_up = (got_bias[:2, 1] + got_bias[2:, 1]).reshape(2, 2, 128)
    bias_up = lax.dynamic_index_in_dim(bias_up, side, 1, keepdims=False).reshape(1, hidden)
    bias_qkv = lax.dynamic_index_in_dim(got_bias[:2, 0] + got_bias[2:, 0], side, 0, keepdims=True)
    return (
        out_y[None],
        out_dx[None],
        out_q,
        bias_qkv[:, 0:64],
        out_k,
        out_v,
        bias_qkv[:, 128:192],
        out_o,
        row_sum[2:3],
        row_sum[0:1],
        row_sum[1:2],
        out_up,
        bias_up,
        out_dn,
        row_sum[5:6],
        row_sum[3:4],
        row_sum[4:5],
        out_pk,
        out_pv,
    )


def solution(mesh):
    placed = (
        P(None, "tok", None),
        P(None, "tok", None),
        P(),
        P("section", None, None),
        P("section", None, None),
        P("section", "tok", None),
        P("section", "tok"),
        P("section", "tok", None),
        P("section", "tok", None),
        P("section", "tok"),
        P("section", "tok", None),
        P("section", "tok"),
        P("section", "tok"),
        P("section", "tok"),
        P("section", "tok", None),
        P("section", "tok"),
        P("section", "tok", None),
        P("section", "tok"),
        P("section", "tok"),
        P("section", "tok"),
    )
    return jax.shard_map(
        cube_local if mesh.shape["tok"] == HEADS else local,
        mesh=mesh,
        in_specs=placed,
        out_specs=(
            P("section", None, "tok", None),
            P("section", None, "tok", None),
            P("section", "tok", None),
            P("section", "tok"),
            P("section", "tok", None),
            P("section", "tok", None),
            P("section", "tok"),
            P("section", "tok", None),
            P("section", "tok"),
            P("section", "tok"),
            P("section", "tok"),
            P("section", "tok", None),
            P("section", "tok"),
            P("section", "tok", None),
            P("section", "tok"),
            P("section", "tok"),
            P("section", "tok"),
            P("section", None, None),
            P("section", None, None),
        ),
        check_vma=False,
    )
```

```python
import jax
import jax.numpy as jnp
from jax import lax
from jax.experimental import pallas as pl
from jax.experimental.pallas import tpu as pltpu
from jax.sharding import PartitionSpec as P

HEADS = 16
HEAD = 64


NEGATIVE = -1e30


def from_behind(block, axis, distance):
    devices = range(lax.axis_size(axis))
    route = [(i - distance, i) for i in devices if i - distance in devices]
    return lax.ppermute(block, axis, route)


def segment_of(lengths_row, positions):
    ends = jnp.cumsum(lengths_row, dtype=jnp.int32)
    return jnp.sum((positions[:, None] >= ends[None, :]).astype(jnp.int32), axis=1, dtype=jnp.int32)


def normalize(value, gain, shift):
    centred = value - jnp.mean(value, axis=-1, keepdims=True)
    spread = jnp.mean(centred * centred, axis=-1, keepdims=True)
    return centred * lax.rsqrt(spread + 1e-05) * gain + shift


def gelu_exact(value):
    return jax.nn.gelu(value, approximate=False)


def project(left, right):
    return jnp.dot(left, right, preferred_element_type=jnp.float32)


def project_back(left, weight):
    return jnp.einsum("tf,df->td", left, weight, preferred_element_type=jnp.float32)


def contract_rows(left, right):
    return jnp.einsum("tf,td->fd", left, right, preferred_element_type=jnp.float32)


def split_heads(value):
    return value.reshape(value.shape[0], HEADS, HEAD)


def in_blocks(step_fn, running, arrays, offset_row):
    total_rows = arrays[0].shape[0]
    block_rows = 1024 if total_rows > 1024 and total_rows % 1024 == 0 else total_rows
    if block_rows == total_rows:
        return step_fn(running, arrays, offset_row)
    stacked = tuple(
        (
            member.reshape((total_rows // block_rows, block_rows) + member.shape[1:])
            for member in arrays
        )
    )
    offsets = offset_row + block_rows * jnp.arange(total_rows // block_rows, dtype=jnp.int32)

    def scan_step(inner, packet):
        return (step_fn(inner, packet[0], packet[1]), None)

    result, unused = lax.scan(scan_step, running, (stacked, offsets))
    return result


def masked_scores(query_part, key_part, query_segment, key_segment):
    raw_scores = jnp.einsum(
        "qhe,khe->hqk",
        split_heads(query_part),
        split_heads(key_part),
        preferred_element_type=jnp.float32,
    ) * HEAD ** (-0.5)
    return jnp.where((query_segment[:, None] == key_segment[None, :])[None], raw_scores, NEGATIVE)


def prefix_scores(queries, prefix_key_rows):
    return jnp.einsum(
        "qhe,khe->hqk",
        split_heads(queries),
        split_heads(prefix_key_rows),
        preferred_element_type=jnp.float32,
    ) * HEAD ** (-0.5)


def gather_weights(shards):
    return (
        lax.all_gather(shards[0], "tok", axis=1, tiled=True),
        lax.all_gather(shards[1], "tok", axis=1, tiled=True),
        lax.all_gather(shards[2], "tok", axis=1, tiled=True),
        lax.all_gather(shards[3], "tok", axis=1, tiled=True),
        lax.all_gather(shards[4], "tok", axis=1, tiled=True),
        lax.all_gather(shards[5], "tok", axis=1, tiled=True),
        lax.all_gather(shards[6], "tok", axis=1, tiled=True),
        lax.all_gather(shards[7], "tok", axis=1, tiled=True),
        lax.all_gather(shards[8], "tok", axis=1, tiled=True),
        lax.all_gather(shards[9], "tok", axis=1, tiled=True),
        lax.all_gather(shards[10], "tok", axis=1, tiled=True),
        lax.all_gather(shards[11], "tok", axis=1, tiled=True),
        lax.all_gather(shards[12], "tok", axis=1, tiled=True),
        lax.all_gather(shards[13], "tok", axis=1, tiled=True),
        lax.all_gather(shards[14], "tok", axis=1, tiled=True),
    )


def front_part(inbound, weights):
    queries = (project(inbound, weights[0]) + weights[1].astype(jnp.float32)).astype(jnp.bfloat16)
    key_rows = project(inbound, weights[2]).astype(jnp.bfloat16)
    value_rows = (project(inbound, weights[3]) + weights[4].astype(jnp.float32)).astype(
        jnp.bfloat16
    )
    return (queries, key_rows, value_rows)


def attention_forward(
    queries, key_rows, value_rows, prefix_key_rows, prefix_value_rows, lengths_row, own_segment
):
    first_scores = prefix_scores(queries, prefix_key_rows)
    highest = jnp.max(first_scores, axis=2)
    denominator = jnp.sum(jnp.exp(first_scores - highest[..., None]), axis=2)

    def total_block(state, piece, offset_row):
        old_high, old_denominator = state
        key_part = piece[0]
        key_segment = segment_of(
            lengths_row, offset_row + jnp.arange(key_part.shape[0], dtype=jnp.int32)
        )
        raw_scores = masked_scores(queries, key_part, own_segment, key_segment)
        new_high = jnp.maximum(old_high, jnp.max(raw_scores, axis=2))
        new_denominator = old_denominator * jnp.exp(old_high - new_high) + jnp.sum(
            jnp.exp(raw_scores - new_high[..., None]), axis=2
        )
        return (new_high, new_denominator)

    highest, denominator = in_blocks(
        total_block,
        (highest, denominator),
        (lax.all_gather(key_rows, "tok", axis=0, tiled=True),),
        jnp.int32(0),
    )
    logsum = highest + jnp.log(denominator)
    summed = jnp.einsum(
        "hqk,khe->qhe",
        jnp.exp(first_scores - logsum[..., None]).astype(jnp.bfloat16),
        split_heads(prefix_value_rows),
        preferred_element_type=jnp.float32,
    )

    def absorb_block(running, piece, offset_row):
        key_part, value_part = piece
        key_segment = segment_of(
            lengths_row, offset_row + jnp.arange(key_part.shape[0], dtype=jnp.int32)
        )
        probs_part = jnp.exp(
            masked_scores(queries, key_part, own_segment, key_segment) - logsum[..., None]
        )
        return running + jnp.einsum(
            "hqk,khe->qhe",
            probs_part.astype(jnp.bfloat16),
            split_heads(value_part),
            preferred_element_type=jnp.float32,
        )

    summed = in_blocks(
        absorb_block,
        summed,
        (
            lax.all_gather(key_rows, "tok", axis=0, tiled=True),
            lax.all_gather(value_rows, "tok", axis=0, tiled=True),
        ),
        jnp.int32(0),
    )
    context = summed.reshape(queries.shape[0], -1)
    return (context, logsum)


def back_part(inbound, context, weights):
    context_low = context.astype(jnp.bfloat16)
    attended = project(context_low, weights[5]) + weights[6].astype(jnp.float32)
    normal_one, pull_one = jax.vjp(
        normalize,
        inbound.astype(jnp.float32) + attended,
        weights[7].astype(jnp.float32),
        weights[8].astype(jnp.float32),
    )
    normal_one_low = normal_one.astype(jnp.bfloat16)
    activation, pull_gelu = jax.vjp(
        gelu_exact, project(normal_one_low, weights[9]) + weights[10].astype(jnp.float32)
    )
    activation_low = activation.astype(jnp.bfloat16)
    mixed = project(activation_low, weights[11]) + weights[12].astype(jnp.float32)
    result, pull_two = jax.vjp(
        normalize,
        normal_one + mixed,
        weights[13].astype(jnp.float32),
        weights[14].astype(jnp.float32),
    )
    return (result, context_low, normal_one_low, pull_one, activation_low, pull_gelu, pull_two)


def query_backward(
    queries,
    d_context,
    logsum,
    delta,
    prefix_key_rows,
    prefix_value_rows,
    key_rows,
    value_rows,
    lengths_row,
    own_segment,
):
    context_heads = split_heads(d_context)
    query_heads = split_heads(queries)
    prefix_prob = jnp.exp(prefix_scores(queries, prefix_key_rows) - logsum[..., None])
    prefix_dprob = jnp.einsum(
        "qhe,khe->hqk",
        context_heads,
        split_heads(prefix_value_rows),
        preferred_element_type=jnp.float32,
    )
    prefix_dscore = (prefix_prob * (prefix_dprob - delta[..., None])).astype(jnp.bfloat16)
    grad_prefix_keys = jnp.einsum(
        "hqk,qhe->khe", prefix_dscore, query_heads, preferred_element_type=jnp.float32
    ) * HEAD ** (-0.5)
    grad_prefix_values = jnp.einsum(
        "hqk,qhe->khe",
        prefix_prob.astype(jnp.bfloat16),
        context_heads,
        preferred_element_type=jnp.float32,
    )
    grad_start = jnp.einsum(
        "hqk,khe->qhe",
        prefix_dscore,
        split_heads(prefix_key_rows),
        preferred_element_type=jnp.float32,
    )

    def pull_block(running, piece, offset_row):
        key_part, value_part = piece
        key_segment = segment_of(
            lengths_row, offset_row + jnp.arange(key_part.shape[0], dtype=jnp.int32)
        )
        probs_part = jnp.exp(
            masked_scores(queries, key_part, own_segment, key_segment) - logsum[..., None]
        )
        dprob = jnp.einsum(
            "qhe,khe->hqk",
            context_heads,
            split_heads(value_part),
            preferred_element_type=jnp.float32,
        )
        dscore = (probs_part * (dprob - delta[..., None])).astype(jnp.bfloat16)
        return running + jnp.einsum(
            "hqk,khe->qhe", dscore, split_heads(key_part), preferred_element_type=jnp.float32
        )

    grad_queries = in_blocks(
        pull_block,
        grad_start,
        (
            lax.all_gather(key_rows, "tok", axis=0, tiled=True),
            lax.all_gather(value_rows, "tok", axis=0, tiled=True),
        ),
        jnp.int32(0),
    )
    row_count = queries.shape[0]
    return (
        (grad_queries * HEAD ** (-0.5)).reshape(row_count, -1),
        grad_prefix_keys.reshape(prefix_key_rows.shape),
        grad_prefix_values.reshape(prefix_value_rows.shape),
    )


def key_backward(queries, d_context, logsum, delta, key_rows, value_rows, lengths_row, own_segment):
    all_logsum, all_delta = (
        lax.all_gather(logsum, "tok", axis=1, tiled=True),
        lax.all_gather(delta, "tok", axis=1, tiled=True),
    )
    value_heads = split_heads(value_rows)

    def spread_block(running, piece, offset_row):
        grad_keys, grad_values = running
        query_part, context_part = piece
        part_rows = query_part.shape[0]
        part_logsum = lax.dynamic_slice_in_dim(all_logsum, offset_row, part_rows, 1)
        part_delta = lax.dynamic_slice_in_dim(all_delta, offset_row, part_rows, 1)
        part_segment = segment_of(lengths_row, offset_row + jnp.arange(part_rows, dtype=jnp.int32))
        probs_part = jnp.exp(
            masked_scores(query_part, key_rows, part_segment, own_segment) - part_logsum[..., None]
        )
        context_heads = split_heads(context_part)
        dprob = jnp.einsum(
            "qhe,khe->hqk", context_heads, value_heads, preferred_element_type=jnp.float32
        )
        dscore = (probs_part * (dprob - part_delta[..., None])).astype(jnp.bfloat16)
        new_keys = grad_keys + jnp.einsum(
            "hqk,qhe->khe", dscore, split_heads(query_part), preferred_element_type=jnp.float32
        )
        new_values = grad_values + jnp.einsum(
            "hqk,qhe->khe",
            probs_part.astype(jnp.bfloat16),
            context_heads,
            preferred_element_type=jnp.float32,
        )
        return (new_keys, new_values)

    def spread(running, piece, offset_row):
        return in_blocks(spread_block, running, piece, offset_row)

    empty = jnp.zeros((key_rows.shape[0], HEADS, HEAD), jnp.float32)
    grad_keys, grad_values = spread(
        (empty, empty),
        (
            lax.all_gather(queries, "tok", axis=0, tiled=True),
            lax.all_gather(d_context, "tok", axis=0, tiled=True),
        ),
        jnp.int32(0),
    )
    row_count = key_rows.shape[0]
    return ((grad_keys * HEAD ** (-0.5)).reshape(row_count, -1), grad_values.reshape(row_count, -1))


def layer_backward(
    inbound, upstream, weights, prefix_key_rows, prefix_value_rows, lengths_row, own_segment
):
    queries, key_rows, value_rows = front_part(inbound, weights)
    context, logsum = attention_forward(
        queries, key_rows, value_rows, prefix_key_rows, prefix_value_rows, lengths_row, own_segment
    )
    result, context_low, normal_one_low, pull_one, activation_low, pull_gelu, pull_two = back_part(
        inbound, context, weights
    )
    d_sum, d_gain_two, d_shift_two = pull_two(upstream.astype(jnp.float32))
    d_mixed = d_sum.astype(jnp.bfloat16)
    grad_down = contract_rows(activation_low, d_mixed)
    grad_down_bias = jnp.sum(d_mixed.astype(jnp.float32), axis=0)
    (d_pre,) = pull_gelu(project_back(d_mixed, weights[11]))
    d_pre_low = d_pre.astype(jnp.bfloat16)
    grad_up = contract_rows(normal_one_low, d_pre_low)
    grad_up_bias = jnp.sum(d_pre_low.astype(jnp.float32), axis=0)
    d_resid, d_gain_one, d_shift_one = pull_one(d_sum + project_back(d_pre_low, weights[9]))
    d_attended = d_resid.astype(jnp.bfloat16)
    grad_out = contract_rows(context_low, d_attended)
    grad_out_bias = jnp.sum(d_attended.astype(jnp.float32), axis=0)
    d_context = project_back(d_attended, weights[5]).astype(jnp.bfloat16)
    delta = jnp.sum(split_heads(d_context).astype(jnp.float32) * split_heads(context), axis=2).T
    grad_queries, grad_prefix_keys, grad_prefix_values = query_backward(
        queries,
        d_context,
        logsum,
        delta,
        prefix_key_rows,
        prefix_value_rows,
        key_rows,
        value_rows,
        lengths_row,
        own_segment,
    )
    grad_keys, grad_values = key_backward(
        queries, d_context, logsum, delta, key_rows, value_rows, lengths_row, own_segment
    )
    queries_low = grad_queries.astype(jnp.bfloat16)
    keys_low = grad_keys.astype(jnp.bfloat16)
    values_low = grad_values.astype(jnp.bfloat16)
    grad_query_weight = contract_rows(inbound, queries_low)
    grad_query_bias = jnp.sum(queries_low.astype(jnp.float32), axis=0)
    grad_key_weight = contract_rows(inbound, keys_low)
    grad_value_weight = contract_rows(inbound, values_low)
    grad_value_bias = jnp.sum(values_low.astype(jnp.float32), axis=0)
    d_input = (
        d_resid
        + project_back(queries_low, weights[0])
        + project_back(keys_low, weights[2])
        + project_back(values_low, weights[3])
    )
    grads = (
        grad_query_weight,
        grad_query_bias,
        grad_key_weight,
        grad_value_weight,
        grad_value_bias,
        grad_out,
        grad_out_bias,
        d_gain_one,
        d_shift_one,
        grad_up,
        grad_up_bias,
        grad_down,
        grad_down_bias,
        d_gain_two,
        d_shift_two,
    )
    return (d_input, grads, (grad_prefix_keys, grad_prefix_values))


def sum_each(grads):
    return (
        lax.psum_scatter(grads[0][None], "tok", scatter_dimension=1, tiled=True),
        lax.psum_scatter(grads[1][None], "tok", scatter_dimension=1, tiled=True),
        lax.psum_scatter(grads[2][None], "tok", scatter_dimension=1, tiled=True),
        lax.psum_scatter(grads[3][None], "tok", scatter_dimension=1, tiled=True),
        lax.psum_scatter(grads[4][None], "tok", scatter_dimension=1, tiled=True),
        lax.psum_scatter(grads[5][None], "tok", scatter_dimension=1, tiled=True),
        lax.psum_scatter(grads[6][None], "tok", scatter_dimension=1, tiled=True),
        lax.psum_scatter(grads[7][None], "tok", scatter_dimension=1, tiled=True),
        lax.psum_scatter(grads[8][None], "tok", scatter_dimension=1, tiled=True),
        lax.psum_scatter(grads[9][None], "tok", scatter_dimension=1, tiled=True),
        lax.psum_scatter(grads[10][None], "tok", scatter_dimension=1, tiled=True),
        lax.psum_scatter(grads[11][None], "tok", scatter_dimension=1, tiled=True),
        lax.psum_scatter(grads[12][None], "tok", scatter_dimension=1, tiled=True),
        lax.psum_scatter(grads[13][None], "tok", scatter_dimension=1, tiled=True),
        lax.psum_scatter(grads[14][None], "tok", scatter_dimension=1, tiled=True),
    )


def by_section(listing, is_first, early_first):
    stacked = jnp.stack(listing)
    window_count = len(listing) - 1
    if early_first:
        return jnp.where(is_first, stacked[:window_count], stacked[1:])
    return jnp.where(is_first, stacked[1:], stacked[:window_count])


def local(
    inputs,
    cotangent,
    lengths,
    prefix_keys,
    prefix_values,
    w_query,
    b_query,
    w_key,
    w_value,
    b_value,
    w_out,
    b_out,
    norm1_gain,
    norm1_shift,
    w_up,
    b_up,
    w_down,
    b_down,
    norm2_gain,
    norm2_shift,
):
    micro_count = inputs.shape[0]
    tok_rows = inputs.shape[1]
    model_width = inputs.shape[2]
    section_index = lax.axis_index("section")
    is_first = section_index == 0
    own_positions = lax.axis_index("tok") * tok_rows + jnp.arange(tok_rows, dtype=jnp.int32)
    shard_list = (
        w_query,
        b_query,
        w_key,
        w_value,
        b_value,
        w_out,
        b_out,
        norm1_gain,
        norm1_shift,
        w_up,
        b_up,
        w_down,
        b_down,
        norm2_gain,
        norm2_shift,
    )
    prefix_key_rows = prefix_keys[0]
    prefix_value_rows = prefix_values[0]
    weights = tuple((member[0] for member in gather_weights(shard_list)))
    received = jnp.zeros((tok_rows, model_width), jnp.bfloat16)
    seen_inputs = []
    seen_outputs = []
    seen_context = []
    seen_logsum = []
    for moment in range(micro_count + 1):
        current = jnp.clip(moment - section_index, 0, micro_count - 1)
        lengths_row = lengths[current]
        own_segment = segment_of(lengths_row, own_positions)
        inbound = jnp.where(is_first, inputs[min(moment, micro_count - 1)], received)
        queries, key_rows, value_rows = front_part(inbound, weights)
        context, logsum = attention_forward(
            queries,
            key_rows,
            value_rows,
            prefix_key_rows,
            prefix_value_rows,
            lengths_row,
            own_segment,
        )
        result = back_part(inbound, context, weights)[0].astype(jnp.bfloat16)
        seen_inputs.append(inbound)
        seen_outputs.append(result)
        seen_context.append(context)
        seen_logsum.append(logsum)
        if moment < micro_count:
            received = from_behind(result, "section", 1)
    kept_inputs = by_section(seen_inputs, is_first, True)
    weights = tuple((member[0] for member in gather_weights(shard_list)))
    back_received = jnp.zeros((tok_rows, model_width), jnp.bfloat16)
    grad_shards = tuple((jnp.zeros(member.shape, jnp.float32) for member in shard_list))
    prefix_key_total = jnp.zeros(prefix_key_rows.shape, jnp.float32)
    prefix_value_total = jnp.zeros(prefix_value_rows.shape, jnp.float32)
    seen_grads = []
    for moment in range(micro_count + 1):
        current = moment - 1 + section_index
        is_valid = ((current >= 0) & (current < micro_count)).astype(jnp.float32)
        picked = jnp.clip(current, 0, micro_count - 1)
        lengths_row = lengths[picked]
        own_segment = segment_of(lengths_row, own_positions)
        upstream = jnp.where(is_first, back_received, cotangent[min(moment, micro_count - 1)])
        d_input, grads, prefix_grads = layer_backward(
            kept_inputs[picked],
            upstream,
            weights,
            prefix_key_rows,
            prefix_value_rows,
            lengths_row,
            own_segment,
        )
        d_input_low = d_input.astype(jnp.bfloat16)
        seen_grads.append(d_input_low)
        if moment < micro_count:
            back_received = from_behind(d_input_low, "section", -1)
        grads = tuple((member * is_valid for member in grads))
        prefix_key_total = prefix_key_total + prefix_grads[0] * is_valid
        prefix_value_total = prefix_value_total + prefix_grads[1] * is_valid
        scattered = sum_each(grads)
        grad_shards = tuple((older + newer for older, newer in zip(grad_shards, scattered)))
    layer_outputs = by_section(seen_outputs, is_first, True)[None]
    input_grads = by_section(seen_grads, is_first, False)[None]
    prefix_sums = lax.psum((prefix_key_total, prefix_value_total), "tok")
    return (
        layer_outputs,
        input_grads,
        grad_shards[0],
        grad_shards[1],
        grad_shards[2],
        grad_shards[3],
        grad_shards[4],
        grad_shards[5],
        grad_shards[6],
        grad_shards[7],
        grad_shards[8],
        grad_shards[9],
        grad_shards[10],
        grad_shards[11],
        grad_shards[12],
        grad_shards[13],
        grad_shards[14],
        prefix_sums[0][None],
        prefix_sums[1][None],
    )


MESH = pl.DeviceIdType.MESH
F32 = jnp.float32
BF16 = jnp.bfloat16
ROWS = 64
PIECE = 16
PIECES = ROWS // PIECE
BLOCK = 256
SQRT_HALF = 0.7071067811865476
INV_SQRT_2PI = 0.3989422804014327
AG_X, AG_N, AG_Z, AG_O = range(4)
RS_O, RS_Z, RS_N, RS_X = range(4)


def flip(bit, other):
    return bit + other - 2 * bit * other


def mm(left, right):
    return jnp.dot(left, right, preferred_element_type=F32)


def mm_nt(left, right):
    return lax.dot_general(left, right, (((1,), (1,)), ((), ())), preferred_element_type=F32)


def mm_tn(left, right):
    return lax.dot_general(left, right, (((0,), (0,)), ((), ())), preferred_element_type=F32)


def rows_at(index, size):
    return pl.ds(pl.multiple_of(index * size, size), size)


def remote(src, dst, send, recv, device):
    return pltpu.make_async_remote_copy(
        src_ref=src, dst_ref=dst, send_sem=send, recv_sem=recv, device_id=device, device_id_type=MESH
    )


def local_copy(src, dst, sem):
    return pltpu.make_async_copy(src, dst, sem)


def bytes_of(ref, sem):
    return pltpu.make_async_copy(ref, ref, sem)


class Place:
    def __init__(self):
        self.x = lax.axis_index("section")
        self.t = lax.axis_index("tok")
        z = self.t // 4
        self.y = (self.t // 2) % 2
        self.core = self.t % 2
        self.cube = z // 2
        self.zl = z % 2
        self.chip = self.x * 4 + self.zl * 2 + self.y
        self.tau = self.chip * 2 + self.core

    def device(self, x, cube):
        return (x, cube * 8 + self.zl * 4 + self.y * 2 + self.core)

    def twin(self):
        return self.device(self.x, 1 - self.cube)

    def sibling(self):
        return (self.x, self.t + 1 - 2 * self.core)

    def peer(self, r):
        zl, y = flip(self.zl, (r // 2) % 2), flip(self.y, r % 2)
        return (flip(self.x, r // 4), self.cube * 8 + zl * 4 + y * 2 + self.core)

    def peer_chip(self, r):
        return flip(self.x, r // 4) * 4 + flip(self.zl, (r // 2) % 2) * 2 + flip(self.y, r % 2)

    def pair_rows(self, j):
        return rows_at(flip(self.x, j // 2) * 2 + flip(self.zl, j % 2), BLOCK)


def hops_of(first, last):
    hops = {(r, q): hop for q in range(PIECES) for r, hop in first}
    for q, (via, step, seen) in enumerate(last):
        hops[(via, q)] = (step, seen)
    return hops


class Pump:
    def __init__(self, rate=2):
        self.waiting = []
        self.rate = rate

    def add(self, starts):
        self.waiting += starts

    def go(self, count=None):
        count = self.rate if count is None else count
        for start in self.waiting[:count]:
            start()
        del self.waiting[:count]


class Gather:
    CUBE = (
        (4, 2, 1), ((1, 2, 4), (3, 6, 5), (7,)), (0, 2, 1, 3),
        hops_of(((1, (2, 3)), (2, (4, 6)), (4, (1, 5))), ((3, 4, 7), (6, 1, 7), (5, 2, 7), (3, 4, 7))),
    )

    def __init__(self, place, buf, recv, sib, sends):
        self.place, self.buf, self.recv, self.sib, self.sends = place, buf, recv, sib, sends
        self.near, self.stages, self.order, self.hops = self.CUBE
        self.pump = Pump()

    def piece(self, r, q, other=0):
        core = flip(self.place.core, other)
        row = (self.place.peer_chip(r) * 2 + core) * ROWS + q * PIECE
        return self.buf.at[pl.ds(pl.multiple_of(row, PIECE), PIECE)]

    def start(self):
        for q in range(PIECES):
            own = self.piece(0, q)
            for r in self.near:
                remote(own, own, self.sends.at[0, r, q], self.recv.at[r, q], self.place.peer(r)).start()
            self.to_sibling(0, q).start()

    def to_sibling(self, r, q):
        rows = self.piece(r, q)
        return remote(rows, rows, self.sends.at[1, r, q], self.sib.at[r, q], self.place.sibling())

    def arrive(self, r, q):
        rows = self.piece(r, q)
        bytes_of(rows, self.recv.at[r, q]).wait()
        if (r, q) in self.hops:
            hop, seen = self.hops[(r, q)]
            remote(rows, rows, self.sends.at[2, r, q], self.recv.at[seen, q], self.place.peer(hop)).start()
        self.to_sibling(r, q).start()

    def stage(self, number):
        for q in range(PIECES):
            for r in self.stages[number]:
                self.arrive(r, q)
            self.pump.go()

    def pair_ready(self, j):
        for r in (2 * j, 2 * j + 1):
            for q in range(PIECES):
                bytes_of(self.piece(r, q, 1), self.sib.at[r, q]).wait()

    def blocks(self, use):
        before = None
        for i, j in enumerate(self.order):
            if i < len(self.stages):
                self.stage(i)
            self.pair_ready(j)
            use(j, before)
            before = j
        self.drain()

    def drain(self):
        own = self.piece(0, 0)
        for q in range(PIECES):
            for r in self.near:
                bytes_of(own, self.sends.at[0, r, q]).wait()
            for r in range(2 * len(self.order)):
                bytes_of(own, self.sends.at[1, r, q]).wait()
        for r, q in self.hops:
            bytes_of(own, self.sends.at[2, r, q]).wait()


class Scatter:
    WAY = {3: (2, (7, 0)), 6: (4, (7, 1)), 5: (1, None), 1: (1, 3), 2: (2, 6), 4: (4, 5)}

    def __init__(self, place, recv, sends, half, keep, sib_out, sib_in, out, inbox):
        self.place, self.recv, self.sends = place, recv, sends
        self.half, self.keep, self.sib_out, self.sib_in = half, keep, sib_out, sib_in
        self.out, self.inbox = out, inbox
        self.pump = Pump()

    def pair(self, r):
        return remote(
            self.sib_out.at[r], self.sib_in.at[r], self.sends.at[0, r], self.recv.at[0, r], self.place.sibling()
        )

    def push(self, r):
        step = self.WAY[r][0]
        return remote(
            self.out.at[r], self.inbox.at[r], self.sends.at[1, r], self.recv.at[1, r], self.place.peer(step)
        )

    def part(self, q):
        rows, slot = pl.ds(q * 32, 32), (7, 0)[q]
        return remote(
            self.out.at[7, rows], self.inbox.at[7, rows], self.sends.at[1, slot], self.recv.at[1, slot],
            self.place.peer((4, 1)[q]),
        )

    def give(self, j, partial):
        for k in range(4):
            self.half[k] = partial[k * ROWS : (k + 1) * ROWS]
        core = self.place.core
        for b in range(2):
            r = 2 * j + flip(self.place.y, b)
            self.keep[r] = self.half[2 * b + core]
            self.sib_out[r] = self.half[2 * b + 1 - core].astype(BF16)
            self.pair(r).start()

    def forward(self, r):
        self.pair(r).wait_recv()
        if r == 7:
            self.out[7] = (self.keep[7] + self.sib_in[7].astype(F32)).astype(BF16)
            self.part(0).start()
            self.part(1).start()
            return
        more = self.WAY[r][1]
        if more is None:
            self.out[r] = (self.keep[r] + self.sib_in[r].astype(F32)).astype(BF16)
        elif isinstance(more, int):
            self.push(more).wait_recv()
            self.out[r] = (self.keep[r] + self.sib_in[r].astype(F32) + self.inbox[more].astype(F32)).astype(BF16)
        else:
            q = more[1]
            self.part(q).wait_recv()
            for k in range(2):
                rows = pl.ds(k * 32, 32)
                total = self.keep[r, rows] + self.sib_in[r, rows].astype(F32)
                if k == q:
                    total = total + self.inbox[7, rows].astype(F32)
                self.out[r, rows] = total.astype(BF16)
        self.push(r).start()

    def run(self, produce):
        def step(i, carry):
            @pl.when(i < 4)
            def _():
                self.give(3 - i, produce(3 - i))

            for when, steps in ((1, (7,)), (2, (5,)), (3, (3, 6)), (4, (1, 2, 4))):
                @pl.when(i == when)
                def _():
                    for r in steps:
                        self.forward(r)
                    self.pump.go()

            return carry

        lax.fori_loop(0, 5, step, 0)

    def rest(self):
        for r in (7, 3, 6, 1, 2, 4):
            self.forward(r)

    def finish(self):
        self.pair(0).wait_recv()
        self.keep[0] = self.keep[0] + self.sib_in[0].astype(F32)
        for r in (1, 2, 4):
            self.push(r).wait_recv()
            self.keep[0] = self.keep[0] + self.inbox[r].astype(F32)
        for r in range(8):
            self.pair(r).wait_send()
        for r in self.WAY:
            self.push(r).wait_send()
        for q in range(2):
            self.part(q).wait_send()
        return self.keep[0]


def norm_forward(value, gain, shift, hat_ref, rstd_ref):
    centred = value - jnp.mean(value, axis=-1, keepdims=True)
    rstd = lax.rsqrt(jnp.mean(centred * centred, axis=-1, keepdims=True) + 1e-05)
    hat = centred * rstd
    hat_ref[...] = hat
    rstd_ref[...] = jnp.broadcast_to(rstd, rstd_ref.shape)
    return hat * gain + shift


def norm_backward(upstream, gain, hat_ref, rstd_ref):
    hat = hat_ref[...]
    scaled = upstream * gain
    mean_one = jnp.mean(scaled, axis=-1, keepdims=True)
    mean_two = jnp.mean(scaled * hat, axis=-1, keepdims=True)
    result = rstd_ref[:, :1] * (scaled - mean_one - hat * mean_two)
    d_gain = jnp.sum(upstream * hat, axis=0, keepdims=True)
    d_shift = jnp.sum(upstream, axis=0, keepdims=True)
    return result, d_gain, d_shift


def column_sum(low):
    return jnp.sum(low.astype(F32), axis=0, keepdims=True)


def kernel(
    lengths, inputs, cotangent, wq_src, wk_src, wv_src, wup_src, wdn_src, wout_src, pk_src, pv_src,
    v0, v1, v2, v3, v4, v5, v6, v7, v8,
    out_y, out_dx, out_q, out_k, out_v, out_o, out_up, out_dn, out_pk, out_pv, got_rows, got_bias,
    ag_recv, ag_sib, ag_send, rs_recv, rs_send,
    wsend, wown, wtwin, wrelay, psem, xsem, osend, orecv, tsend, trecv, gsend, grecv, rsem,
    raw_qkv, raw_up, pack_qkv, pack_up, vrows, u0, u1, u2, u3, u4, u5, u6, u7, u8,
    wqkv, wup, wdn, wout, pre,
    qseg, kseg, xg, ng, dzg, dog, param,
    qs, ks, vs, kt, vt, lse, ctb, ctf,
    hat1, rstd1, hat2, rstd2, act, dact,
    half, keep, sib_out, sib_in, rs_out, inbox,
    own_a, own_b, ystage, dstage,
    dfs, dcb, delta, dqt, dkacc, dvacc, dqkv, dqkvt,
    rowacc, biasacc, g_qkv, g_up, g_dn, g_out, g_prefix,
    t_qkv, t_up, t_dn, t_out, t_prefix,
    got_qkv, got_up, got_dn, got_out, got_prefix,
):
    place = Place()
    x, t, cube, core, tau = place.x, place.t, place.cube, place.core, place.tau
    tokens = qs.shape[1]
    width = xg.shape[2]
    half_rows = 8 * ROWS
    barrier = pltpu.get_barrier_semaphore()

    def greet(i, carry):
        gx, gt = i // 16, i % 16

        @pl.when((gx != x) | (gt != t))
        def _():
            pl.semaphore_signal(barrier, inc=1, device_id=(gx, gt), device_id_type=MESH)

        return carry

    lax.fori_loop(0, 32, greet, 0)

    raw = [local_copy(src.at[0], raw_qkv.at[i], rsem.at[i]) for i, src in enumerate((wq_src, wk_src, wv_src))]
    raw.append(local_copy(wup_src.at[0], raw_up, rsem.at[3]))
    vectors = (u0, u1, u2, u3, u4, u5, u6, u7, u8)
    for i, (src, dst) in enumerate(zip((v0, v1, v2, v3, v4, v5, v6, v7, v8), vectors)):
        raw.append(local_copy(src, dst, rsem.at[4 + i]))
    for copy in raw:
        copy.start()
    vrows[...] = jnp.zeros_like(vrows)
    for copy in raw:
        copy.wait()
    for i in range(8):
        vrows[i : i + 1, 0:64] = vectors[i][...].astype(F32)
    up_row = u8[...].astype(F32)
    for i in range(4):
        vrows[8 + i : 9 + i, 0:64] = up_row[:, i * 64 : (i + 1) * 64]
    vector_columns = vrows[...].T[0:64]

    def pack_heads(h, carry):
        cols = rows_at(h, 128)
        parts = [raw_qkv[i, :, cols].astype(F32) for i in range(3)]
        for s in range(2):
            sides = [part[:, s * 64 : (s + 1) * 64] for part in parts]
            pack_qkv[2 * h + s] = jnp.concatenate(sides + [vector_columns], axis=1).astype(BF16)
        return carry

    lax.fori_loop(0, 8, pack_heads, 0)
    for side in range(2):
        for rest in range(8):
            for zhi in range(2):
                start = (zhi * 8 + rest) * 256 + side * 128
                pack_up[side * 8 + rest, :, zhi * 128 : (zhi + 1) * 128] = raw_up[:, start : start + 128]

    pl.semaphore_wait(barrier, 31)

    own_rows = rows_at(tau, ROWS)
    first, last = pl.ds(0, 32), pl.ds(32, 32)
    diagonal = place.device(1 - x, 1 - cube)
    neighbour = place.device(1 - x, cube)

    def shares(source, target, far, sem):
        here = local_copy(source.at[cube], target, xsem.at[sem])
        to_twin = remote(source.at[1 - cube, first], target.at[first], xsem.at[sem + 1], xsem.at[sem + 2], place.twin())
        to_diagonal = remote(source.at[1 - cube, last], far.at[last], xsem.at[sem + 1], xsem.at[sem + 3], diagonal)

        def start():
            @pl.when(x == cube)
            def _():
                to_twin.start()
                here.start()

            pl.when(x != cube)(to_diagonal.start)

        def arrived():
            @pl.when(x != cube)
            def _():
                to_twin.wait_recv()
                to_diagonal.wait_recv()

            pl.when(x == cube)(here.wait)

        def sent():
            pl.when(x == cube)(to_twin.wait_send)
            pl.when(x != cube)(to_diagonal.wait_send)

        return start, arrived, sent

    x_start, x_arrived, x_sent = shares(inputs, xg.at[0, own_rows], xg.at[0, rows_at(tau + 8 - 16 * x, ROWS)], 0)
    d_start, d_arrived, d_sent = shares(cotangent, dstage.at[2], dstage.at[2], 4)
    x_start()

    def spread_pushes(kind):
        src_all, dst_all = (pack_qkv, pack_up)[kind], (wqkv, wup)[kind]
        dst, sem = dst_all.at[rows_at(x * 16 + t, ROWS)], wown.at[kind, x, t % 8]
        for k in range(16):
            to = lax.rem(k + tau + 1, 16)

            def go(to=to):
                src = src_all.at[to]
                pl.when(to == tau)(local_copy(src, dst, sem).start)
                pl.when(to != tau)(remote(src, dst, wsend.at[kind], sem, (to // 8, cube * 8 + to % 8)).start)

            yield go

    def slice_pushes():
        neighbour = place.device(1 - x, cube)

        def give_out():
            src, dst = wout_src.at[0], wout.at[x]
            pl.when(x == cube)(local_copy(src, dst, wown.at[2, x, 0]).start)
            pl.when(x != cube)(remote(src, dst, wsend.at[2], wown.at[2, x, 0], neighbour).start)

        def give_down():
            for side in range(2):
                src = wdn_src.at[0, pl.ds(side * 128, 128)]
                dst = wdn.at[x, rows_at(cube, 128)]
                pl.when(x == side)(local_copy(src, dst, wown.at[3, x, 0]).start)
                pl.when(x != side)(remote(src, dst, wsend.at[3], wown.at[3, x, 0], neighbour).start)

        return give_out, give_down

    def prefix_out():
        for side, index in ((x, 0), (1 - x, 1)):
            for kind, src_all in ((0, pk_src), (1, pv_src)):
                src = src_all.at[0, :, rows_at(side * 4 + place.zl * 2 + place.y, 128)]
                dst = pre.at[x, kind]
                if index == 0:
                    yield local_copy(src, dst, psem.at[0, kind])
                else:
                    yield remote(src, dst, psem.at[1, kind], psem.at[2, kind], place.device(1 - x, cube))

    def slice_ref(kind, l, zhi):
        if kind < 2:
            return (wqkv, wup)[kind].at[rows_at(l * 2 + zhi, half_rows)]
        if kind == 3:
            return wdn.at[l, rows_at(zhi, 128)]
        return wout.at[l]

    def to_twin(ref, kind, l):
        return remote(ref, ref, wrelay.at[kind, l], wtwin.at[kind, l], place.twin())

    def relay_blocks(kind, l):
        def one(i, carry):
            k = lax.rem(jnp.where(x == l, tau, 0) + 7 - i, 8)
            ref = (wqkv, wup)[kind].at[rows_at((l * 2 + cube) * 8 + k, ROWS)]
            bytes_of(ref, wown.at[kind, l, k]).wait()
            to_twin(ref, kind, l).start()
            return carry

        lax.fori_loop(0, 8, one, 0)

    def relay_out(l):
        @pl.when(x == cube)
        def _():
            bytes_of(wout.at[l], wown.at[2, l, 0]).wait()
            to_twin(wout.at[l], 2, l).start()

    def relay_down(l):
        dn = slice_ref(3, l, cube)
        bytes_of(dn, wown.at[3, l, 0]).wait()
        to_twin(dn, 3, l).start()

    def weights_in(kind, l):
        wait = bytes_of(slice_ref(kind, l, 1 - cube), wtwin.at[kind, l]).wait
        if kind == 2:
            pl.when(x != cube)(wait)
        else:
            wait()

    def weights_drain():
        for kind, ref in ((0, pack_qkv), (1, pack_up)):
            bytes_of(ref.at[pl.ds(0, 15)], wsend.at[kind]).wait()
        bytes_of(wdn.at[0, pl.ds(0, 128)], wsend.at[3]).wait()
        pl.when(x != cube)(bytes_of(wout.at[0], wsend.at[2]).wait)
        for l in range(2):
            for kind in (0, 1, 3):
                to_twin(slice_ref(kind, l, cube), kind, l).wait_send()
            pl.when(x == cube)(to_twin(wout.at[l], 2, l).wait_send)

    def weight(ref, l):
        return ref[rows_at(l, 16 * ROWS)]

    def own_half(pair):
        return jnp.where(core == 0, pair[:, :64], pair[:, 64:])

    def gather(buf, phase):
        return Gather(place, buf, ag_recv.at[phase], ag_sib.at[phase], ag_send)

    def scatter(phase):
        boxes = phase % 2
        return Scatter(
            place, rs_recv.at[phase], rs_send, half, keep, sib_out, sib_in.at[boxes], rs_out, inbox.at[boxes],
        )

    prefixes = list(prefix_out())
    for copy in prefixes:
        copy.start()

    @pl.when(x == 0)
    def _():
        for start in spread_pushes(0):
            start()

    rowacc[...] = jnp.zeros_like(rowacc)
    biasacc[...] = jnp.zeros_like(biasacc)
    dqt[64:128] = jnp.zeros((64, tokens), F32)
    along = lax.broadcasted_iota(jnp.int32, (8, tokens), 1)
    down = lax.broadcasted_iota(jnp.int32, (tokens, 128), 0)
    segment_q, segment_k = jnp.zeros((8, tokens), jnp.int32), jnp.zeros((tokens, 128), jnp.int32)
    end = jnp.int32(0)
    for j in range(lengths.shape[1]):
        end = end + lengths[cube, j]
        segment_q = segment_q + (along >= end).astype(jnp.int32)
        segment_k = segment_k + (down >= end).astype(jnp.int32)
    qseg[...] = segment_q
    kseg[0:tokens] = segment_k
    kseg[tokens:] = jnp.full((kseg.shape[0] - tokens, 128), -1, jnp.int32)

    relay_blocks(0, 0)
    x_arrived()

    def result_out(stage, out, kind, layer):
        dst = out.at[cube]
        is_self = (layer == x) & (x == cube)
        here = local_copy(stage, dst, orecv.at[kind, cube])
        there = remote(stage, dst, osend.at[kind, layer], orecv.at[kind, cube], place.device(layer, x))
        return is_self, here, there

    def visible(cols):
        key_part = kseg[...]
        keys_two = jnp.concatenate([key_part, key_part], axis=1)
        return (keys_two == qseg[0:1, cols]) | (keys_two < 0)

    def forward_layer(l, carry):
        gather_x = gather(xg.at[l], AG_X)
        gather_x.start()

        @pl.when(l == 0)
        def _():
            def first_layer(start):
                return lambda: pl.when(x == 0)(start)

            give_out, give_down = slice_pushes()
            gather_x.pump.add([first_layer(start) for start in (give_out, *spread_pushes(1), give_down)])
            gather_x.stage(0)
            gather_x.pump.go(1)
            relay_out(0)
            gather_x.stage(1)
            gather_x.pump.go(len(gather_x.pump.waiting))
            relay_blocks(1, 0)
            gather_x.stage(2)
            relay_down(0)
            d_start()
            for copy in prefixes[:2]:
                copy.wait()
            for copy in prefixes[2:]:
                copy.wait()

        weights_in(0, l)
        tail = wqkv[rows_at(l, 16 * ROWS), 128:256].astype(F32).T
        param[l] = tail[64:80]
        biases = own_half(param[l, 0:8, rows_at(tau // 2, 128)])[6:8]
        empty = jnp.zeros((1, 64), F32)
        qkv_bias = jnp.concatenate([biases[0:1], empty, biases[1:2], empty], axis=1)
        prefix = jnp.concatenate(
            [own_half(pre[l, 0].astype(F32)), own_half(pre[l, 1].astype(F32))], axis=1
        )
        ks[l, tokens:] = prefix[:, :64].astype(BF16)
        vs[l, tokens:] = prefix[:, 64:].astype(BF16)
        prefix_t = prefix.T
        kt[l, :, tokens:] = prefix_t[:64].astype(BF16)
        vt[l, :, tokens:] = prefix_t[64:].astype(BF16)

        for i, j in enumerate(gather_x.order):
            if i < 3:
                @pl.when(l == 1)
                def _():
                    gather_x.stage(i)

            gather_x.pair_ready(j)
            rows = place.pair_rows(j)
            value = mm(xg[l, rows], weight(wqkv, l)) + qkv_bias
            qs[l, rows] = (value[:, :64] * 0.125).astype(BF16)
            ks[l, rows] = value[:, 64:128].astype(BF16)
            vs[l, rows] = value[:, 128:192].astype(BF16)
            value_t = value.T
            kt[l, :, rows] = value_t[64:128].astype(BF16)
            vt[l, :, rows] = value_t[128:192].astype(BF16)
        gather_x.drain()

        def second_layer(start):
            return lambda: pl.when((l == 0) & (x == 1))(start)

        give_out, give_down = slice_pushes()
        scatter_o = scatter(RS_O)
        scatter_o.pump = Pump(5)
        scatter_o.pump.add(
            [second_layer(start) for start in (*spread_pushes(0), give_out, give_down, *spread_pushes(1))]
        )

        def attend(j):
            cols = place.pair_rows(j)
            scores = jnp.where(visible(cols), mm_nt(ks[l], qs[l, cols]), NEGATIVE)
            top = jnp.max(scores, axis=0, keepdims=True)
            grown = jnp.exp(scores - top)
            total = jnp.sum(grown, axis=0, keepdims=True)
            probs = (grown * (1.0 / total)).astype(BF16)
            lse[l, 0:1, cols] = top + jnp.log(total)
            context_t = mm(vt[l], probs)
            ctf[l, :, cols] = context_t
            low = context_t.astype(BF16)
            ctb[l, :, cols] = low
            return mm_tn(low, wout[l])

        pl.when(l == 0)(lambda: weights_in(2, 0))
        pl.when(l == 1)(lambda: weights_in(2, 1))
        scatter_o.run(attend)
        scatter_o.pump.go(len(scatter_o.pump.waiting))
        attended = scatter_o.finish() + param[l, 0:1]
        normal = norm_forward(
            xg[l, own_rows].astype(F32) + attended,
            param[l, 1:2], param[l, 2:3], hat1.at[l], rstd1.at[l],
        )
        own_a[...] = normal
        ng[l, own_rows] = normal.astype(BF16)
        gather_n = gather(ng.at[l], AG_N)
        gather_n.start()

        @pl.when(l == 0)
        def _():
            relay_blocks(0, 1)

        weights_in(1, l)
        weights_in(3, l)
        up_part = own_half(param[l, 8:16, rows_at(place.zl * 2 + place.y, 128)])
        up_more = own_half(param[l, 8:16, rows_at(4 + place.zl * 2 + place.y, 128)])
        up_parts = jnp.where(x == 0, up_part[0:2], up_part[2:4])
        up_more = jnp.where(x == 0, up_more[0:2], up_more[2:4])
        up_bias = jnp.concatenate([up_parts[0:1], up_parts[1:2], up_more[0:1], up_more[1:2]], axis=1)
        scatter_z = scatter(RS_Z)

        def feed_block(j, before):
            rows = place.pair_rows(j)
            value = mm(ng[l, rows], weight(wup, l)) + up_bias
            cdf = 0.5 * (1.0 + lax.erf(value * SQRT_HALF))
            low = (value * cdf).astype(BF16)
            act[l, rows] = low
            dact[l, rows] = cdf + value * (jnp.exp(-0.5 * value * value) * INV_SQRT_2PI)
            scatter_z.give(j, mm(low, wdn[l]))
            if j == 1:
                scatter_z.forward(5)

        gather_n.blocks(feed_block)
        scatter_z.rest()

        @pl.when(l == 0)
        def _():
            relay_out(1)
            relay_blocks(1, 1)
            relay_down(1)

        mixed = scatter_z.finish() + param[l, 3:4]
        result = norm_forward(
            own_a[...] + mixed, param[l, 4:5], param[l, 5:6], hat2.at[l], rstd2.at[l]
        ).astype(BF16)
        ystage[l] = result

        @pl.when(l == 0)
        def _():
            xg[1, own_rows] = result

        is_self, here, there = result_out(ystage.at[l], out_y, 0, l)
        pl.when(is_self)(here.start)
        pl.when(jnp.logical_not(is_self))(there.start)
        return carry

    lax.fori_loop(0, 2, forward_layer, 0)

    d_arrived()

    other_half, this_half = 1 - cube, cube

    def twin_parts(kind, l):
        if kind == 0:
            return g_qkv.at[l, rows_at(other_half, half_rows)], t_qkv, g_qkv.at[l, rows_at(this_half, half_rows)]
        if kind == 1:
            return g_up.at[l, rows_at(other_half, half_rows)], t_up, g_up.at[l, rows_at(this_half, half_rows)]
        if kind == 2:
            return g_prefix.at[l, rows_at(other_half, 32)], t_prefix, g_prefix.at[l, rows_at(this_half, 32)]
        if kind == 3:
            return g_dn.at[l, rows_at(other_half, 128)], t_dn, g_dn.at[l, rows_at(this_half, 128)]
        return g_out.at[l], t_out, g_out.at[l]

    def twin_send(kind, l):
        src, box, own = twin_parts(kind, l)
        return remote(src, box.at[l], tsend.at[kind, l], trecv.at[kind, l], place.twin())

    def twin_chunks(kind, l):
        src, box, own = twin_parts(kind, l)
        rows = ROWS if kind < 2 else 16
        for k in range(src.shape[0] // rows):
            part = pl.ds(k * rows, rows)
            yield remote(
                src.at[part], box.at[l, part], tsend.at[kind, l], trecv.at[kind, l], place.twin()
            ).start

    def twin_start(kind, l):
        copy = twin_send(kind, l)
        if kind == 4:
            pl.when(x != cube)(copy.start)
        else:
            copy.start()

    def owner_pushes(kind, l):
        src, box, own = twin_parts(kind, l)
        mine = x == l

        def start(is_self, part, dst, dev, condition=None):
            def go():
                pl.when(is_self)(local_copy(part, dst, grecv.at[kind]).start)
                pl.when(jnp.logical_not(is_self))(
                    remote(part, dst, gsend.at[kind, l], grecv.at[kind], dev).start
                )

            return go if condition is None else lambda: pl.when(condition)(go)

        if kind < 2:
            got = (got_qkv, got_up)[kind]
            for k in range(8):
                to = lax.rem(k + t + 1, 8)
                yield start(mine & (to == t % 8), own.at[rows_at(to, ROWS)], got.at[tau], (l, cube * 8 + to))
        elif kind == 2:
            for k in range(16):
                to = lax.rem(k + t + 1, 16)
                yield start(mine & (to == t), own, got_prefix.at[tau, rows_at(this_half, 32)], (l, to))
        elif kind == 3:
            yield start(mine, own, got_dn.at[rows_at(x, 128)], place.device(l, cube))
        else:
            yield start(mine, own, got_out, place.device(l, cube), x == cube)

    def owner_add(kind, l):
        src, box, own = twin_parts(kind, l)

        def add():
            twin_send(kind, l).wait_recv()
            own[...] = (own[...].astype(F32) + box[l].astype(F32)).astype(BF16)

        if kind == 4:
            pl.when(x == cube)(add)
        else:
            add()

    def owner_start(kind, l):
        owner_add(kind, l)
        for start in owner_pushes(kind, l):
            start()

    def grads_drain(l):
        for kind in range(5):
            if kind == 4:
                pl.when(x != cube)(twin_send(kind, l).wait_send)
            else:
                twin_send(kind, l).wait_send()
        for kind, ref in ((0, got_qkv), (1, got_up)):
            pl.when(x == l)(bytes_of(ref.at[pl.ds(0, 7)], gsend.at[kind, l]).wait)
            pl.when(x != l)(bytes_of(ref.at[pl.ds(0, 8)], gsend.at[kind, l]).wait)
        for count, condition in ((15, x == l), (16, x != l)):
            pl.when(condition)(bytes_of(got_prefix.at[pl.ds(0, count), pl.ds(0, 32)], gsend.at[2, l]).wait)
            pl.when(condition)(bytes_of(got_rows.at[pl.ds(0, count)], gsend.at[5, l]).wait)
        pl.when(x != l)(bytes_of(g_dn.at[0, pl.ds(0, 128)], gsend.at[3, l]).wait)
        pl.when((x != l) & (x == cube))(bytes_of(g_out.at[0], gsend.at[4, l]).wait)
        for to, src, dst in bias_pairs(l):
            is_self = (x == l) & (cube == to)
            pl.when(jnp.logical_not(is_self))(bytes_of(src, gsend.at[6 + to, l]).wait)

    def rows_start(l):
        def one(k, carry):
            to = lax.rem(k + t + 1, 16)
            src, dst = rowacc.at[l, :, rows_at(to // 2, 128)], got_rows.at[cube * 16 + tau]
            is_self = (x == l) & (to == t)
            pl.when(is_self)(local_copy(src, dst, grecv.at[5]).start)
            pl.when(jnp.logical_not(is_self))(remote(src, dst, gsend.at[5, l], grecv.at[5], (l, to)).start)
            return carry

        lax.fori_loop(0, 16, one, 0)

    def bias_pairs(l):
        for to in range(2):
            yield to, biasacc.at[l], got_bias.at[cube * 2 + x]

    def bias_start(l):
        for to, src, dst in bias_pairs(l):
            is_self = (x == l) & (cube == to)
            pl.when(is_self)(local_copy(src, dst, grecv.at[6]).start)
            pl.when(jnp.logical_not(is_self))(
                remote(src, dst, gsend.at[6 + to, l], grecv.at[6], place.device(l, to)).start
            )

    def backward_layer(step, carry):
        l = 1 - step
        upstream = dstage[l + 1].astype(F32)
        d_sum, d_gain, d_shift = norm_backward(upstream, param[l, 4:5], hat2.at[l], rstd2.at[l])
        own_b[...] = d_sum
        low = d_sum.astype(BF16)
        dzg[own_rows] = low
        gather_z = gather(dzg, AG_Z)
        gather_z.start()
        rowacc[l, 3:4] = d_gain
        rowacc[l, 4:5] = d_shift
        rowacc[l, 5:6] = column_sum(low)
        scatter_n = scatter(RS_N)

        def back_block(j, before):
            rows = place.pair_rows(j)
            low = (dact[l, rows] * mm_nt(dzg[rows], wdn[l])).astype(BF16)
            dfs[rows] = low
            scatter_n.give(j, mm_nt(low, weight(wup, l)))
            if j == 1:
                scatter_n.forward(5)

        gather_z.blocks(back_block)
        scatter_n.rest()
        biasacc[l, 1:2] = column_sum(dfs[...])

        def down_tile(i, carry):
            cols = rows_at(i, 256)
            g_dn[l, :, cols] = mm_tn(act[l], dzg[:, cols]).astype(BF16)
            return carry

        lax.fori_loop(0, width // 256, down_tile, 0)

        def up_tile(i, carry):
            cols = rows_at(i, 256)
            g_up[l, cols] = mm_tn(ng[l, :, cols], dfs[...]).astype(BF16)
            return carry

        lax.fori_loop(0, width // 256, up_tile, 0)
        @pl.when(l == 0)
        def _():
            for kind in (3, 1, 2, 4, 0):
                owner_add(kind, 1)

        def older(start):
            return lambda: pl.when(l == 0)(start)

        pump = Pump(1)
        twins = [*twin_chunks(3, l), *twin_chunks(1, l)]
        olds = [older(start) for kind in (3, 1, 4, 0, 2) for start in owner_pushes(kind, 1)]
        for k in range(17):
            pump.add(twins[k : k + 1] + olds[2 * k : 2 * k + 2])
        pump.go(3)

        d_normal = own_b[...] + scatter_n.finish()
        d_sum, d_gain, d_shift = norm_backward(d_normal, param[l, 1:2], hat1.at[l], rstd1.at[l])
        own_a[...] = d_sum
        low = d_sum.astype(BF16)
        dog[own_rows] = low
        gather_o = gather(dog, AG_O)
        gather_o.pump = pump
        gather_o.start()
        rowacc[l, 0:1] = d_gain
        rowacc[l, 1:2] = d_shift
        rowacc[l, 2:3] = column_sum(low)
        rows_start(l)


        dkacc[...] = jnp.zeros_like(dkacc)
        dvacc[...] = jnp.zeros_like(dvacc)

        def attend_back(j, before):
            cols = place.pair_rows(j)
            d_context = mm_nt(dog[cols], wout[l]).astype(BF16)
            dcb[cols] = d_context
            d_context_t = mm_nt(wout[l], dog[cols]).astype(BF16).astype(F32)
            sums = jnp.sum(d_context_t * ctf[l, :, cols], axis=0, keepdims=True)
            scores = jnp.where(visible(cols), mm_nt(ks[l], qs[l, cols]), NEGATIVE)
            probs = jnp.exp(scores - lse[l, 0:1, cols])
            d_probs = mm_nt(vs[l], d_context)
            d_scores = (probs * (d_probs - sums)).astype(BF16)
            dvacc[...] += mm(probs.astype(BF16), d_context)
            dkacc[...] += mm(d_scores, qs[l, cols])
            dqt[0:64, cols] = mm(kt[l], d_scores) * 0.125
            pump.go(3)

        gather_o.blocks(attend_back)
        g_prefix[l] = jnp.concatenate([dkacc[tokens:], dvacc[tokens:]], axis=1).astype(BF16)
        twin_start(2, l)
        g_out[l] = mm(ctb[l], dog[...]).astype(BF16)
        twin_start(4, l)

        def assemble(i, carry):
            rows = rows_at(i, BLOCK)
            d_query = dqt[:, rows].T[:, :64]
            value = jnp.concatenate(
                [d_query, dkacc[rows], dvacc[rows], jnp.zeros((BLOCK, 64), F32)], axis=1
            )
            dqkv[rows] = value.astype(BF16)
            dqkvt[:, rows] = value.T.astype(BF16)
            return carry

        lax.fori_loop(0, tokens // BLOCK, assemble, 0)

        def qkv_tile(i, carry):
            cols = rows_at(i, 256)
            g_qkv[l, cols] = mm(dqkvt[...], xg[l, :, cols]).T.astype(BF16)
            return carry

        lax.fori_loop(other_half * 2, other_half * 2 + 2, qkv_tile, 0)
        pump.add(list(twin_chunks(0, l)))
        pump.go(2)
        scatter_x = scatter(RS_X)
        scatter_x.pump = pump
        pump.rate = 2
        scatter_x.run(lambda j: mm_nt(dqkv[place.pair_rows(j)], weight(wqkv, l)))
        biasacc[l, 0:1, 0:256] = column_sum(dqkv[...])
        bias_start(l)
        lax.fori_loop(this_half * 2, this_half * 2 + 2, qkv_tile, 0)
        pump.go(len(pump.waiting))

        dstage[l] = (own_a[...] + scatter_x.finish()).astype(BF16)
        is_self, here, there = result_out(dstage.at[l], out_dx, 1, l)
        pl.when(is_self)(here.start)
        pl.when(jnp.logical_not(is_self))(there.start)
        return carry

    lax.fori_loop(0, 2, backward_layer, 0)
    for kind in (3, 1, 2, 4, 0):
        owner_start(kind, 0)

    x_sent()
    d_sent()
    weights_drain()
    for l in range(2):
        grads_drain(l)
        for kind, stage, out in ((0, ystage.at[l], out_y), (1, dstage.at[l], out_dx)):
            is_self, here, there = result_out(stage, out, kind, l)
            pl.when(jnp.logical_not(is_self))(there.wait_send)
    for kind, out in ((0, out_y), (1, out_dx)):
        for m in range(2):
            bytes_of(out.at[m], orecv.at[kind, m]).wait()

    def landed(kind):
        ref = (got_qkv, got_up, got_prefix, got_dn, got_out, got_rows, got_bias)[kind]
        bytes_of(ref, grecv.at[kind]).wait()

    landed(3)
    out_dn[0] = got_dn[...].astype(F32)
    landed(1)
    for side in range(2):
        for rest in range(8):
            for zhi in range(2):
                start = (zhi * 8 + rest) * 256 + side * 128
                part = got_up[side * 8 + rest, :, zhi * 128 : (zhi + 1) * 128]
                out_up[0, :, start : start + 128] = part.astype(F32)
    landed(4)
    out_o[0] = got_out[...].astype(F32)

    def heads_together(got, outs):
        for h in range(8):
            pair = [got[2 * h].astype(F32), got[2 * h + 1].astype(F32)]
            for i, out in enumerate(outs):
                sides = [value[:, i * 64 : (i + 1) * 64] for value in pair]
                out[0, :, h * 128 : (h + 1) * 128] = jnp.concatenate(sides, axis=1)

    landed(2)
    heads_together(got_prefix, (out_pk, out_pv))
    landed(0)
    heads_together(got_qkv, (out_q, out_k, out_v))
    landed(5)
    landed(6)


def cube_local(
    inputs, cotangent, lengths, prefix_keys, prefix_values,
    w_query, b_query, w_key, w_value, b_value, w_out, b_out, norm1_gain, norm1_shift,
    w_up, b_up, w_down, b_down, norm2_gain, norm2_shift,
):
    t = lax.axis_index("tok")
    rows, width = w_query.shape[1], w_query.shape[2]
    heads = width // HEAD
    tokens = inputs.shape[1] * lax.axis_size("tok")
    prefix = prefix_keys.shape[1]
    keys = tokens + prefix
    hidden = b_up.shape[1]

    anywhere = pl.BlockSpec(memory_space=pl.ANY)
    smem = pl.BlockSpec(memory_space=pltpu.SMEM)
    dma = pltpu.SemaphoreType.DMA
    V = pltpu.VMEM
    L = 2
    shape = jax.ShapeDtypeStruct
    results = pl.pallas_call(
        kernel,
        out_shape=(
            shape((2, ROWS, width), BF16), shape((2, ROWS, width), BF16),
            shape((1, rows, width), F32), shape((1, rows, width), F32), shape((1, rows, width), F32),
            shape((1, rows, width), F32), shape((1, rows, 4 * width), F32), shape((1, hidden, width), F32),
            shape((1, prefix, width), F32), shape((1, prefix, width), F32),
            shape((32, 8, 128), F32), shape((4, 8, hidden), F32),
        ),
        in_specs=[smem] + [anywhere] * 19,
        out_specs=[anywhere] * 2 + [pl.BlockSpec(memory_space=pltpu.VMEM)] * 8 + [anywhere] * 2,
        scratch_shapes=[
            dma((4, 8, PIECES)), dma((4, 8, PIECES)), dma((3, 8, PIECES)), dma((4, 2, 8)), dma((2, 8)),
            dma((4,)), dma((4, 2, 8)), dma((4, 2)), dma((4, 2)), dma((3, 2)), dma((8,)),
            dma((2, 2)), dma((2, 2)), dma((5, 2)), dma((5, 2)), dma((8, 2)), dma((7,)), dma((13,)),
            V((3, rows, width), BF16), V((rows, 4 * width), BF16), V((heads, rows, 256), BF16), V((heads, rows, 256), BF16),
            V((64, 128), F32),
            *[V((1, rows), BF16)] * 8, V((1, hidden), BF16),
            V((L * 1024, 256), BF16), V((L * 1024, 256), BF16), V((L, hidden, width), BF16),
            V((L, ROWS, width), BF16), V((L, 2, prefix, 128), BF16),
            V((8, tokens), jnp.int32), V((keys, 128), jnp.int32),
            V((L, tokens, width), BF16), V((L, tokens, width), BF16),
            V((tokens, width), BF16), V((tokens, width), BF16), V((L, 16, width), F32),
            V((L, tokens, HEAD), BF16), V((L, keys, HEAD), BF16), V((L, keys, HEAD), BF16),
            V((L, HEAD, keys), BF16), V((L, HEAD, keys), BF16),
            V((L, 8, tokens), F32), V((L, HEAD, tokens), BF16), V((L, HEAD, tokens), F32),
            V((L, ROWS, width), F32), V((L, ROWS, 128), F32), V((L, ROWS, width), F32), V((L, ROWS, 128), F32),
            V((L, tokens, hidden), BF16), V((L, tokens, hidden), F32),
            V((4, ROWS, width), F32), V((8, ROWS, width), F32), V((8, ROWS, width), BF16),
            V((2, 8, ROWS, width), BF16), V((8, ROWS, width), BF16), V((2, 8, ROWS, width), BF16),
            V((ROWS, width), F32), V((ROWS, width), F32), V((L, ROWS, width), BF16), V((L + 1, ROWS, width), BF16),
            V((tokens, hidden), BF16), V((tokens, HEAD), BF16), V((8, tokens), F32), V((128, tokens), F32),
            V((keys, HEAD), F32), V((keys, HEAD), F32), V((tokens, 256), BF16), V((256, tokens), BF16),
            V((L, 8, width), F32), V((L, 8, hidden), F32),
            V((L, width, 256), BF16), V((L, width, hidden), BF16), V((L, hidden, width), BF16),
            V((L, ROWS, width), BF16), V((L, prefix, 128), BF16),
            V((L, width // 2, 256), BF16), V((L, width // 2, 256), BF16), V((L, hidden // 2, width), BF16),
            V((L, ROWS, width), BF16), V((L, prefix // 2, 128), BF16),
            V((16, ROWS, 256), BF16), V((16, ROWS, 256), BF16), V((hidden, width), BF16), V((ROWS, width), BF16),
            V((16, prefix, 128), BF16),
        ],
        compiler_params=pltpu.CompilerParams(
            collective_id=0, has_side_effects=True, vmem_limit_bytes=60 * 2**20
        ),
    )(
        lengths, inputs, cotangent, w_query, w_key, w_value, w_up, w_down, w_out, prefix_keys, prefix_values,
        b_out, norm1_gain, norm1_shift, b_down, norm2_gain, norm2_shift, b_query, b_value, b_up,
    )
    out_y, out_dx, out_q, out_k, out_v, out_o, out_up, out_dn, out_pk, out_pv, got_rows, got_bias = results
    row_sum = lax.dynamic_slice_in_dim(jnp.sum(got_rows, axis=0), (t % 2) * 64, 64, 1)
    side = t // 8
    bias_up = (got_bias[:2, 1] + got_bias[2:, 1]).reshape(2, 2, 128)
    bias_up = lax.dynamic_index_in_dim(bias_up, side, 1, keepdims=False).reshape(1, hidden)
    bias_qkv = lax.dynamic_index_in_dim(got_bias[:2, 0] + got_bias[2:, 0], side, 0, keepdims=True)
    return (
        out_y[None],
        out_dx[None],
        out_q,
        bias_qkv[:, 0:64],
        out_k,
        out_v,
        bias_qkv[:, 128:192],
        out_o,
        row_sum[2:3],
        row_sum[0:1],
        row_sum[1:2],
        out_up,
        bias_up,
        out_dn,
        row_sum[5:6],
        row_sum[3:4],
        row_sum[4:5],
        out_pk,
        out_pv,
    )


def solution(mesh):
    placed = (
        P(None, "tok", None),
        P(None, "tok", None),
        P(),
        P("section", None, None),
        P("section", None, None),
        P("section", "tok", None),
        P("section", "tok"),
        P("section", "tok", None),
        P("section", "tok", None),
        P("section", "tok"),
        P("section", "tok", None),
        P("section", "tok"),
        P("section", "tok"),
        P("section", "tok"),
        P("section", "tok", None),
        P("section", "tok"),
        P("section", "tok", None),
        P("section", "tok"),
        P("section", "tok"),
        P("section", "tok"),
    )
    return jax.shard_map(
        cube_local if mesh.shape["tok"] == HEADS else local,
        mesh=mesh,
        in_specs=placed,
        out_specs=(
            P("section", None, "tok", None),
            P("section", None, "tok", None),
            P("section", "tok", None),
            P("section", "tok"),
            P("section", "tok", None),
            P("section", "tok", None),
            P("section", "tok"),
            P("section", "tok", None),
            P("section", "tok"),
            P("section", "tok"),
            P("section", "tok"),
            P("section", "tok", None),
            P("section", "tok"),
            P("section", "tok", None),
            P("section", "tok"),
            P("section", "tok"),
            P("section", "tok"),
            P("section", None, None),
            P("section", None, None),
        ),
        check_vma=False,
    )
```
